256 devices in a mesh: dp: 4 (over y_hi, core), seq: 64 (over y_lo, z, x).
Axes of the slice: x: 4, y: 4 (y_hi: 2, y_lo: 2; y = y_hi * 2 + y_lo), z: 8, core: 2. Of those that a mesh axis runs over, the one named last changes fastest.
Arguments:
- block_input: bfloat16 [4, 64, 128, 1152], P('dp', 'seq'), may hold values from -6 to 6
- spatial_queries: bfloat16 [4, 64, 128, 576], P('dp', 'seq'), may hold values from -13.5 to 13.5
- spatial_keys: bfloat16 [4, 64, 128, 576], P('dp', 'seq'), may hold values from -4 to 4
- cotangent: bfloat16 [4, 64, 128, 1152], P('dp', None, 'seq'), may hold values from -16 to 16
- temporal_queries: bfloat16 [4, 64, 128, 576], P('dp', None, 'seq'), may hold values from -13.5 to 13.5
- temporal_keys: bfloat16 [4, 64, 128, 576], P('dp', None, 'seq'), may hold values from -4 to 4
- weights: bfloat16 [4, 1152, 576], replicated, may hold values from -0.1875 to 0.1875
Outputs:
- input_grad: bfloat16 [4, 64, 128, 1152], P('dp', 'seq')
- spatial_query_grad: bfloat16 [4, 64, 128, 576], P('dp', 'seq')
- spatial_key_grad: bfloat16 [4, 64, 128, 576], P('dp', 'seq')
- temporal_query_grad: bfloat16 [4, 64, 128, 576], P('dp', None, 'seq')
- temporal_key_grad: bfloat16 [4, 64, 128, 576], P('dp', None, 'seq')
- weight_grads: float32 [4, 1152, 576], P(None, 'seq', 'dp')
The draws below stay inside these ranges and needn't reach their ends.
All inputs are finite; a program needn't handle non-finite values.
Results may differ from the reference program's by a relative error of at most 0.014.
Values may be sent and summed in bfloat16 or wider, within the bound.
A program may use at most 128 MiB of HBM per device.

```python
import jax
import jax.numpy as jnp
from jax import lax

D = 1152
HEADS = 8
HEAD_DIM = 72
INNER = 576
P_SIZE = 128
FRAMES = 64
CLIPS = 4


def normal_part(key, full_shape):
    return jnp.clip(jax.random.normal(key, full_shape, jnp.float32), -4.0, 4.0)


def draw_spatial_queries(key, part):
    full_shape = (CLIPS, FRAMES, P_SIZE, INNER)
    key = jax.random.fold_in(key, 1)
    values = normal_part(key, full_shape)
    return values.astype(jnp.bfloat16)


def draw_spatial_keys(key, part):
    full_shape = (CLIPS, FRAMES, P_SIZE, INNER)
    key = jax.random.fold_in(key, 2)
    values = normal_part(key, full_shape)
    return values.astype(jnp.bfloat16)


def draw_temporal_queries(key, part):
    full_shape = (CLIPS, FRAMES, P_SIZE, INNER)
    key = jax.random.fold_in(key, 3)
    values = normal_part(key, full_shape)
    return values.astype(jnp.bfloat16)


def draw_temporal_keys(key, part):
    full_shape = (CLIPS, FRAMES, P_SIZE, INNER)
    key = jax.random.fold_in(key, 4)
    values = normal_part(key, full_shape)
    return values.astype(jnp.bfloat16)


def strengthened(values, stream_key, source, target, parts, factor):
    def block_of(axis_at):
        return (jnp.arange(values.shape[axis_at]) // (values.shape[axis_at] // parts)).reshape((-1,) + (1,) * (values.ndim - 1 - axis_at))

    near = jax.random.permutation(stream_key, parts)[block_of(target)]
    other_side = (block_of(target) + parts // 2) % parts
    return jnp.where((block_of(source) == near) | (block_of(source) == other_side), factor * values, values)


def block_levels(rng, dims, split, low, high):
    factor_of = 1.0
    for axis_at, parts in split:
        draws = jax.random.uniform(jax.random.fold_in(jax.random.fold_in(rng, 6), axis_at), (parts,), jnp.float32, low / len(split), high / len(split))
        factor_of = factor_of * jnp.repeat(jnp.exp(draws), dims[axis_at] // parts).reshape((-1,) + (1,) * (len(dims) - 1 - axis_at))
    return factor_of


def gaussian(rng, extent, deviation, limit, cuts=(), dtype=jnp.bfloat16):
    level = block_levels(rng, extent, cuts, -0.22, 0.18) if cuts else 1.0
    values = jax.random.normal(rng, extent, jnp.float32) * deviation * level
    return jnp.minimum(jnp.maximum(values, -limit), limit).astype(dtype)


def heavy_noise(key, extent, width, bound, pieces, heavy, kind=jnp.bfloat16):
    array = width * jax.random.normal(key, extent, jnp.float32)
    if pieces:
        array = array * block_levels(key, extent, pieces, -0.22, 0.18)
    return jnp.clip(strengthened(array, jax.random.fold_in(key, 3), *heavy), -bound, bound).astype(kind)


def setup_inputs(seed: int = 0) -> dict:
    key_of = jax.random.split(jax.random.key(seed), 8)
    return {
        "block_input": gaussian(key_of[0], (CLIPS, FRAMES, P_SIZE, D), 1.0, 6.0, ((0, 4), (1, 64))),
        "spatial_queries": draw_spatial_queries(jax.random.fold_in(key_of[7], 71), 0),
        "spatial_keys": draw_spatial_keys(jax.random.fold_in(key_of[7], 71), 0),
        "cotangent": heavy_noise(key_of[3], (CLIPS, FRAMES, P_SIZE, D), 1.0, 16.0, ((0, 4), (2, 64)), (2, 3, 64, 4.0)),
        "temporal_queries": draw_temporal_queries(jax.random.fold_in(key_of[7], 71), 0),
        "temporal_keys": draw_temporal_keys(jax.random.fold_in(key_of[7], 71), 0),
        "weights": gaussian(key_of[6], (4, D, INNER), D ** -0.5, 0.1875),
    }


def product(einsum_form, left_side, right_side):
    left_side, right_side = lax.optimization_barrier((left_side, right_side))
    return jnp.einsum(einsum_form, left_side.astype(jnp.float32), right_side.astype(jnp.float32))


def with_heads(tensor):
    return tensor.reshape(tensor.shape[:-1] + (HEADS, HEAD_DIM))


def without_heads(tensor):
    return tensor.reshape(tensor.shape[:-2] + (HEADS * HEAD_DIM,))


def chances(queries, key_rows):
    scores = product('xlyhe,xmyhe->xyhlm', queries, key_rows) * HEAD_DIM ** -0.5
    return jax.nn.softmax(scores, axis=-1)


def attend(prob_map, values):
    return product('xyhlm,xmyhe->xlyhe', prob_map.astype(jnp.bfloat16), values).astype(jnp.bfloat16)


def attend_back(prob_map, queries, key_rows, values, out_grad):
    rounded = prob_map.astype(jnp.bfloat16)
    prob_grad = product('xlyhe,xmyhe->xyhlm', out_grad, values)
    value_grad = product('xyhlm,xlyhe->xmyhe', rounded, out_grad).astype(jnp.bfloat16)
    centre = jnp.sum(prob_map * prob_grad, axis=-1, keepdims=True)
    score_grad = (prob_map * (prob_grad - centre)).astype(jnp.bfloat16)
    query_grad = (product('xyhlm,xmyhe->xlyhe', score_grad, key_rows) * HEAD_DIM ** -0.5).astype(jnp.bfloat16)
    key_grad = (product('xyhlm,xlyhe->xmyhe', score_grad, queries) * HEAD_DIM ** -0.5).astype(jnp.bfloat16)
    return query_grad, key_grad, value_grad


def spatial_view(tensor):
    return with_heads(tensor)[None, :, None]


def frame_forward(item):
    queries, key_rows, values = item
    prob_map = chances(spatial_view(queries), spatial_view(key_rows))
    return without_heads(attend(prob_map, spatial_view(values)))[0, :, 0]


def frame_backward(item):
    queries, key_rows, values, out_grad = item
    prob_map = chances(spatial_view(queries), spatial_view(key_rows))
    grads = attend_back(prob_map, spatial_view(queries), spatial_view(key_rows), spatial_view(values), spatial_view(out_grad))
    return tuple(without_heads(entry)[0, :, 0] for entry in grads)


def flatten_frames(tensor):
    return tensor.reshape(CLIPS * FRAMES, P_SIZE, tensor.shape[-1])


def restore_frames(tensor):
    return tensor.reshape(CLIPS, FRAMES, P_SIZE, tensor.shape[-1])


def reference(block_input, spatial_queries, spatial_keys, cotangent, temporal_queries, temporal_keys, weights):
    value_sp = product('cfpd,de->cfpe', block_input, weights[0]).astype(jnp.bfloat16)
    attended = restore_frames(lax.map(frame_forward, (flatten_frames(spatial_queries), flatten_frames(spatial_keys), flatten_frames(value_sp))))
    mixed = (block_input.astype(jnp.float32) + product('cfpe,de->cfpd', attended, weights[1])).astype(jnp.bfloat16)
    value_tm = product('cfpd,de->cfpe', mixed, weights[2]).astype(jnp.bfloat16)
    query_heads = with_heads(temporal_queries)
    key_heads = with_heads(temporal_keys)
    prob_tm = chances(query_heads, key_heads)
    attended_tm = without_heads(attend(prob_tm, with_heads(value_tm)))
    out_weight_tm = product('cfpd,cfpe->de', cotangent, attended_tm)
    attended_tm_grad = product('cfpd,de->cfpe', cotangent, weights[3]).astype(jnp.bfloat16)
    query_tm_grad, key_tm_grad, value_tm_grad = attend_back(prob_tm, query_heads, key_heads, with_heads(value_tm), with_heads(attended_tm_grad))
    value_tm_grad = without_heads(value_tm_grad)
    value_weight_tm = product('cfpd,cfpe->de', mixed, value_tm_grad)
    mixed_grad = (cotangent.astype(jnp.float32) + product('cfpe,de->cfpd', value_tm_grad, weights[2])).astype(jnp.bfloat16)
    out_weight_sp = product('cfpd,cfpe->de', mixed_grad, attended)
    attended_grad = product('cfpd,de->cfpe', mixed_grad, weights[1]).astype(jnp.bfloat16)
    query_sp_grad, key_sp_grad, value_sp_grad = lax.map(frame_backward, (flatten_frames(spatial_queries), flatten_frames(spatial_keys), flatten_frames(value_sp), flatten_frames(attended_grad)))
    query_sp_grad = restore_frames(query_sp_grad)
    key_sp_grad = restore_frames(key_sp_grad)
    value_sp_grad = restore_frames(value_sp_grad)
    value_weight_sp = product('cfpd,cfpe->de', block_input, value_sp_grad)
    input_grad = (mixed_grad.astype(jnp.float32) + product('cfpe,de->cfpd', value_sp_grad, weights[0])).astype(jnp.bfloat16)
    grad_scale = float(CLIPS * FRAMES * P_SIZE) ** -0.5
    weight_grads = jnp.stack([value_weight_sp, out_weight_sp, value_weight_tm, out_weight_tm]) * grad_scale
    return (input_grad, query_sp_grad, key_sp_grad, without_heads(query_tm_grad), without_heads(key_tm_grad), weight_grads)
```

```python
import jax
import jax.numpy as jnp
from jax import lax
from jax.sharding import PartitionSpec as P

HEADS = 8
HEAD_DIM = 72


def project(einsum_form, left_side, right_side):
    return jnp.einsum(einsum_form, left_side, right_side, preferred_element_type=jnp.float32)


def with_heads(tensor):
    return tensor.reshape(tensor.shape[:-1] + (HEADS, HEAD_DIM))


def without_heads(tensor):
    return tensor.reshape(tensor.shape[:-2] + (HEADS * HEAD_DIM,))


def chances(queries, key_rows):
    scores = project("xlyhe,xmyhe->xyhlm", queries, key_rows) * HEAD_DIM ** (-0.5)
    return jax.nn.softmax(scores, axis=-1)


def attend(prob_map, values):
    return project("xyhlm,xmyhe->xlyhe", prob_map.astype(jnp.bfloat16), values).astype(jnp.bfloat16)


def attend_back(prob_map, queries, key_rows, values, out_grad):
    rounded = prob_map.astype(jnp.bfloat16)
    prob_grad = project("xlyhe,xmyhe->xyhlm", out_grad, values)
    value_grad = project("xyhlm,xlyhe->xmyhe", rounded, out_grad).astype(jnp.bfloat16)
    centre = jnp.sum(prob_map * prob_grad, axis=-1, keepdims=True)
    score_grad = (prob_map * (prob_grad - centre)).astype(jnp.bfloat16)
    query_grad = (project("xyhlm,xmyhe->xlyhe", score_grad, key_rows) * HEAD_DIM ** (-0.5)).astype(
        jnp.bfloat16
    )
    key_grad = (project("xyhlm,xlyhe->xmyhe", score_grad, queries) * HEAD_DIM ** (-0.5)).astype(
        jnp.bfloat16
    )
    return (query_grad, key_grad, value_grad)


def reduce_grads(terms):
    count, rows, columns = terms.shape
    over_dp, over_seq = lax.axis_size("dp"), lax.axis_size("seq")
    blocks = terms.astype(jnp.bfloat16).reshape(
        count, over_seq, rows // over_seq, over_dp, columns // over_dp
    )
    blocks = blocks.transpose(3, 1, 0, 2, 4).reshape(over_dp, over_seq, -1)
    blocks = lax.all_to_all(blocks, "dp", split_axis=0, concat_axis=0, tiled=True)
    part = jnp.sum(blocks.astype(jnp.float32), axis=0).astype(jnp.bfloat16)
    part = lax.all_to_all(part, "seq", split_axis=0, concat_axis=0, tiled=True)
    share = jnp.sum(part.astype(jnp.float32), axis=0)
    return share.reshape(count, rows // over_seq, columns // over_dp)


def body(
    block_input, spatial_queries, spatial_keys, cotangent, temporal_queries, temporal_keys, weights
):
    clip_count, frame_count, patch_count, model_width = block_input.shape
    grad_scale = float(
        clip_count * lax.axis_size("dp") * frame_count * lax.axis_size("seq") * patch_count
    ) ** (-0.5)

    def spatial_view(tensor):
        return tensor.reshape(clip_count * frame_count, patch_count, 1, HEADS, HEAD_DIM)

    def spatial_flat(tensor):
        return tensor.reshape(clip_count, frame_count, patch_count, HEADS * HEAD_DIM)

    query_sp = spatial_view(spatial_queries)
    key_sp = spatial_view(spatial_keys)
    value_sp = project("cfpd,de->cfpe", block_input, weights[0]).astype(jnp.bfloat16)
    prob_sp = chances(query_sp, key_sp)
    attended = spatial_flat(attend(prob_sp, spatial_view(value_sp)))
    mixed = (
        block_input.astype(jnp.float32) + project("cfpe,de->cfpd", attended, weights[1])
    ).astype(jnp.bfloat16)
    mixed_tm = lax.all_to_all(mixed, "seq", split_axis=2, concat_axis=1, tiled=True)
    value_tm = project("cfpd,de->cfpe", mixed_tm, weights[2]).astype(jnp.bfloat16)
    query_heads = with_heads(temporal_queries)
    key_heads = with_heads(temporal_keys)
    prob_tm = chances(query_heads, key_heads)
    attended_tm = without_heads(attend(prob_tm, with_heads(value_tm)))
    out_weight_tm = project("cfpd,cfpe->de", cotangent, attended_tm)
    attended_tm_grad = project("cfpd,de->cfpe", cotangent, weights[3]).astype(jnp.bfloat16)
    query_tm_grad, key_tm_grad, value_tm_grad = attend_back(
        prob_tm, query_heads, key_heads, with_heads(value_tm), with_heads(attended_tm_grad)
    )
    value_tm_grad = without_heads(value_tm_grad)
    value_weight_tm = project("cfpd,cfpe->de", mixed_tm, value_tm_grad)
    mixed_tm_grad = (
        cotangent.astype(jnp.float32) + project("cfpe,de->cfpd", value_tm_grad, weights[2])
    ).astype(jnp.bfloat16)
    mixed_grad = lax.all_to_all(mixed_tm_grad, "seq", split_axis=1, concat_axis=2, tiled=True)
    out_weight_sp = project("cfpd,cfpe->de", mixed_grad, attended)
    attended_grad = project("cfpd,de->cfpe", mixed_grad, weights[1]).astype(jnp.bfloat16)
    query_sp_grad, key_sp_grad, value_sp_grad = attend_back(
        prob_sp, query_sp, key_sp, spatial_view(value_sp), spatial_view(attended_grad)
    )
    value_sp_grad = spatial_flat(value_sp_grad)
    value_weight_sp = project("cfpd,cfpe->de", block_input, value_sp_grad)
    input_grad = (
        mixed_grad.astype(jnp.float32) + project("cfpe,de->cfpd", value_sp_grad, weights[0])
    ).astype(jnp.bfloat16)
    weight_grads = reduce_grads(
        jnp.stack([value_weight_sp, out_weight_sp, value_weight_tm, out_weight_tm]) * grad_scale
    )
    return (
        input_grad,
        spatial_flat(query_sp_grad),
        spatial_flat(key_sp_grad),
        without_heads(query_tm_grad),
        without_heads(key_tm_grad),
        weight_grads,
    )


def solution(mesh):
    placed = (
        P("dp", "seq", None, None),
        P("dp", "seq", None, None),
        P("dp", "seq", None, None),
        P("dp", None, "seq", None),
        P("dp", None, "seq", None),
        P("dp", None, "seq", None),
        P(),
    )
    return jax.shard_map(
        body,
        mesh=mesh,
        in_specs=placed,
        out_specs=(
            P("dp", "seq", None, None),
            P("dp", "seq", None, None),
            P("dp", "seq", None, None),
            P("dp", None, "seq", None),
            P("dp", None, "seq", None),
            P(None, "seq", "dp"),
        ),
        check_vma=False,
    )
```

```python
import functools

import jax
import jax.numpy as jnp
import numpy as np
from jax import lax
from jax.experimental import pallas as pl
from jax.experimental.pallas import tpu as pltpu
from jax.sharding import PartitionSpec as P

HEADS = 8
HEAD_DIM = 72
WIDTH = 1152
INNER = 576
TOKENS = 128
SCORE_SCALE = HEAD_DIM ** (-0.5)
ROW_BLOCK = 144
LANES = 384
SHARE_ROWS = 32
CUT = 80
F32 = jnp.float32
BF16 = jnp.bfloat16
MESH = pl.DeviceIdType.MESH


def one_hot(source, size):
    table = np.zeros((len(source), size), np.float32)
    for row, at in enumerate(source):
        if at >= 0:
            table[row, at] = 1.0
    return table


def make_tables():
    def natural(y_lo, z, x, p):
        return 2 * (y_lo * 32 + z * 4 + x) + p

    to_z = [natural(y, z, x, p) for z in range(8) for y in range(2) for x in range(4) for p in range(2)]
    to_plane = [z * 16 + q * 2 + p for q in range(8) for z in range(8) for p in range(2)]
    to_natural = [
        (y * 4 + x) * 16 + z * 2 + p for y in range(2) for z in range(8) for x in range(4) for p in range(2)
    ]
    token_moves = np.stack([one_hot(order, TOKENS) for order in (to_z, to_plane, to_natural)])
    feature_moves = np.stack(
        [
            one_hot(
                [y * 64 + z * 72 + x * 18 + r for x in range(4) for z in range(8) for r in range(18)], 640
            )
            for y in range(2)
        ]
    )
    picks = np.zeros((2, 2, 2, INNER, LANES), np.float32)
    for core in range(2):
        for matrix in range(2):
            for y_hi in range(2):
                for column in range(144):
                    picks[core, matrix, y_hi, (2 * y_hi + core) * 144 + column, matrix * 144 + column] = 1.0
    share_moves = one_hot([z * 18 + r if r < 18 else -1 for z in range(8) for r in range(SHARE_ROWS)], ROW_BLOCK)
    return [jnp.asarray(table, BF16) for table in (token_moves, feature_moves, picks, share_moves)]


def dot(left, right):
    return jnp.dot(left, right, preferred_element_type=F32)


def dot_nt(left, right):
    return lax.dot_general(left, right, (((1,), (1,)), ((), ())), preferred_element_type=F32)


def dot_tn(left, right):
    return lax.dot_general(left, right, (((0,), (0,)), ((), ())), preferred_element_type=F32)


def head_window(head):
    start = head * HEAD_DIM // 128 * 128
    stop = min(-(-(head * HEAD_DIM + HEAD_DIM) // 128) * 128, INNER)
    return start, stop


def head_mask(head):
    start, stop = head_window(head)
    lane = lax.broadcasted_iota(jnp.int32, (TOKENS, stop - start), 1) + start
    return (lane >= head * HEAD_DIM) & (lane < (head + 1) * HEAD_DIM)


def window(ref, head):
    start, stop = head_window(head)
    return ref[:, start:stop]


def masked_window(ref, head):
    return jnp.where(head_mask(head), window(ref, head).astype(F32), 0.0).astype(BF16)


def join_heads(parts):
    tiles = [None] * 5
    for head, part in enumerate(parts):
        start, stop = head_window(head)
        part = jnp.where(head_mask(head), part, 0.0)
        for at in range(start, stop, 128):
            piece = part[:, at - start : min(at - start + 128, stop - start)]
            tiles[at // 128] = piece if tiles[at // 128] is None else tiles[at // 128] + piece
    return jnp.concatenate(tiles, axis=1)


def softmax_heads(queries, key_rows, chance_ref, bias):
    for head in range(HEADS):
        scores = dot_nt(masked_window(queries, head), window(key_rows, head)) * SCORE_SCALE
        if bias is not None:
            scores = scores + bias
        powers = jnp.exp(scores - jnp.max(scores, axis=1, keepdims=True))
        chance_ref[head] = powers / jnp.sum(powers, axis=1, keepdims=True)


def attend(chance_ref, values):
    return join_heads([dot(chance_ref[h].astype(BF16), window(values, h)) for h in range(HEADS)])


def attend_values_back(chance_ref, out_grad):
    return join_heads([dot_tn(chance_ref[h].astype(BF16), window(out_grad, h)) for h in range(HEADS)])


def attend_scores_back(chance_ref, queries, key_rows, values, out_grad):
    query_parts, key_parts = [], []
    for head in range(HEADS):
        chance = chance_ref[head]
        chance_grad = dot_nt(masked_window(out_grad, head), window(values, head))
        centre = jnp.sum(chance * chance_grad, axis=1, keepdims=True)
        score_grad = (chance * (chance_grad - centre)).astype(BF16)
        query_parts.append(dot(score_grad, window(key_rows, head)))
        key_parts.append(dot_tn(score_grad, window(queries, head)))
    return join_heads(query_parts) * SCORE_SCALE, join_heads(key_parts) * SCORE_SCALE


def kernel(
    grad_scale,
    block_hbm, sq_hbm, sk_hbm, cot_hbm, tq_hbm, tk_hbm, weights_hbm,
    token_moves_hbm, feature_moves_hbm, picks_hbm, share_moves_hbm,
    input_grad, sq_grad, sk_grad, tq_grad, tk_grad, weight_grads,
    block, sq, sk, cot, tq, tk, weights, token_moves, feature_moves, picks, share_moves,
    chance_s, chance_t, value_s, value_t, attended_s, attended_t, at_grad, as_grad, vt_grad, vs_grad,
    mixed, mixed_grad,
    out_z, in_z, out_plane, in_plane,
    factors, picked, picked_out, sums, arrived, sums_two, arrived_two, shares, shares_in,
    load_sem, z_send, z_recv, plane_send, plane_recv, factor_send, factor_recv, picked_send, picked_recv,
    ring_send, ring_recv, ring_two_send, ring_two_recv, share_send, share_recv,
):
    dp, seq = lax.axis_index("dp"), lax.axis_index("seq")
    y_hi, core = dp // 2, dp % 2
    y_lo, z, x = seq // 32, (seq // 4) % 8, seq % 4
    y = y_hi * 2 + y_lo
    q = y_lo * 4 + x

    def device(y_hi_at=y_hi, core_at=core, y_lo_at=y_lo, z_at=z, x_at=x):
        return (y_hi_at * 2 + core_at, y_lo_at * 32 + z_at * 4 + x_at)

    def along_z(step):
        return device(z_at=(z + step) % 8)

    def in_the_plane(step):
        to = (q + step) % 8
        return device(y_lo_at=to // 4, x_at=to % 4)

    def along_x(step):
        return device(x_at=(x + step) % 4)

    def along_y(step):
        to = (y + step) % 4
        return device(y_hi_at=to // 2, y_lo_at=to % 2)

    sibling = device(core_at=1 - core)

    loads = []
    for number, (source, target) in enumerate(
        [
            (tq_hbm, tq), (tk_hbm, tk), (cot_hbm, cot), (weights_hbm.at[3], weights.at[3]),
            (weights_hbm.at[2], weights.at[2]), (token_moves_hbm, token_moves), (block_hbm, block),
            (weights_hbm.at[0], weights.at[0]), (sq_hbm, sq), (sk_hbm, sk), (weights_hbm.at[1], weights.at[1]),
            (feature_moves_hbm, feature_moves), (picks_hbm, picks), (share_moves_hbm, share_moves),
        ]
    ):
        copy = pltpu.make_async_copy(source, target, load_sem.at[number])
        copy.start()
        loads.append(copy)

    barrier = pltpu.get_barrier_semaphore()
    greeted = [along_z(step) for step in range(1, 8)] + [in_the_plane(step) for step in range(1, 8)]
    greeted += [device(y_hi_at=1 - y_hi, y_lo_at=1 - y_lo), sibling]
    for peer in greeted:
        pl.semaphore_signal(barrier, inc=1, device_id=peer, device_id_type=MESH)

    sent = []

    def send(source, target, send_sem, recv_sem, peer):
        copy = pltpu.make_async_remote_copy(
            src_ref=source, dst_ref=target, send_sem=send_sem, recv_sem=recv_sem,
            device_id=peer, device_id_type=MESH,
        )
        copy.start()
        sent.append(copy)
        return copy

    def move_tokens(number, rows):
        return dot(token_moves[number], rows).astype(BF16)

    def start_z(item):
        copies = []
        for step in range(1, 8):
            to = (z + step) % 8
            copies.append(
                send(
                    out_z.at[item, pl.ds(to * 16, 16)], in_z.at[item, pl.ds(z * 16, 16)],
                    z_send.at[item, step - 1], z_recv.at[item, step - 1], along_z(step),
                )
            )
        own = pl.ds(pl.multiple_of(z * 16, 16), 16)
        in_z[item, own, :] = out_z[item, own, :]
        return copies

    def start_plane(item):
        copies = []
        for step in range(1, 8):
            to = (q + step) % 8
            copies.append(
                send(
                    out_plane.at[item, pl.ds(to * 16, 16)], in_plane.at[item, pl.ds(q * 16, 16)],
                    plane_send.at[item, step - 1], plane_recv.at[item, step - 1], in_the_plane(step),
                )
            )
        own = pl.ds(pl.multiple_of(q * 16, 16), 16)
        in_plane[item, own, :] = out_plane[item, own, :]
        return copies

    def arrive(copies):
        for copy in copies:
            copy.wait_recv()

    def start_features(number, rows_ref):
        for half in range(2):
            factors[number, half * INNER : (half + 1) * INNER, 0:TOKENS] = dot_nt(
                feature_moves[half], rows_ref[:, half * 512 : half * 512 + 640]
            ).astype(BF16)
        return send(
            factors.at[number, :, 0:TOKENS], factors.at[number, :, TOKENS : 2 * TOKENS],
            factor_send.at[number], factor_recv.at[number], sibling,
        )

    def start_columns(number, rows):
        for side in range(2):
            picked[number, side, 0:TOKENS, :] = dot(rows, picks[core, number % 2, side]).astype(BF16)
            picked_out[number, side] = dot(rows, picks[1 - core, number % 2, side]).astype(BF16)
        return send(
            picked_out.at[number], picked.at[number, :, TOKENS : 2 * TOKENS],
            picked_send.at[number], picked_recv.at[number], sibling,
        )

    def block_sum(pair, side, y_lo_at, x_at):
        rows = pl.ds(pl.multiple_of((y_lo_at * 4 + x_at) * ROW_BLOCK, 16), ROW_BLOCK)
        total = dot(factors[2 * pair, rows, :], picked[2 * pair, side])
        total += dot(factors[2 * pair + 1, rows, :], picked[2 * pair + 1, side])
        sums[pair, side, y_lo_at, x_at] = total.astype(BF16)

    def piece(pair, to, half):
        if pair == 0:
            return sums.at[0, half, :, to]
        return sums.at[1, to // 2, to % 2, 2 * half : 2 * half + 2]

    def make_pieces(pair, to):
        if pair == 0:
            for side in range(2):
                for y_lo_at in range(2):
                    block_sum(0, side, y_lo_at, to)
        else:
            for x_at in range(4):
                block_sum(1, to // 2, to % 2, x_at)

    places = (x, y)
    rings = (along_x, along_y)

    def ring_copy(pair, slot, source):
        peer = rings[pair](1 if slot % 2 == 0 else -1 + 4)
        return send(source, arrived.at[pair, slot], ring_send.at[pair, slot], ring_recv.at[pair, slot], peer)

    def first_ring(pair):
        place = places[pair]
        after, across, before = (place + 1) % 4, (place + 2) % 4, (place + 3) % 4
        copies = {}
        make_pieces(pair, across)
        copies[0] = ring_copy(pair, 0, piece(pair, across, 0))
        copies[1] = ring_copy(pair, 1, piece(pair, across, 1))
        make_pieces(pair, after)
        copies[2] = ring_copy(pair, 2, piece(pair, after, 1))
        make_pieces(pair, before)
        copies[3] = ring_copy(pair, 3, piece(pair, before, 0))
        make_pieces(pair, place)
        return copies

    def first_relay(pair, copies):
        place = places[pair]
        after, before = (place + 1) % 4, (place + 3) % 4
        for slot, to, half in ((0, after, 0), (1, before, 1)):
            copies[slot].wait_recv()
            ref = piece(pair, to, half)
            ref[...] = (ref[...].astype(F32) + arrived[pair, slot].astype(F32)).astype(BF16)
            copies[slot + 4] = ring_copy(pair, slot + 4, ref)

    def first_end(pair, copies):
        for half, slots in ((0, (3, 4)), (1, (2, 5))):
            total = piece(pair, places[pair], half)[...].astype(F32)
            for slot in slots:
                copies[slot].wait_recv()
                total += arrived[pair, slot].astype(F32)
            sums_two[pair, 2 * half : 2 * half + 2] = total.astype(BF16)

    def part_two(pair, to, half):
        return sums_two.at[pair, to, 0:CUT] if half == 0 else sums_two.at[pair, to, CUT:ROW_BLOCK]

    def slot_two(pair, slot, half):
        return arrived_two.at[pair, slot, 0 : (CUT if half == 0 else ROW_BLOCK - CUT)]

    slot_half = (0, 1, 1, 0, 0, 1)

    def ring_two_copy(pair, slot, source):
        peer = rings[1 - pair](1 if slot % 2 == 0 else -1 + 4)
        return send(
            source, slot_two(pair, slot, slot_half[slot]),
            ring_two_send.at[pair, slot], ring_two_recv.at[pair, slot], peer,
        )

    def second_ring(pair):
        place = places[1 - pair]
        after, across, before = (place + 1) % 4, (place + 2) % 4, (place + 3) % 4
        copies = {}
        copies[0] = ring_two_copy(pair, 0, part_two(pair, across, 0))
        copies[1] = ring_two_copy(pair, 1, part_two(pair, across, 1))
        copies[2] = ring_two_copy(pair, 2, part_two(pair, after, 1))
        copies[3] = ring_two_copy(pair, 3, part_two(pair, before, 0))
        return copies

    def second_relay(pair, copies):
        place = places[1 - pair]
        after, before = (place + 1) % 4, (place + 3) % 4
        for slot, to, half in ((0, after, 0), (1, before, 1)):
            copies[slot].wait_recv()
            ref = part_two(pair, to, half)
            ref[...] = (ref[...].astype(F32) + slot_two(pair, slot, half)[...].astype(F32)).astype(BF16)
            copies[slot + 4] = ring_two_copy(pair, slot + 4, ref)

    def second_end(pair, copies):
        place = places[1 - pair]
        halves = []
        for half, slots in ((0, (3, 4)), (1, (2, 5))):
            total = part_two(pair, place, half)[...].astype(F32)
            for slot in slots:
                copies[slot].wait_recv()
                total += slot_two(pair, slot, half)[...].astype(F32)
            halves.append(total.astype(BF16))
        shares[pair] = dot(share_moves[...], jnp.concatenate(halves, axis=0)).astype(BF16)
        last = []
        for step in range(1, 8):
            to = (z + step) % 8
            last.append(
                send(
                    shares.at[pair, pl.ds(to * SHARE_ROWS, SHARE_ROWS)], shares_in.at[pair, step - 1],
                    share_send.at[pair, step - 1], share_recv.at[pair, step - 1], along_z(step),
                )
            )
        return last

    def finish(pair, copies):
        own = pl.ds(pl.multiple_of(z * SHARE_ROWS, SHARE_ROWS), SHARE_ROWS)
        total = shares[pair, own, :].astype(F32)
        for step in range(1, 8):
            copies[step - 1].wait_recv()
            total += shares_in[pair, step - 1].astype(F32)
        total = total * grad_scale
        weight_grads[2 * pair] = total[0:18, 0:144]
        weight_grads[2 * pair + 1] = total[0:18, 144:288]

    loads[0].wait()
    loads[1].wait()
    row_patch = lax.broadcasted_iota(jnp.int32, (TOKENS, TOKENS), 0) % 2
    column_patch = lax.broadcasted_iota(jnp.int32, (TOKENS, TOKENS), 1) % 2
    softmax_heads(tq, tk, chance_t, jnp.where(row_patch == column_patch, 0.0, -1e30))
    loads[2].wait()
    loads[3].wait()
    at_grad[...] = dot(cot[...], weights[3]).astype(BF16)
    vt_grad[...] = attend_values_back(chance_t, at_grad).astype(BF16)
    loads[4].wait()
    loads[5].wait()
    out_z[1] = move_tokens(0, (cot[...].astype(F32) + dot_nt(vt_grad[...], weights[2])).astype(BF16))
    pl.semaphore_wait(barrier, len(greeted))
    grad_z = start_z(1)

    for number in (6, 7, 8, 9, 10):
        loads[number].wait()
    value_s[...] = dot(block[...], weights[0]).astype(BF16)
    softmax_heads(sq, sk, chance_s, None)
    attended_s[...] = attend(chance_s, value_s).astype(BF16)
    out_z[0] = move_tokens(0, (block[...].astype(F32) + dot_nt(attended_s[...], weights[1])).astype(BF16))
    mixed_z = start_z(0)

    for number in (11, 12, 13):
        loads[number].wait()
    arrive(grad_z)
    out_plane[1] = move_tokens(1, in_z[1])
    grad_plane = start_plane(1)
    feature_copies, column_copies = {}, {}
    feature_copies[0] = start_features(0, block)
    feature_copies[3] = start_features(3, cot)
    column_copies[1] = start_columns(1, attended_s[...])
    column_copies[2] = start_columns(2, vt_grad[...])
    arrive(mixed_z)
    out_plane[0] = move_tokens(1, in_z[0])
    mixed_plane = start_plane(0)

    arrive(grad_plane)
    mixed_grad[...] = move_tokens(2, in_plane[1])
    feature_copies[1] = start_features(1, mixed_grad)
    as_grad[...] = dot(mixed_grad[...], weights[1]).astype(BF16)
    vs_grad[...] = attend_values_back(chance_s, as_grad).astype(BF16)
    column_copies[0] = start_columns(0, vs_grad[...])

    arrive(mixed_plane)
    mixed[...] = move_tokens(2, in_plane[0])
    feature_copies[2] = start_features(2, mixed)
    value_t[...] = dot(mixed[...], weights[2]).astype(BF16)
    attended_t[...] = attend(chance_t, value_t).astype(BF16)
    column_copies[3] = start_columns(3, attended_t[...])

    arrive([feature_copies[0], feature_copies[1], column_copies[0], column_copies[1]])
    first_s = first_ring(0)
    arrive([feature_copies[2], feature_copies[3], column_copies[2], column_copies[3]])
    first_t = first_ring(1)
    first_relay(0, first_s)
    query_part, key_part = attend_scores_back(chance_s, sq, sk, value_s, as_grad)
    sq_grad[...] = query_part.astype(BF16)
    sk_grad[...] = key_part.astype(BF16)
    first_relay(1, first_t)
    input_grad[...] = (mixed_grad[...].astype(F32) + dot_nt(vs_grad[...], weights[0])).astype(BF16)
    query_part, key_part = attend_scores_back(chance_t, tq, tk, value_t, at_grad)
    tq_grad[...] = query_part.astype(BF16)
    tk_grad[...] = key_part.astype(BF16)

    first_end(0, first_s)
    second_s = second_ring(0)
    first_end(1, first_t)
    second_t = second_ring(1)
    second_relay(0, second_s)
    second_relay(1, second_t)
    last_s = second_end(0, second_s)
    last_t = second_end(1, second_t)
    finish(0, last_s)
    finish(1, last_t)
    for copy in sent:
        copy.wait_send()


def body(
    block_input, spatial_queries, spatial_keys, cotangent, temporal_queries, temporal_keys, weights
):
    grad_scale = float(4 * 64 * 128) ** (-0.5)
    tables = make_tables()
    arrays = [
        block_input.reshape(TOKENS, WIDTH),
        spatial_queries.reshape(TOKENS, INNER),
        spatial_keys.reshape(TOKENS, INNER),
        cotangent.reshape(TOKENS, WIDTH),
        temporal_queries.reshape(TOKENS, INNER),
        temporal_keys.reshape(TOKENS, INNER),
        weights,
    ] + tables
    wide, narrow = (TOKENS, WIDTH), (TOKENS, INNER)
    chances = pltpu.VMEM((HEADS, TOKENS, TOKENS), F32)
    dma = pltpu.SemaphoreType.DMA
    scratch = [pltpu.VMEM(array.shape, BF16) for array in arrays]
    scratch += [chances, chances] + [pltpu.VMEM(narrow, BF16)] * 8
    scratch += [pltpu.VMEM(wide, BF16)] * 2 + [pltpu.VMEM((2,) + wide, BF16)] * 4
    scratch += [
        pltpu.VMEM((4, WIDTH, 2 * TOKENS), BF16),
        pltpu.VMEM((4, 2, 2 * TOKENS, LANES), BF16),
        pltpu.VMEM((4, 2, TOKENS, LANES), BF16),
        pltpu.VMEM((2, 2, 2, 4, ROW_BLOCK, LANES), BF16),
        pltpu.VMEM((2, 6, 2, ROW_BLOCK, LANES), BF16),
        pltpu.VMEM((2, 4, ROW_BLOCK, LANES), BF16),
        pltpu.VMEM((2, 6, CUT, LANES), BF16),
        pltpu.VMEM((2, 8 * SHARE_ROWS, LANES), BF16),
        pltpu.VMEM((2, 7, SHARE_ROWS, LANES), BF16),
    ]
    scratch += [dma((14,))] + [dma((2, 7))] * 4 + [dma((4,))] * 4 + [dma((2, 6))] * 4 + [dma((2, 7))] * 2
    bf16_out = [jax.ShapeDtypeStruct(wide, BF16)] + [jax.ShapeDtypeStruct(narrow, BF16)] * 4
    input_grad, sq_grad, sk_grad, tq_grad, tk_grad, weight_grads = pl.pallas_call(
        functools.partial(kernel, grad_scale),
        out_shape=bf16_out + [jax.ShapeDtypeStruct((4, 18, 144), F32)],
        in_specs=[pl.BlockSpec(memory_space=pl.ANY)] * len(arrays),
        out_specs=[pl.BlockSpec(memory_space=pltpu.VMEM)] * 6,
        scratch_shapes=scratch,
        compiler_params=pltpu.CompilerParams(
            collective_id=0, has_side_effects=True, vmem_limit_bytes=56 * 2**20
        ),
        name="block_backward",
    )(*arrays)
    return (
        input_grad.reshape(block_input.shape),
        sq_grad.reshape(spatial_queries.shape),
        sk_grad.reshape(spatial_keys.shape),
        tq_grad.reshape(temporal_queries.shape),
        tk_grad.reshape(temporal_keys.shape),
        weight_grads,
    )


def solution(mesh):
    placed = (
        P("dp", "seq", None, None),
        P("dp", "seq", None, None),
        P("dp", "seq", None, None),
        P("dp", None, "seq", None),
        P("dp", None, "seq", None),
        P("dp", None, "seq", None),
        P(),
    )
    return jax.shard_map(
        body,
        mesh=mesh,
        in_specs=placed,
        out_specs=(
            P("dp", "seq", None, None),
            P("dp", "seq", None, None),
            P("dp", "seq", None, None),
            P("dp", None, "seq", None),
            P("dp", None, "seq", None),
            P(None, "seq", "dp"),
        ),
        check_vma=False,
    )
```

```python
import functools

import jax
import jax.numpy as jnp
import numpy as np
from jax import lax
from jax.experimental import pallas as pl
from jax.experimental.pallas import tpu as pltpu
from jax.sharding import PartitionSpec as P

HEADS = 8
HEAD_DIM = 72
WIDTH = 1152
INNER = 576
TOKENS = 128
FRAMES = 64
SCORE_SCALE = HEAD_DIM ** (-0.5)
ROW_BLOCK = 144
LANES = 384
SHARE_ROWS = 32
CUT = 80
F32 = jnp.float32
BF16 = jnp.bfloat16
MESH = pl.DeviceIdType.MESH


def one_hot(source, size):
    table = np.zeros((len(source), size), np.float32)
    for row, at in enumerate(source):
        if at >= 0:
            table[row, at] = 1.0
    return table


def make_tables():
    def natural(y_lo, z, x, p):
        return 2 * (y_lo * 32 + z * 4 + x) + p

    to_z = [natural(y, z, x, p) for z in range(8) for y in range(2) for x in range(4) for p in range(2)]
    to_plane = [z * 16 + q * 2 + p for q in range(8) for z in range(8) for p in range(2)]
    to_natural = [
        (y * 4 + x) * 16 + z * 2 + p for y in range(2) for z in range(8) for x in range(4) for p in range(2)
    ]
    token_moves = np.stack([one_hot(order, TOKENS) for order in (to_z, to_plane, to_natural)])
    feature_moves = np.stack(
        [
            one_hot(
                [y * 64 + z * 72 + x * 18 + r for x in range(4) for z in range(8) for r in range(18)], 640
            )
            for y in range(2)
        ]
    )
    picks = np.zeros((2, 2, 2, INNER, LANES), np.float32)
    for core in range(2):
        for matrix in range(2):
            for y_hi in range(2):
                for column in range(144):
                    picks[core, matrix, y_hi, (2 * y_hi + core) * 144 + column, matrix * 144 + column] = 1.0
    share_moves = one_hot([z * 18 + r if r < 18 else -1 for z in range(8) for r in range(SHARE_ROWS)], ROW_BLOCK)
    return [jnp.asarray(table, BF16) for table in (token_moves, feature_moves, picks, share_moves)]


def dot(left, right):
    return jnp.dot(left, right, preferred_element_type=F32)


def dot_nt(left, right):
    return lax.dot_general(left, right, (((1,), (1,)), ((), ())), preferred_element_type=F32)


def dot_tn(left, right):
    return lax.dot_general(left, right, (((0,), (0,)), ((), ())), preferred_element_type=F32)


def head_window(head):
    start = head * HEAD_DIM // 128 * 128
    stop = min(-(-(head * HEAD_DIM + HEAD_DIM) // 128) * 128, INNER)
    return start, stop


def head_mask(head):
    start, stop = head_window(head)
    lane = lax.broadcasted_iota(jnp.int32, (TOKENS, stop - start), 1) + start
    return (lane >= head * HEAD_DIM) & (lane < (head + 1) * HEAD_DIM)


def window(ref, head):
    start, stop = head_window(head)
    return ref[:, start:stop]


def masked_window(ref, head):
    return jnp.where(head_mask(head), window(ref, head).astype(F32), 0.0).astype(BF16)


def join_heads(parts):
    tiles = [None] * 5
    for head, part in enumerate(parts):
        start, stop = head_window(head)
        part = jnp.where(head_mask(head), part, 0.0)
        for at in range(start, stop, 128):
            piece = part[:, at - start : min(at - start + 128, stop - start)]
            tiles[at // 128] = piece if tiles[at // 128] is None else tiles[at // 128] + piece
    return jnp.concatenate(tiles, axis=1)


def softmax_heads(queries, key_rows, chance_ref, bias):
    for head in range(HEADS):
        scores = dot_nt(masked_window(queries, head), window(key_rows, head)) * SCORE_SCALE
        if bias is not None:
            scores = scores + bias
        powers = jnp.exp(scores - jnp.max(scores, axis=1, keepdims=True))
        chance_ref[head] = powers / jnp.sum(powers, axis=1, keepdims=True)


def attend(chance_ref, values):
    return join_heads([dot(chance_ref[h].astype(BF16), window(values, h)) for h in range(HEADS)])


def attend_values_back(chance_ref, out_grad):
    return join_heads([dot_tn(chance_ref[h].astype(BF16), window(out_grad, h)) for h in range(HEADS)])


def attend_scores_back(chance_ref, queries, key_rows, values, out_grad):
    query_parts, key_parts = [], []
    for head in range(HEADS):
        chance = chance_ref[head]
        chance_grad = dot_nt(masked_window(out_grad, head), window(values, head))
        centre = jnp.sum(chance * chance_grad, axis=1, keepdims=True)
        score_grad = (chance * (chance_grad - centre)).astype(BF16)
        query_parts.append(dot(score_grad, window(key_rows, head)))
        key_parts.append(dot_tn(score_grad, window(queries, head)))
    return join_heads(query_parts) * SCORE_SCALE, join_heads(key_parts) * SCORE_SCALE


def kernel(
    grad_scale,
    block_hbm, sq_hbm, sk_hbm, cot_hbm, tq_hbm, tk_hbm, weights_hbm,
    token_moves_hbm, feature_moves_hbm, picks_hbm, share_moves_hbm,
    input_grad, sq_grad, sk_grad, tq_grad, tk_grad, weight_grads,
    block, sq_turned, sk_turned, cot_pairs, tq_pairs, tk_pairs, weights, token_moves, feature_moves, picks, share_moves,
    sq, sk, cot, tq, tk, rows_wide, rows_one, rows_two,
    chance_s, chance_t, value_s, value_t, attended_s, attended_t, at_grad, as_grad, vt_grad, vs_grad,
    mixed, mixed_grad,
    out_z, in_z, out_plane, in_plane,
    factors, picked, picked_out, sums, arrived, sums_two, arrived_two, shares, shares_in,
    load_sem, z_send, z_recv, plane_send, plane_recv, factor_send, factor_recv, picked_send, picked_recv,
    ring_send, ring_recv, ring_two_send, ring_two_recv, share_send, share_recv,
):
    dp, seq = lax.axis_index("dp"), lax.axis_index("seq")
    y_hi, core = dp // 2, dp % 2
    y_lo, z, x = seq // 32, (seq // 4) % 8, seq % 4
    y = y_hi * 2 + y_lo
    q = y_lo * 4 + x

    def device(y_hi_at=y_hi, core_at=core, y_lo_at=y_lo, z_at=z, x_at=x):
        return (y_hi_at * 2 + core_at, y_lo_at * 32 + z_at * 4 + x_at)

    def along_z(step):
        return device(z_at=(z + step) % 8)

    def in_the_plane(step):
        to = (q + step) % 8
        return device(y_lo_at=to // 4, x_at=to % 4)

    def along_x(step):
        return device(x_at=(x + step) % 4)

    def along_y(step):
        to = (y + step) % 4
        return device(y_hi_at=to // 2, y_lo_at=to % 2)

    sibling = device(core_at=1 - core)

    loads = []
    for number, (source, target) in enumerate(
        [
            (tq_hbm, tq_pairs), (tk_hbm, tk_pairs), (cot_hbm, cot_pairs), (weights_hbm.at[3], weights.at[3]),
            (weights_hbm.at[2], weights.at[2]), (token_moves_hbm, token_moves), (block_hbm, block),
            (weights_hbm.at[0], weights.at[0]), (sq_hbm, sq_turned), (sk_hbm, sk_turned), (weights_hbm.at[1], weights.at[1]),
            (feature_moves_hbm, feature_moves), (picks_hbm, picks), (share_moves_hbm, share_moves),
        ]
    ):
        copy = pltpu.make_async_copy(source, target, load_sem.at[number])
        copy.start()
        loads.append(copy)

    barrier = pltpu.get_barrier_semaphore()
    greeted = [along_z(step) for step in range(1, 8)] + [in_the_plane(step) for step in range(1, 8)]
    greeted += [device(y_hi_at=1 - y_hi, y_lo_at=1 - y_lo), sibling]
    for peer in greeted:
        pl.semaphore_signal(barrier, inc=1, device_id=peer, device_id_type=MESH)

    sent = []

    def send(source, target, send_sem, recv_sem, peer):
        copy = pltpu.make_async_remote_copy(
            src_ref=source, dst_ref=target, send_sem=send_sem, recv_sem=recv_sem,
            device_id=peer, device_id_type=MESH,
        )
        copy.start()
        sent.append(copy)
        return copy

    def move_tokens(number, rows):
        return dot(token_moves[number], rows).astype(BF16)

    def start_z(item):
        copies = []
        for step in range(1, 8):
            to = (z + step) % 8
            copies.append(
                send(
                    out_z.at[item, pl.ds(to * 16, 16)], in_z.at[item, pl.ds(z * 16, 16)],
                    z_send.at[item, step - 1], z_recv.at[item, step - 1], along_z(step),
                )
            )
        own = pl.ds(pl.multiple_of(z * 16, 16), 16)
        in_z[item, own, :] = out_z[item, own, :]
        return copies

    def start_plane(item):
        copies = []
        for step in range(1, 8):
            to = (q + step) % 8
            copies.append(
                send(
                    out_plane.at[item, pl.ds(to * 16, 16)], in_plane.at[item, pl.ds(q * 16, 16)],
                    plane_send.at[item, step - 1], plane_recv.at[item, step - 1], in_the_plane(step),
                )
            )
        own = pl.ds(pl.multiple_of(q * 16, 16), 16)
        in_plane[item, own, :] = out_plane[item, own, :]
        return copies

    def arrive(copies):
        for copy in copies:
            copy.wait_recv()

    def start_features(number, rows_ref):
        for half in range(2):
            factors[number, half * INNER : (half + 1) * INNER, 0:TOKENS] = dot_nt(
                feature_moves[half], rows_ref[:, half * 512 : half * 512 + 640]
            ).astype(BF16)
        return send(
            factors.at[number, :, 0:TOKENS], factors.at[number, :, TOKENS : 2 * TOKENS],
            factor_send.at[number], factor_recv.at[number], sibling,
        )

    def start_columns(number, rows):
        for side in range(2):
            picked[number, side, 0:TOKENS, :] = dot(rows, picks[core, number % 2, side]).astype(BF16)
            picked_out[number, side] = dot(rows, picks[1 - core, number % 2, side]).astype(BF16)
        return send(
            picked_out.at[number], picked.at[number, :, TOKENS : 2 * TOKENS],
            picked_send.at[number], picked_recv.at[number], sibling,
        )

    def block_sum(pair, side, y_lo_at, x_at):
        rows = pl.ds(pl.multiple_of((y_lo_at * 4 + x_at) * ROW_BLOCK, 16), ROW_BLOCK)
        total = dot(factors[2 * pair, rows, :], picked[2 * pair, side])
        total += dot(factors[2 * pair + 1, rows, :], picked[2 * pair + 1, side])
        sums[pair, side, y_lo_at, x_at] = total.astype(BF16)

    def piece(pair, to, half):
        if pair == 0:
            return sums.at[0, half, :, to]
        return sums.at[1, to // 2, to % 2, 2 * half : 2 * half + 2]

    def make_pieces(pair, to):
        if pair == 0:
            for side in range(2):
                for y_lo_at in range(2):
                    block_sum(0, side, y_lo_at, to)
        else:
            for x_at in range(4):
                block_sum(1, to // 2, to % 2, x_at)

    places = (x, y)
    rings = (along_x, along_y)

    def ring_copy(pair, slot, source):
        peer = rings[pair](1 if slot % 2 == 0 else -1 + 4)
        return send(source, arrived.at[pair, slot], ring_send.at[pair, slot], ring_recv.at[pair, slot], peer)

    def first_ring(pair):
        place = places[pair]
        after, across, before = (place + 1) % 4, (place + 2) % 4, (place + 3) % 4
        copies = {}
        make_pieces(pair, across)
        copies[0] = ring_copy(pair, 0, piece(pair, across, 0))
        copies[1] = ring_copy(pair, 1, piece(pair, across, 1))
        make_pieces(pair, after)
        copies[2] = ring_copy(pair, 2, piece(pair, after, 1))
        make_pieces(pair, before)
        copies[3] = ring_copy(pair, 3, piece(pair, before, 0))
        make_pieces(pair, place)
        return copies

    def first_relay(pair, copies):
        place = places[pair]
        after, before = (place + 1) % 4, (place + 3) % 4
        for slot, to, half in ((0, after, 0), (1, before, 1)):
            copies[slot].wait_recv()
            ref = piece(pair, to, half)
            ref[...] = (ref[...].astype(F32) + arrived[pair, slot].astype(F32)).astype(BF16)
            copies[slot + 4] = ring_copy(pair, slot + 4, ref)

    def first_end(pair, copies):
        for half, slots in ((0, (3, 4)), (1, (2, 5))):
            total = piece(pair, places[pair], half)[...].astype(F32)
            for slot in slots:
                copies[slot].wait_recv()
                total += arrived[pair, slot].astype(F32)
            sums_two[pair, 2 * half : 2 * half + 2] = total.astype(BF16)

    def part_two(pair, to, half):
        return sums_two.at[pair, to, 0:CUT] if half == 0 else sums_two.at[pair, to, CUT:ROW_BLOCK]

    def slot_two(pair, slot, half):
        return arrived_two.at[pair, slot, 0 : (CUT if half == 0 else ROW_BLOCK - CUT)]

    slot_half = (0, 1, 1, 0, 0, 1)

    def ring_two_copy(pair, slot, source):
        peer = rings[1 - pair](1 if slot % 2 == 0 else -1 + 4)
        return send(
            source, slot_two(pair, slot, slot_half[slot]),
            ring_two_send.at[pair, slot], ring_two_recv.at[pair, slot], peer,
        )

    def second_ring(pair):
        place = places[1 - pair]
        after, across, before = (place + 1) % 4, (place + 2) % 4, (place + 3) % 4
        copies = {}
        copies[0] = ring_two_copy(pair, 0, part_two(pair, across, 0))
        copies[1] = ring_two_copy(pair, 1, part_two(pair, across, 1))
        copies[2] = ring_two_copy(pair, 2, part_two(pair, after, 1))
        copies[3] = ring_two_copy(pair, 3, part_two(pair, before, 0))
        return copies

    def second_relay(pair, copies):
        place = places[1 - pair]
        after, before = (place + 1) % 4, (place + 3) % 4
        for slot, to, half in ((0, after, 0), (1, before, 1)):
            copies[slot].wait_recv()
            ref = part_two(pair, to, half)
            ref[...] = (ref[...].astype(F32) + slot_two(pair, slot, half)[...].astype(F32)).astype(BF16)
            copies[slot + 4] = ring_two_copy(pair, slot + 4, ref)

    def second_end(pair, copies):
        place = places[1 - pair]
        halves = []
        for half, slots in ((0, (3, 4)), (1, (2, 5))):
            total = part_two(pair, place, half)[...].astype(F32)
            for slot in slots:
                copies[slot].wait_recv()
                total += slot_two(pair, slot, half)[...].astype(F32)
            halves.append(total.astype(BF16))
        shares[pair] = dot(share_moves[...], jnp.concatenate(halves, axis=0)).astype(BF16)
        last = []
        for step in range(1, 8):
            to = (z + step) % 8
            last.append(
                send(
                    shares.at[pair, pl.ds(to * SHARE_ROWS, SHARE_ROWS)], shares_in.at[pair, step - 1],
                    share_send.at[pair, step - 1], share_recv.at[pair, step - 1], along_z(step),
                )
            )
        return last

    def finish(pair, copies):
        own = pl.ds(pl.multiple_of(z * SHARE_ROWS, SHARE_ROWS), SHARE_ROWS)
        total = shares[pair, own, :].astype(F32)
        for step in range(1, 8):
            copies[step - 1].wait_recv()
            total += shares_in[pair, step - 1].astype(F32)
        total = total * grad_scale
        weight_grads[:, 2 * pair, :] = total[0:18, 0:144]
        weight_grads[:, 2 * pair + 1, :] = total[0:18, 144:288]

    def join_pairs(pairs, rows):
        for frame in range(FRAMES):
            rows[2 * frame : 2 * frame + 2, :] = pairs[frame].astype(F32)
        return rows[...].astype(BF16)

    def split_pairs(rows, pairs):
        for frame in range(FRAMES):
            pairs[frame] = rows[2 * frame : 2 * frame + 2, :].astype(BF16)

    loads[0].wait()
    loads[1].wait()
    tq[...] = join_pairs(tq_pairs, rows_one)
    tk[...] = join_pairs(tk_pairs, rows_two)
    row_patch = lax.broadcasted_iota(jnp.int32, (TOKENS, TOKENS), 0) % 2
    column_patch = lax.broadcasted_iota(jnp.int32, (TOKENS, TOKENS), 1) % 2
    softmax_heads(tq, tk, chance_t, jnp.where(row_patch == column_patch, 0.0, -1e30))
    loads[2].wait()
    loads[3].wait()
    cot[...] = join_pairs(cot_pairs, rows_wide)
    at_grad[...] = dot_nt(cot[...], weights[3]).astype(BF16)
    vt_grad[...] = attend_values_back(chance_t, at_grad).astype(BF16)
    loads[4].wait()
    loads[5].wait()
    out_z[1] = move_tokens(0, (cot[...].astype(F32) + dot(vt_grad[...], weights[2])).astype(BF16))
    pl.semaphore_wait(barrier, len(greeted))
    grad_z = start_z(1)

    for number in (6, 7, 8, 9, 10):
        loads[number].wait()
    sq[...] = sq_turned[...].T
    sk[...] = sk_turned[...].T
    value_s[...] = dot_nt(block[...], weights[0]).astype(BF16)
    softmax_heads(sq, sk, chance_s, None)
    attended_s[...] = attend(chance_s, value_s).astype(BF16)
    out_z[0] = move_tokens(0, (block[...].astype(F32) + dot(attended_s[...], weights[1])).astype(BF16))
    mixed_z = start_z(0)

    for number in (11, 12, 13):
        loads[number].wait()
    arrive(grad_z)
    out_plane[1] = move_tokens(1, in_z[1])
    grad_plane = start_plane(1)
    feature_copies, column_copies = {}, {}
    feature_copies[0] = start_features(0, block)
    feature_copies[3] = start_features(3, cot)
    column_copies[1] = start_columns(1, attended_s[...])
    column_copies[2] = start_columns(2, vt_grad[...])
    arrive(mixed_z)
    out_plane[0] = move_tokens(1, in_z[0])
    mixed_plane = start_plane(0)

    arrive(grad_plane)
    mixed_grad[...] = move_tokens(2, in_plane[1])
    feature_copies[1] = start_features(1, mixed_grad)
    as_grad[...] = dot_nt(mixed_grad[...], weights[1]).astype(BF16)
    vs_grad[...] = attend_values_back(chance_s, as_grad).astype(BF16)
    column_copies[0] = start_columns(0, vs_grad[...])

    arrive(mixed_plane)
    mixed[...] = move_tokens(2, in_plane[0])
    feature_copies[2] = start_features(2, mixed)
    value_t[...] = dot_nt(mixed[...], weights[2]).astype(BF16)
    attended_t[...] = attend(chance_t, value_t).astype(BF16)
    column_copies[3] = start_columns(3, attended_t[...])

    arrive([feature_copies[0], feature_copies[1], column_copies[0], column_copies[1]])
    first_s = first_ring(0)
    arrive([feature_copies[2], feature_copies[3], column_copies[2], column_copies[3]])
    first_t = first_ring(1)
    first_relay(0, first_s)
    query_part, key_part = attend_scores_back(chance_s, sq, sk, value_s, as_grad)
    sq_grad[...] = query_part.astype(BF16).T
    sk_grad[...] = key_part.astype(BF16).T
    first_relay(1, first_t)
    input_grad[...] = (mixed_grad[...].astype(F32) + dot(vs_grad[...], weights[0])).astype(BF16)
    query_part, key_part = attend_scores_back(chance_t, tq, tk, value_t, at_grad)
    rows_one[...] = query_part
    rows_two[...] = key_part
    split_pairs(rows_one, tq_grad)
    split_pairs(rows_two, tk_grad)

    first_end(0, first_s)
    second_s = second_ring(0)
    first_end(1, first_t)
    second_t = second_ring(1)
    second_relay(0, second_s)
    second_relay(1, second_t)
    last_s = second_end(0, second_s)
    last_t = second_end(1, second_t)
    finish(0, last_s)
    finish(1, last_t)
    for copy in sent:
        copy.wait_send()


def hand_over(*refs):
    semaphores = refs[12]
    copies = [pltpu.make_async_copy(refs[at], refs[6 + at], semaphores.at[at]) for at in range(6)]
    for copy in copies:
        copy.start()
    for copy in copies:
        copy.wait()


def body(
    block_input, spatial_queries, spatial_keys, cotangent, temporal_queries, temporal_keys, weights
):
    grad_scale = float(4 * 64 * 128) ** (-0.5)
    tables = make_tables()
    arrays = [
        block_input.reshape(TOKENS, WIDTH),
        spatial_queries.reshape(TOKENS, INNER).T,
        spatial_keys.reshape(TOKENS, INNER).T,
        cotangent.reshape(FRAMES, 2, WIDTH),
        temporal_queries.reshape(FRAMES, 2, INNER),
        temporal_keys.reshape(FRAMES, 2, INNER),
        weights.transpose(0, 2, 1),
    ] + tables
    wide, narrow = (TOKENS, WIDTH), (TOKENS, INNER)
    chances = pltpu.VMEM((HEADS, TOKENS, TOKENS), F32)
    dma = pltpu.SemaphoreType.DMA
    scratch = [pltpu.VMEM(array.shape, BF16) for array in arrays]
    scratch += [pltpu.VMEM(narrow, BF16)] * 2 + [pltpu.VMEM(wide, BF16)] + [pltpu.VMEM(narrow, BF16)] * 2
    scratch += [pltpu.VMEM(wide, F32)] + [pltpu.VMEM(narrow, F32)] * 2
    scratch += [chances, chances] + [pltpu.VMEM(narrow, BF16)] * 8
    scratch += [pltpu.VMEM(wide, BF16)] * 2 + [pltpu.VMEM((2,) + wide, BF16)] * 4
    scratch += [
        pltpu.VMEM((4, WIDTH, 2 * TOKENS), BF16),
        pltpu.VMEM((4, 2, 2 * TOKENS, LANES), BF16),
        pltpu.VMEM((4, 2, TOKENS, LANES), BF16),
        pltpu.VMEM((2, 2, 2, 4, ROW_BLOCK, LANES), BF16),
        pltpu.VMEM((2, 6, 2, ROW_BLOCK, LANES), BF16),
        pltpu.VMEM((2, 4, ROW_BLOCK, LANES), BF16),
        pltpu.VMEM((2, 6, CUT, LANES), BF16),
        pltpu.VMEM((2, 8 * SHARE_ROWS, LANES), BF16),
        pltpu.VMEM((2, 7, SHARE_ROWS, LANES), BF16),
    ]
    scratch += [dma((14,))] + [dma((2, 7))] * 4 + [dma((4,))] * 4 + [dma((2, 6))] * 4 + [dma((2, 7))] * 2
    results = [
        jax.ShapeDtypeStruct(wide, BF16),
        jax.ShapeDtypeStruct((INNER, TOKENS), BF16),
        jax.ShapeDtypeStruct((INNER, TOKENS), BF16),
        jax.ShapeDtypeStruct((FRAMES, 2, INNER), BF16),
        jax.ShapeDtypeStruct((FRAMES, 2, INNER), BF16),
        jax.ShapeDtypeStruct((18, 4, 144), F32),
    ]
    made = pl.pallas_call(
        functools.partial(kernel, grad_scale),
        out_shape=results,
        in_specs=[pl.BlockSpec(memory_space=pl.ANY)] * len(arrays),
        out_specs=[pl.BlockSpec(memory_space=pltpu.VMEM)] * 6,
        scratch_shapes=scratch,
        compiler_params=pltpu.CompilerParams(
            collective_id=0, has_side_effects=True, vmem_limit_bytes=56 * 2**20
        ),
        name="block_backward",
    )(*arrays)
    input_grad, sq_grad, sk_grad, tq_grad, tk_grad, weight_grads = pl.pallas_call(
        hand_over,
        out_shape=results,
        in_specs=[pl.BlockSpec(memory_space=pl.ANY)] * 6,
        out_specs=[pl.BlockSpec(memory_space=pl.ANY)] * 6,
        scratch_shapes=[pltpu.SemaphoreType.DMA((6,))],
        compiler_params=pltpu.CompilerParams(vmem_limit_bytes=60 * 2**20),
        name="hand_over",
    )(*made)
    return (
        input_grad.reshape(block_input.shape),
        sq_grad.T.reshape(spatial_queries.shape),
        sk_grad.T.reshape(spatial_keys.shape),
        tq_grad.reshape(temporal_queries.shape),
        tk_grad.reshape(temporal_keys.shape),
        weight_grads.transpose(1, 0, 2),
    )


def solution(mesh):
    placed = (
        P("dp", "seq", None, None),
        P("dp", "seq", None, None),
        P("dp", "seq", None, None),
        P("dp", None, "seq", None),
        P("dp", None, "seq", None),
        P("dp", None, "seq", None),
        P(),
    )
    return jax.shard_map(
        body,
        mesh=mesh,
        in_specs=placed,
        out_specs=(
            P("dp", "seq", None, None),
            P("dp", "seq", None, None),
            P("dp", "seq", None, None),
            P("dp", None, "seq", None),
            P("dp", None, "seq", None),
            P(None, "seq", "dp"),
        ),
        check_vma=False,
    )
```

```python
import functools

import jax
import jax.numpy as jnp
import numpy as np
from jax import lax
from jax.experimental import pallas as pl
from jax.experimental.pallas import tpu as pltpu
from jax.sharding import PartitionSpec as P

HEADS = 8
HEAD_DIM = 72
WIDTH = 1152
INNER = 576
TOKENS = 128
FRAMES = 64
SCORE_SCALE = HEAD_DIM ** (-0.5)
ROW_BLOCK = 144
LANES = 384
SHARE_ROWS = 32
CUT = 80
F32 = jnp.float32
BF16 = jnp.bfloat16
MESH = pl.DeviceIdType.MESH


def one_hot(source, size):
    table = np.zeros((len(source), size), np.float32)
    for row, at in enumerate(source):
        if at >= 0:
            table[row, at] = 1.0
    return table


def make_tables():
    def natural(y_lo, z, x, p):
        return 2 * (y_lo * 32 + z * 4 + x) + p

    to_z = [natural(y, z, x, p) for z in range(8) for y in range(2) for x in range(4) for p in range(2)]
    to_plane = [z * 16 + q * 2 + p for q in range(8) for z in range(8) for p in range(2)]
    to_natural = [
        (y * 4 + x) * 16 + z * 2 + p for y in range(2) for z in range(8) for x in range(4) for p in range(2)
    ]
    forth = [one_hot(order, TOKENS) for order in (to_z, to_plane, to_natural)]
    token_moves = np.stack(forth + [table.T for table in forth])
    feature_moves = np.stack(
        [
            one_hot(
                [y * 64 + z * 72 + x * 18 + r for x in range(4) for z in range(8) for r in range(18)], 640
            )
            for y in range(2)
        ]
    )
    picks = np.zeros((2, 2, 2, INNER, LANES), np.float32)
    for core in range(2):
        for matrix in range(2):
            for y_hi in range(2):
                for column in range(144):
                    picks[core, matrix, y_hi, (2 * y_hi + core) * 144 + column, matrix * 144 + column] = 1.0
    share_moves = one_hot([z * 18 + r if r < 18 else -1 for z in range(8) for r in range(SHARE_ROWS)], ROW_BLOCK)
    return [jnp.asarray(table, BF16) for table in (token_moves, feature_moves, picks, share_moves)]


def line_order(frame):
    y_lo, z, x = frame // 32, frame // 4 % 8, frame % 4
    start = 2 * (z * 8 + y_lo * 4 + x)
    return slice(start, start + 2)


def dot(left, right):
    return jnp.dot(left, right, preferred_element_type=F32)


def dot_nt(left, right):
    return lax.dot_general(left, right, (((1,), (1,)), ((), ())), preferred_element_type=F32)


def dot_tn(left, right):
    return lax.dot_general(left, right, (((0,), (0,)), ((), ())), preferred_element_type=F32)


def head_window(head):
    start = head * HEAD_DIM // 128 * 128
    stop = min(-(-(head * HEAD_DIM + HEAD_DIM) // 128) * 128, INNER)
    return start, stop


def head_mask(head):
    start, stop = head_window(head)
    lane = lax.broadcasted_iota(jnp.int32, (TOKENS, stop - start), 1) + start
    return (lane >= head * HEAD_DIM) & (lane < (head + 1) * HEAD_DIM)


def window(ref, head):
    start, stop = head_window(head)
    return ref[:, start:stop]


def masked_window(ref, head):
    return jnp.where(head_mask(head), window(ref, head).astype(F32), 0.0).astype(BF16)


def join_heads(parts):
    tiles = [None] * 5
    for head, part in enumerate(parts):
        start, stop = head_window(head)
        part = jnp.where(head_mask(head), part, 0.0)
        for at in range(start, stop, 128):
            piece = part[:, at - start : min(at - start + 128, stop - start)]
            tiles[at // 128] = piece if tiles[at // 128] is None else tiles[at // 128] + piece
    return jnp.concatenate(tiles, axis=1)


def softmax_heads(queries, key_rows, chance_ref, bias):
    for head in range(HEADS):
        scores = dot_nt(masked_window(queries, head), window(key_rows, head)) * SCORE_SCALE
        if bias is not None:
            scores = scores + bias
        powers = jnp.exp(scores - jnp.max(scores, axis=1, keepdims=True))
        chance_ref[head] = powers / jnp.sum(powers, axis=1, keepdims=True)


def attend(chance_ref, values):
    return join_heads([dot(chance_ref[h].astype(BF16), window(values, h)) for h in range(HEADS)])


def attend_values_back(chance_ref, out_grad):
    return join_heads([dot_tn(chance_ref[h].astype(BF16), window(out_grad, h)) for h in range(HEADS)])


def attend_scores_back(chance_ref, queries, key_rows, values, out_grad):
    query_parts, key_parts = [], []
    for head in range(HEADS):
        chance = chance_ref[head]
        chance_grad = dot_nt(masked_window(out_grad, head), window(values, head))
        centre = jnp.sum(chance * chance_grad, axis=1, keepdims=True)
        score_grad = (chance * (chance_grad - centre)).astype(BF16)
        query_parts.append(dot(score_grad, window(key_rows, head)))
        key_parts.append(dot_tn(score_grad, window(queries, head)))
    return join_heads(query_parts) * SCORE_SCALE, join_heads(key_parts) * SCORE_SCALE


def kernel(
    grad_scale,
    block_hbm, sq_hbm, sk_hbm, cot_hbm, tq_hbm, tk_hbm, weights_hbm,
    token_moves_hbm, feature_moves_hbm, picks_hbm, share_moves_hbm,
    input_grad, sq_grad, sk_grad, tq_grad, tk_grad, weight_grads,
    block, sq_turned, sk_turned, cot_pairs, tq_pairs, tk_pairs, weights, token_moves, feature_moves, picks, share_moves,
    sq, sk, cot, tq, tk, rows_wide, rows_one, rows_two,
    chance_s, chance_t, value_s, value_t, attended_s, attended_t, at_grad, as_grad, vt_grad, vs_grad,
    mixed, mixed_grad, cot_frame, vt_grad_frame,
    in_z_wide, out_plane_wide, in_plane_wide, out_plane, in_plane, out_z, in_z,
    factors, picked, picked_out, sums, arrived, sums_two, arrived_two, shares, shares_in,
    load_sem, z_send, z_recv, plane_send, plane_recv, factor_send, factor_recv, picked_send, picked_recv,
    ring_send, ring_recv, ring_two_send, ring_two_recv, share_send, share_recv,
):
    dp, seq = lax.axis_index("dp"), lax.axis_index("seq")
    y_hi, core = dp // 2, dp % 2
    y_lo, z, x = seq // 32, (seq // 4) % 8, seq % 4
    y = y_hi * 2 + y_lo
    q = y_lo * 4 + x

    def device(y_hi_at=y_hi, core_at=core, y_lo_at=y_lo, z_at=z, x_at=x):
        return (y_hi_at * 2 + core_at, y_lo_at * 32 + z_at * 4 + x_at)

    def along_z(step):
        return device(z_at=(z + step) % 8)

    def in_the_plane(step):
        to = (q + step) % 8
        return device(y_lo_at=to // 4, x_at=to % 4)

    def along_x(step):
        return device(x_at=(x + step) % 4)

    def along_y(step):
        to = (y + step) % 4
        return device(y_hi_at=to // 2, y_lo_at=to % 2)

    sibling = device(core_at=1 - core)

    loads = []
    for number, (source, target) in enumerate(
        [
            (cot_hbm, cot_pairs), (tq_hbm, tq_pairs), (tk_hbm, tk_pairs), (weights_hbm.at[3], weights.at[3]),
            (token_moves_hbm, token_moves), (block_hbm, block), (weights_hbm.at[0], weights.at[0]),
            (sq_hbm, sq_turned), (sk_hbm, sk_turned), (weights_hbm.at[1], weights.at[1]), (weights_hbm.at[2], weights.at[2]),
            (feature_moves_hbm, feature_moves), (picks_hbm, picks), (share_moves_hbm, share_moves),
        ]
    ):
        copy = pltpu.make_async_copy(source, target, load_sem.at[number])
        copy.start()
        loads.append(copy)

    barrier = pltpu.get_barrier_semaphore()
    greeted = [along_z(step) for step in range(1, 8)] + [in_the_plane(step) for step in range(1, 8)]
    greeted += [device(y_hi_at=1 - y_hi, y_lo_at=1 - y_lo), sibling]
    for peer in greeted:
        pl.semaphore_signal(barrier, inc=1, device_id=peer, device_id_type=MESH)

    sent = []

    def send(source, target, send_sem, recv_sem, peer):
        copy = pltpu.make_async_remote_copy(
            src_ref=source, dst_ref=target, send_sem=send_sem, recv_sem=recv_sem,
            device_id=peer, device_id_type=MESH,
        )
        copy.start()
        sent.append(copy)
        return copy

    def move_tokens(number, rows):
        return dot(token_moves[number], rows).astype(BF16)

    def start_z(item, source, target):
        copies = []
        for step in range(1, 8):
            to = (z + step) % 8
            copies.append(
                send(
                    source.at[pl.ds(to * 16, 16)], target.at[pl.ds(z * 16, 16)],
                    z_send.at[item, step - 1], z_recv.at[item, step - 1], along_z(step),
                )
            )
        own = pl.ds(pl.multiple_of(z * 16, 16), 16)
        target[own, :] = source[own, :]
        return copies

    def start_plane(item, source, target):
        copies = []
        for step in range(1, 8):
            to = (q + step) % 8
            copies.append(
                send(
                    source.at[pl.ds(to * 16, 16)], target.at[pl.ds(q * 16, 16)],
                    plane_send.at[item, step - 1], plane_recv.at[item, step - 1], in_the_plane(step),
                )
            )
        own = pl.ds(pl.multiple_of(q * 16, 16), 16)
        target[own, :] = source[own, :]
        return copies

    def arrive(copies):
        for copy in copies:
            copy.wait_recv()

    def start_features(number, rows_ref):
        for half in range(2):
            factors[number, half * INNER : (half + 1) * INNER, 0:TOKENS] = dot_nt(
                feature_moves[half], rows_ref[:, half * 512 : half * 512 + 640]
            ).astype(BF16)
        return send(
            factors.at[number, :, 0:TOKENS], factors.at[number, :, TOKENS : 2 * TOKENS],
            factor_send.at[number], factor_recv.at[number], sibling,
        )

    def start_columns(number, rows):
        for side in range(2):
            picked[number, side, 0:TOKENS, :] = dot(rows, picks[core, number % 2, side]).astype(BF16)
            picked_out[number, side] = dot(rows, picks[1 - core, number % 2, side]).astype(BF16)
        return send(
            picked_out.at[number], picked.at[number, :, TOKENS : 2 * TOKENS],
            picked_send.at[number], picked_recv.at[number], sibling,
        )

    def block_sum(pair, side, y_lo_at, x_at):
        rows = pl.ds(pl.multiple_of((y_lo_at * 4 + x_at) * ROW_BLOCK, 16), ROW_BLOCK)
        total = dot(factors[2 * pair, rows, :], picked[2 * pair, side])
        total += dot(factors[2 * pair + 1, rows, :], picked[2 * pair + 1, side])
        sums[pair, side, y_lo_at, x_at] = total.astype(BF16)

    def piece(pair, to, half):
        if pair == 0:
            return sums.at[0, half, :, to]
        return sums.at[1, to // 2, to % 2, 2 * half : 2 * half + 2]

    def make_pieces(pair, to):
        if pair == 0:
            for side in range(2):
                for y_lo_at in range(2):
                    block_sum(0, side, y_lo_at, to)
        else:
            for x_at in range(4):
                block_sum(1, to // 2, to % 2, x_at)

    places = (x, y)
    rings = (along_x, along_y)

    def ring_copy(pair, slot, source):
        peer = rings[pair](1 if slot % 2 == 0 else -1 + 4)
        return send(source, arrived.at[pair, slot], ring_send.at[pair, slot], ring_recv.at[pair, slot], peer)

    def first_ring(pair):
        place = places[pair]
        after, across, before = (place + 1) % 4, (place + 2) % 4, (place + 3) % 4
        copies = {}
        make_pieces(pair, across)
        copies[0] = ring_copy(pair, 0, piece(pair, across, 0))
        copies[1] = ring_copy(pair, 1, piece(pair, across, 1))
        make_pieces(pair, after)
        copies[2] = ring_copy(pair, 2, piece(pair, after, 1))
        make_pieces(pair, before)
        copies[3] = ring_copy(pair, 3, piece(pair, before, 0))
        make_pieces(pair, place)
        return copies

    def first_relay(pair, copies):
        place = places[pair]
        after, before = (place + 1) % 4, (place + 3) % 4
        for slot, to, half in ((0, after, 0), (1, before, 1)):
            copies[slot].wait_recv()
            ref = piece(pair, to, half)
            ref[...] = (ref[...].astype(F32) + arrived[pair, slot].astype(F32)).astype(BF16)
            copies[slot + 4] = ring_copy(pair, slot + 4, ref)

    def first_end(pair, copies):
        for half, slots in ((0, (3, 4)), (1, (2, 5))):
            total = piece(pair, places[pair], half)[...].astype(F32)
            for slot in slots:
                copies[slot].wait_recv()
                total += arrived[pair, slot].astype(F32)
            sums_two[pair, 2 * half : 2 * half + 2] = total.astype(BF16)

    def part_two(pair, to, half):
        return sums_two.at[pair, to, 0:CUT] if half == 0 else sums_two.at[pair, to, CUT:ROW_BLOCK]

    def slot_two(pair, slot, half):
        return arrived_two.at[pair, slot, 0 : (CUT if half == 0 else ROW_BLOCK - CUT)]

    slot_half = (0, 1, 1, 0, 0, 1)

    def ring_two_copy(pair, slot, source):
        peer = rings[1 - pair](1 if slot % 2 == 0 else -1 + 4)
        return send(
            source, slot_two(pair, slot, slot_half[slot]),
            ring_two_send.at[pair, slot], ring_two_recv.at[pair, slot], peer,
        )

    def second_ring(pair):
        place = places[1 - pair]
        after, across, before = (place + 1) % 4, (place + 2) % 4, (place + 3) % 4
        copies = {}
        copies[0] = ring_two_copy(pair, 0, part_two(pair, across, 0))
        copies[1] = ring_two_copy(pair, 1, part_two(pair, across, 1))
        copies[2] = ring_two_copy(pair, 2, part_two(pair, after, 1))
        copies[3] = ring_two_copy(pair, 3, part_two(pair, before, 0))
        return copies

    def second_relay(pair, copies):
        place = places[1 - pair]
        after, before = (place + 1) % 4, (place + 3) % 4
        for slot, to, half in ((0, after, 0), (1, before, 1)):
            copies[slot].wait_recv()
            ref = part_two(pair, to, half)
            ref[...] = (ref[...].astype(F32) + slot_two(pair, slot, half)[...].astype(F32)).astype(BF16)
            copies[slot + 4] = ring_two_copy(pair, slot + 4, ref)

    def second_end(pair, copies):
        place = places[1 - pair]
        halves = []
        for half, slots in ((0, (3, 4)), (1, (2, 5))):
            total = part_two(pair, place, half)[...].astype(F32)
            for slot in slots:
                copies[slot].wait_recv()
                total += slot_two(pair, slot, half)[...].astype(F32)
            halves.append(total.astype(BF16))
        shares[pair] = dot(share_moves[...], jnp.concatenate(halves, axis=0)).astype(BF16)
        last = []
        for step in range(1, 8):
            to = (z + step) % 8
            last.append(
                send(
                    shares.at[pair, pl.ds(to * SHARE_ROWS, SHARE_ROWS)], shares_in.at[pair, step - 1],
                    share_send.at[pair, step - 1], share_recv.at[pair, step - 1], along_z(step),
                )
            )
        return last

    def finish(pair, copies):
        own = pl.ds(pl.multiple_of(z * SHARE_ROWS, SHARE_ROWS), SHARE_ROWS)
        total = shares[pair, own, :].astype(F32)
        for step in range(1, 8):
            copies[step - 1].wait_recv()
            total += shares_in[pair, step - 1].astype(F32)
        total = total * grad_scale
        weight_grads[:, 2 * pair, :] = total[0:18, 0:144]
        weight_grads[:, 2 * pair + 1, :] = total[0:18, 144:288]

    def join_pairs(pairs, rows):
        for frame in range(FRAMES):
            rows[line_order(frame), :] = pairs[frame].astype(F32)
        return rows[...].astype(BF16)

    def split_pairs(rows, pairs):
        for frame in range(FRAMES):
            pairs[frame] = rows[line_order(frame), :].astype(BF16)

    loads[0].wait()
    cot[...] = join_pairs(cot_pairs, rows_wide)
    pl.semaphore_wait(barrier, len(greeted))
    cot_z = start_z(0, cot, in_z_wide)
    loads[1].wait()
    loads[2].wait()
    tq[...] = join_pairs(tq_pairs, rows_one)
    tk[...] = join_pairs(tk_pairs, rows_two)
    row_patch = lax.broadcasted_iota(jnp.int32, (TOKENS, TOKENS), 0) % 2
    column_patch = lax.broadcasted_iota(jnp.int32, (TOKENS, TOKENS), 1) % 2
    softmax_heads(tq, tk, chance_t, jnp.where(row_patch == column_patch, 0.0, -1e30))
    loads[3].wait()
    loads[4].wait()
    at_grad[...] = dot_nt(cot[...], weights[3]).astype(BF16)
    vt_grad[...] = attend_values_back(chance_t, at_grad).astype(BF16)
    out_plane[0] = move_tokens(1, vt_grad[...])
    grad_plane = start_plane(1, out_plane.at[0], in_plane.at[0])

    for number in (5, 6, 7, 8, 9, 10):
        loads[number].wait()
    sq[...] = sq_turned[...].T
    sk[...] = sk_turned[...].T
    value_s[...] = dot_nt(block[...], weights[0]).astype(BF16)
    softmax_heads(sq, sk, chance_s, None)
    attended_s[...] = attend(chance_s, value_s).astype(BF16)
    mixed[...] = (block[...].astype(F32) + dot(attended_s[...], weights[1])).astype(BF16)
    out_plane[1] = move_tokens(5, dot_nt(mixed[...], weights[2]).astype(BF16))
    value_plane = start_plane(2, out_plane.at[1], in_plane.at[1])

    arrive(grad_plane)
    out_z[0] = move_tokens(4, in_plane[0])
    grad_z = start_z(1, out_z.at[0], in_z.at[0])
    for number in (11, 12, 13):
        loads[number].wait()
    feature_copies, column_copies = {}, {}
    feature_copies[0] = start_features(0, block)
    column_copies[1] = start_columns(1, attended_s[...])
    arrive(cot_z)
    out_plane_wide[...] = move_tokens(1, in_z_wide[...])
    cot_plane = start_plane(0, out_plane_wide, in_plane_wide)
    arrive(value_plane)
    out_z[1] = move_tokens(4, in_plane[1])
    value_z = start_z(2, out_z.at[1], in_z.at[1])
    feature_copies[2] = start_features(2, mixed)
    feature_copies[3] = start_features(3, cot)

    arrive(cot_plane)
    cot_frame[...] = move_tokens(2, in_plane_wide[...])
    arrive(grad_z)
    vt_grad_frame[...] = move_tokens(3, in_z[0])
    mixed_grad[...] = (cot_frame[...].astype(F32) + dot(vt_grad_frame[...], weights[2])).astype(BF16)
    feature_copies[1] = start_features(1, mixed_grad)
    as_grad[...] = dot_nt(mixed_grad[...], weights[1]).astype(BF16)
    vs_grad[...] = attend_values_back(chance_s, as_grad).astype(BF16)
    column_copies[0] = start_columns(0, vs_grad[...])
    column_copies[2] = start_columns(2, vt_grad_frame[...])

    arrive([feature_copies[0], feature_copies[1], column_copies[0], column_copies[1]])
    first_s = first_ring(0)
    arrive(value_z)
    value_t[...] = in_z[1]
    attended_t[...] = attend(chance_t, value_t).astype(BF16)
    column_copies[3] = start_columns(3, attended_t[...])
    arrive([feature_copies[2], feature_copies[3], column_copies[2], column_copies[3]])
    first_t = first_ring(1)
    first_relay(0, first_s)
    query_part, key_part = attend_scores_back(chance_s, sq, sk, value_s, as_grad)
    sq_grad[...] = query_part.astype(BF16).T
    sk_grad[...] = key_part.astype(BF16).T
    first_relay(1, first_t)
    input_grad[...] = (mixed_grad[...].astype(F32) + dot(vs_grad[...], weights[0])).astype(BF16)
    query_part, key_part = attend_scores_back(chance_t, tq, tk, value_t, at_grad)
    rows_one[...] = query_part
    rows_two[...] = key_part
    split_pairs(rows_one, tq_grad)
    split_pairs(rows_two, tk_grad)

    first_end(0, first_s)
    second_s = second_ring(0)
    first_end(1, first_t)
    second_t = second_ring(1)
    second_relay(0, second_s)
    second_relay(1, second_t)
    last_s = second_end(0, second_s)
    last_t = second_end(1, second_t)
    finish(0, last_s)
    finish(1, last_t)
    for copy in sent:
        copy.wait_send()


def hand_over(*refs):
    for at in range(6):
        refs[6 + at][...] = refs[at][...]


def body(
    block_input, spatial_queries, spatial_keys, cotangent, temporal_queries, temporal_keys, weights
):
    grad_scale = float(4 * 64 * 128) ** (-0.5)
    tables = make_tables()
    arrays = [
        block_input.reshape(TOKENS, WIDTH),
        spatial_queries.reshape(TOKENS, INNER).T,
        spatial_keys.reshape(TOKENS, INNER).T,
        cotangent.reshape(FRAMES, 2, WIDTH),
        temporal_queries.reshape(FRAMES, 2, INNER),
        temporal_keys.reshape(FRAMES, 2, INNER),
        weights.transpose(0, 2, 1),
    ] + tables
    wide, narrow = (TOKENS, WIDTH), (TOKENS, INNER)
    chances = pltpu.VMEM((HEADS, TOKENS, TOKENS), F32)
    dma = pltpu.SemaphoreType.DMA
    scratch = [pltpu.VMEM(array.shape, BF16) for array in arrays]
    scratch += [pltpu.VMEM(narrow, BF16)] * 2 + [pltpu.VMEM(wide, BF16)] + [pltpu.VMEM(narrow, BF16)] * 2
    scratch += [pltpu.VMEM(wide, F32)] + [pltpu.VMEM(narrow, F32)] * 2
    scratch += [chances, chances] + [pltpu.VMEM(narrow, BF16)] * 8
    scratch += [pltpu.VMEM(wide, BF16)] * 3 + [pltpu.VMEM(narrow, BF16)]
    scratch += [pltpu.VMEM(wide, BF16)] * 3 + [pltpu.VMEM((2,) + narrow, BF16)] * 4
    scratch += [
        pltpu.VMEM((4, WIDTH, 2 * TOKENS), BF16),
        pltpu.VMEM((4, 2, 2 * TOKENS, LANES), BF16),
        pltpu.VMEM((4, 2, TOKENS, LANES), BF16),
        pltpu.VMEM((2, 2, 2, 4, ROW_BLOCK, LANES), BF16),
        pltpu.VMEM((2, 6, 2, ROW_BLOCK, LANES), BF16),
        pltpu.VMEM((2, 4, ROW_BLOCK, LANES), BF16),
        pltpu.VMEM((2, 6, CUT, LANES), BF16),
        pltpu.VMEM((2, 8 * SHARE_ROWS, LANES), BF16),
        pltpu.VMEM((2, 7, SHARE_ROWS, LANES), BF16),
    ]
    scratch += [dma((14,))] + [dma((3, 7))] * 4 + [dma((4,))] * 4 + [dma((2, 6))] * 4 + [dma((2, 7))] * 2
    results = [
        jax.ShapeDtypeStruct(wide, BF16),
        jax.ShapeDtypeStruct((INNER, TOKENS), BF16),
        jax.ShapeDtypeStruct((INNER, TOKENS), BF16),
        jax.ShapeDtypeStruct((FRAMES, 2, INNER), BF16),
        jax.ShapeDtypeStruct((FRAMES, 2, INNER), BF16),
        jax.ShapeDtypeStruct((18, 4, 144), F32),
    ]
    made = pl.pallas_call(
        functools.partial(kernel, grad_scale),
        out_shape=results,
        in_specs=[pl.BlockSpec(memory_space=pl.ANY)] * len(arrays),
        out_specs=[pl.BlockSpec(memory_space=pltpu.VMEM)] * 6,
        scratch_shapes=scratch,
        compiler_params=pltpu.CompilerParams(
            collective_id=0, has_side_effects=True, vmem_limit_bytes=56 * 2**20
        ),
        name="block_backward",
    )(*arrays)
    input_grad, sq_grad, sk_grad, tq_grad, tk_grad, weight_grads = pl.pallas_call(
        hand_over,
        out_shape=results,
        in_specs=[pl.BlockSpec(memory_space=pltpu.VMEM)] * 6,
        out_specs=[pl.BlockSpec(memory_space=pltpu.VMEM)] * 6,
        compiler_params=pltpu.CompilerParams(vmem_limit_bytes=60 * 2**20),
        name="hand_over",
    )(*made)
    return (
        input_grad.reshape(block_input.shape),
        sq_grad.T.reshape(spatial_queries.shape),
        sk_grad.T.reshape(spatial_keys.shape),
        tq_grad.reshape(temporal_queries.shape),
        tk_grad.reshape(temporal_keys.shape),
        weight_grads.transpose(1, 0, 2),
    )


def solution(mesh):
    placed = (
        P("dp", "seq", None, None),
        P("dp", "seq", None, None),
        P("dp", "seq", None, None),
        P("dp", None, "seq", None),
        P("dp", None, "seq", None),
        P("dp", None, "seq", None),
        P(),
    )
    return jax.shard_map(
        body,
        mesh=mesh,
        in_specs=placed,
        out_specs=(
            P("dp", "seq", None, None),
            P("dp", "seq", None, None),
            P("dp", "seq", None, None),
            P("dp", None, "seq", None),
            P("dp", None, "seq", None),
            P(None, "seq", "dp"),
        ),
        check_vma=False,
    )
```

```python
import functools

import jax
import jax.numpy as jnp
import numpy as np
from jax import lax
from jax.experimental import pallas as pl
from jax.experimental.pallas import tpu as pltpu
from jax.sharding import PartitionSpec as P

HEADS = 8
HEAD_DIM = 72
WIDTH = 1152
INNER = 576
TOKENS = 128
FRAMES = 64
SCORE_SCALE = HEAD_DIM ** (-0.5)
ROW_BLOCK = 144
LANES = 384
PIECE = 9 * ROW_BLOCK
CUT = 640
BLOCK_ROWS = 2 * ROW_BLOCK + 48
SHARE_ROWS = 96
PAIRS = ((1, 2), (0, 3))
F32 = jnp.float32
BF16 = jnp.bfloat16
MESH = pl.DeviceIdType.MESH


def one_hot(source, size):
    table = np.zeros((len(source), size), np.float32)
    for row, at in enumerate(source):
        if at >= 0:
            table[row, at] = 1.0
    return table


def make_tables():
    def natural(y_lo, z, x, p):
        return 2 * (y_lo * 32 + z * 4 + x) + p

    to_z = [natural(y, z, x, p) for z in range(8) for y in range(2) for x in range(4) for p in range(2)]
    to_plane = [z * 16 + q * 2 + p for q in range(8) for z in range(8) for p in range(2)]
    to_natural = [
        (y * 4 + x) * 16 + z * 2 + p for y in range(2) for z in range(8) for x in range(4) for p in range(2)
    ]
    forth = [one_hot(order, TOKENS) for order in (to_z, to_plane, to_natural)]
    token_moves = np.stack(forth + [table.T for table in forth])
    feature_moves = np.stack(
        [
            one_hot(
                [y * 64 + z * 72 + x * 18 + r for x in range(4) for z in range(8) for r in range(18)], 640
            )
            for y in range(2)
        ]
    )
    picks = np.zeros((2, 2, 2, INNER, LANES), np.float32)
    for core in range(2):
        for matrix in range(2):
            for y_hi in range(2):
                for column in range(144):
                    picks[core, matrix, y_hi, (2 * y_hi + core) * 144 + column, matrix * 144 + column] = 1.0
    share_moves = one_hot(
        [
            part * 144 + z * 18 + r if part < 4 else -1
            for z in range(8)
            for part, r in [divmod(row, 18) for row in range(80)]
        ],
        4 * ROW_BLOCK,
    )
    rest_moves = []
    for group in range(4):
        source = []
        for z in range(8):
            for row in range(16):
                at = z * 18 + 9 * (group % 2) + row
                place, turn = at // 16, (group - at // 16) % 4
                source.append(turn * 48 + place // 4 * 16 + at % 16 if row < 9 else -1)
        rest_moves.append(one_hot(source, 192))
    tables = (token_moves, feature_moves, picks, share_moves, np.stack(rest_moves))
    return [jnp.asarray(table, BF16) for table in tables]


def line_order(frame):
    y_lo, z, x = frame // 32, frame // 4 % 8, frame % 4
    start = 2 * (z * 8 + y_lo * 4 + x)
    return slice(start, start + 2)


def dot(left, right):
    return jnp.dot(left, right, preferred_element_type=F32)


def dot_nt(left, right):
    return lax.dot_general(left, right, (((1,), (1,)), ((), ())), preferred_element_type=F32)


def dot_tn(left, right):
    return lax.dot_general(left, right, (((0,), (0,)), ((), ())), preferred_element_type=F32)


def head_window(head):
    start = head * HEAD_DIM // 128 * 128
    stop = min(-(-(head * HEAD_DIM + HEAD_DIM) // 128) * 128, INNER)
    return start, stop


def head_mask(head):
    start, stop = head_window(head)
    lane = lax.broadcasted_iota(jnp.int32, (TOKENS, stop - start), 1) + start
    return (lane >= head * HEAD_DIM) & (lane < (head + 1) * HEAD_DIM)


def window(ref, head):
    start, stop = head_window(head)
    return ref[:, start:stop]


def masked_window(ref, head):
    return jnp.where(head_mask(head), window(ref, head).astype(F32), 0.0).astype(BF16)


def join_heads(parts):
    tiles = [None] * 5
    for head, part in enumerate(parts):
        start, stop = head_window(head)
        part = jnp.where(head_mask(head), part, 0.0)
        for at in range(start, stop, 128):
            piece = part[:, at - start : min(at - start + 128, stop - start)]
            tiles[at // 128] = piece if tiles[at // 128] is None else tiles[at // 128] + piece
    return jnp.concatenate(tiles, axis=1)


def softmax_heads(queries, key_rows, chance_ref, bias):
    for head in range(HEADS):
        scores = dot_nt(masked_window(queries, head), window(key_rows, head)) * SCORE_SCALE
        if bias is not None:
            scores = scores + bias
        powers = jnp.exp(scores - jnp.max(scores, axis=1, keepdims=True))
        chance_ref[head] = powers / jnp.sum(powers, axis=1, keepdims=True)


def attend(chance_ref, values):
    return join_heads([dot(chance_ref[h].astype(BF16), window(values, h)) for h in range(HEADS)])


def attend_values_back(chance_ref, out_grad):
    return join_heads([dot_tn(chance_ref[h].astype(BF16), window(out_grad, h)) for h in range(HEADS)])


def attend_scores_back(chance_ref, queries, key_rows, values, out_grad):
    query_parts, key_parts = [], []
    for head in range(HEADS):
        chance = chance_ref[head]
        chance_grad = dot_nt(masked_window(out_grad, head), window(values, head))
        centre = jnp.sum(chance * chance_grad, axis=1, keepdims=True)
        score_grad = (chance * (chance_grad - centre)).astype(BF16)
        query_parts.append(dot(score_grad, window(key_rows, head)))
        key_parts.append(dot_tn(score_grad, window(queries, head)))
    return join_heads(query_parts) * SCORE_SCALE, join_heads(key_parts) * SCORE_SCALE


def kernel(
    grad_scale,
    block_hbm, sq_hbm, sk_hbm, cot_hbm, tq_hbm, tk_hbm, weights_hbm,
    token_moves_hbm, feature_moves_hbm, picks_hbm, share_moves_hbm, rest_moves_hbm,
    input_grad, sq_grad, sk_grad, tq_grad, tk_grad, weight_grads,
    block, sq_turned, sk_turned, cot_pairs, tq_pairs, tk_pairs, weights, token_moves, feature_moves, picks, share_moves, rest_moves,
    sq, sk, cot, tq, tk, rows_wide, rows_one, rows_two,
    chance_s, chance_t, value_s, value_t, attended_s, attended_t, at_grad, as_grad, vt_grad, vs_grad,
    mixed, mixed_grad, cot_frame, vt_grad_frame,
    in_z_wide, out_plane_wide, in_plane_wide, out_plane, in_plane, out_z, in_z,
    factors, picked, picked_out, sums, arrived, total_one, sums_two, arrived_two, shares, shares_in, total_share,
    load_sem, z_send, z_recv, plane_send, plane_recv, factor_send, factor_recv, picked_send, picked_recv,
    ring_send, ring_recv, ring_two_send, ring_two_recv, share_send, share_recv,
):
    dp, seq = lax.axis_index("dp"), lax.axis_index("seq")
    y_hi, core = dp // 2, dp % 2
    y_lo, z, x = seq // 32, (seq // 4) % 8, seq % 4
    y = y_hi * 2 + y_lo
    q = y_lo * 4 + x

    def device(y_hi_at=y_hi, core_at=core, y_lo_at=y_lo, z_at=z, x_at=x):
        return (y_hi_at * 2 + core_at, y_lo_at * 32 + z_at * 4 + x_at)

    def along_z(step):
        return device(z_at=(z + step) % 8)

    def in_the_plane(step):
        to = (q + step) % 8
        return device(y_lo_at=to // 4, x_at=to % 4)

    def along_x(step):
        return device(x_at=(x + step) % 4)

    def along_y(step):
        to = (y + step) % 4
        return device(y_hi_at=to // 2, y_lo_at=to % 2)

    sibling = device(core_at=1 - core)

    loads = []
    for number, (source, target) in enumerate(
        [
            (cot_hbm, cot_pairs), (tq_hbm, tq_pairs), (tk_hbm, tk_pairs), (weights_hbm.at[3], weights.at[3]),
            (token_moves_hbm, token_moves), (block_hbm, block), (weights_hbm.at[0], weights.at[0]),
            (sq_hbm, sq_turned), (sk_hbm, sk_turned), (weights_hbm.at[1], weights.at[1]), (weights_hbm.at[2], weights.at[2]),
            (feature_moves_hbm, feature_moves), (picks_hbm, picks), (share_moves_hbm, share_moves),
            (rest_moves_hbm, rest_moves),
        ]
    ):
        copy = pltpu.make_async_copy(source, target, load_sem.at[number])
        if number < 11:
            copy.start()
        loads.append(copy)

    barrier = pltpu.get_barrier_semaphore()
    greeted = [along_z(step) for step in range(1, 8)] + [in_the_plane(step) for step in range(1, 8)]
    greeted += [device(y_hi_at=1 - y_hi, y_lo_at=1 - y_lo), sibling]
    for peer in greeted:
        pl.semaphore_signal(barrier, inc=1, device_id=peer, device_id_type=MESH)

    sent = []

    def send(source, target, send_sem, recv_sem, peer):
        copy = pltpu.make_async_remote_copy(
            src_ref=source, dst_ref=target, send_sem=send_sem, recv_sem=recv_sem,
            device_id=peer, device_id_type=MESH,
        )
        copy.start()
        sent.append(copy)
        return copy

    def move_tokens(number, rows):
        return dot(token_moves[number], rows).astype(BF16)

    def start_z(item, source, target):
        copies = []
        for step in range(1, 8):
            to = (z + step) % 8
            copies.append(
                send(
                    source.at[pl.ds(to * 16, 16)], target.at[pl.ds(z * 16, 16)],
                    z_send.at[item, step - 1], z_recv.at[item, step - 1], along_z(step),
                )
            )
        own = pl.ds(pl.multiple_of(z * 16, 16), 16)
        target[own, :] = source[own, :]
        return copies

    def start_plane(item, source, target):
        copies = []
        for step in range(1, 8):
            to = (q + step) % 8
            copies.append(
                send(
                    source.at[pl.ds(to * 16, 16)], target.at[pl.ds(q * 16, 16)],
                    plane_send.at[item, step - 1], plane_recv.at[item, step - 1], in_the_plane(step),
                )
            )
        own = pl.ds(pl.multiple_of(q * 16, 16), 16)
        target[own, :] = source[own, :]
        return copies

    def arrive(copies):
        for copy in copies:
            copy.wait_recv()

    def start_features(number, rows_ref):
        for half in range(2):
            factors[number, half * INNER : (half + 1) * INNER, 0:TOKENS] = dot_nt(
                feature_moves[half], rows_ref[:, half * 512 : half * 512 + 640]
            ).astype(BF16)
        return send(
            factors.at[number, :, 0:TOKENS], factors.at[number, :, TOKENS : 2 * TOKENS],
            factor_send.at[number], factor_recv.at[number], sibling,
        )

    def start_columns(number, rows):
        for side in range(2):
            place = 0 if number < 2 else 1
            picked[number, side, 0:TOKENS, :] = dot(rows, picks[core, place, side]).astype(BF16)
            picked_out[number, side] = dot(rows, picks[1 - core, place, side]).astype(BF16)
        return send(
            picked_out.at[number], picked.at[number, :, TOKENS : 2 * TOKENS],
            picked_send.at[number], picked_recv.at[number], sibling,
        )

    def make_pieces(pair, to):
        rests = None
        for sub in range(4):
            side, y_lo_at, x_at = (sub // 2, sub % 2, to) if pair == 0 else (to // 2, to % 2, sub)
            rows = pl.ds(pl.multiple_of((y_lo_at * 4 + x_at) * ROW_BLOCK, 16), ROW_BLOCK)
            one, two = PAIRS[pair]
            total = dot(factors[one, rows, :], picked[one, side]) + dot(factors[two, rows, :], picked[two, side])
            at = 2 * sub * ROW_BLOCK
            sums[pair, to, at : at + ROW_BLOCK, :] = total[:, 0:128].astype(BF16)
            sums[pair, to, at + ROW_BLOCK : at + 2 * ROW_BLOCK, :] = total[:, 128:256].astype(BF16)
            rest = total[:, 256:384]
            rests = rest if sub == 0 else rests + pltpu.roll(rest, 32 * sub, 1)
        sums[pair, to, 8 * ROW_BLOCK : PIECE, :] = rests.astype(BF16)

    def piece(pair, to, half):
        return sums.at[pair, to, 0:CUT] if half == 0 else sums.at[pair, to, CUT:PIECE]

    slot_half = (0, 1, 1, 0, 0, 1)

    def slot_ref(pair, slot):
        return arrived.at[pair, slot, 0 : (CUT if slot_half[slot] == 0 else PIECE - CUT)]

    places = (x, y)
    rings = (along_x, along_y)

    def ring_copy(pair, slot, source):
        peer = rings[pair](1 if slot % 2 == 0 else -1 + 4)
        return send(source, slot_ref(pair, slot), ring_send.at[pair, slot], ring_recv.at[pair, slot], peer)

    def first_ring(pair):
        place = places[pair]
        after, across, before = (place + 1) % 4, (place + 2) % 4, (place + 3) % 4
        copies = {}
        make_pieces(pair, across)
        copies[0] = ring_copy(pair, 0, piece(pair, across, 0))
        copies[1] = ring_copy(pair, 1, piece(pair, across, 1))
        make_pieces(pair, after)
        copies[2] = ring_copy(pair, 2, piece(pair, after, 1))
        make_pieces(pair, before)
        copies[3] = ring_copy(pair, 3, piece(pair, before, 0))
        make_pieces(pair, place)
        return copies

    def first_relay(pair, copies):
        place = places[pair]
        after, before = (place + 1) % 4, (place + 3) % 4
        for slot, to, half in ((0, after, 0), (1, before, 1)):
            copies[slot].wait_recv()
            ref = piece(pair, to, half)
            ref[...] = (ref[...].astype(F32) + slot_ref(pair, slot)[...].astype(F32)).astype(BF16)
            copies[slot + 4] = ring_copy(pair, slot + 4, ref)

    lane_group = lax.broadcasted_iota(jnp.int32, (16, 128), 1) // 32

    def first_end(pair, copies):
        for half, slots in ((0, (3, 4)), (1, (2, 5))):
            total = piece(pair, places[pair], half)[...].astype(F32)
            for slot in slots:
                copies[slot].wait_recv()
                total += slot_ref(pair, slot)[...].astype(F32)
            total_one[(0 if half == 0 else CUT) : (CUT if half == 0 else PIECE), :] = total
        for sub in range(4):
            at = 2 * sub * ROW_BLOCK
            sums_two[pair, sub, 0 : 2 * ROW_BLOCK, :] = total_one[at : at + 2 * ROW_BLOCK, :].astype(BF16)
            for tile in range(3):
                packed = jnp.zeros((16, 128), F32)
                for group in range(4 if tile < 2 else 1):
                    start = 8 * ROW_BLOCK + 16 * (4 * tile + group)
                    rest = pltpu.roll(total_one[start : start + 16, :], 32 * ((group - sub) % 4), 1)
                    packed = jnp.where(lane_group == group, rest, packed)
                start = 2 * ROW_BLOCK + 16 * tile
                sums_two[pair, sub, start : start + 16, :] = packed.astype(BF16)

    def second_ring(pair):
        place = places[1 - pair]
        copies = []
        for step in range(1, 4):
            copies.append(
                send(
                    sums_two.at[pair, (place + step) % 4], arrived_two.at[pair, step - 1],
                    ring_two_send.at[pair, step - 1], ring_two_recv.at[pair, step - 1], rings[1 - pair](step),
                )
            )
        return copies

    def second_end(pair, copies):
        total = sums_two[pair, places[1 - pair]].astype(F32)
        for step in range(1, 4):
            copies[step - 1].wait_recv()
            total += arrived_two[pair, step - 1].astype(F32)
        return total

    def last_line(totals):
        whole = jnp.concatenate([total[0 : 2 * ROW_BLOCK] for total in totals], axis=0).astype(BF16)
        moved = dot(share_moves[...], whole).astype(BF16)
        rest = jnp.zeros((TOKENS, 128), F32)
        lanes = lax.broadcasted_iota(jnp.int32, (TOKENS, 128), 1) // 32
        for pair, total in enumerate(totals):
            ends = total[2 * ROW_BLOCK : BLOCK_ROWS]
            turned = [ends] + [pltpu.roll(ends, 32 * turn, 1) for turn in range(1, 4)]
            turned = jnp.concatenate(turned, axis=0).astype(BF16)
            for group in (2 * pair, 2 * pair + 1):
                rest = jnp.where(lanes == group, dot(rest_moves[group], turned), rest)
        rest = rest.astype(BF16)
        for z_at in range(8):
            shares[z_at, 0:80, :] = moved[80 * z_at : 80 * z_at + 80]
            shares[z_at, 80:96, :] = rest[16 * z_at : 16 * z_at + 16]
        copies = []
        for step in range(1, 8):
            copies.append(
                send(
                    shares.at[(z + step) % 8], shares_in.at[step - 1],
                    share_send.at[step - 1], share_recv.at[step - 1], along_z(step),
                )
            )
        return copies

    def finish(copies):
        total = shares[z].astype(F32)
        for step in range(1, 8):
            copies[step - 1].wait_recv()
            total += shares_in[step - 1].astype(F32)
        total_share[...] = total * grad_scale
        for pair, (one, two) in enumerate(PAIRS):
            left = total_share[36 * pair : 36 * pair + 18, :]
            right = total_share[36 * pair + 18 : 36 * pair + 36, :]
            weight_grads[:, one, 0:128] = left
            weight_grads[:, one, 128:144] = right[:, 0:16]
            weight_grads[:, two, 0:112] = right[:, 16:128]
            for half in range(2):
                start = 64 * pair + 32 * half
                weight_grads[9 * half : 9 * half + 9, two, 112:144] = total_share[80:89, start : start + 32]

    def join_pairs(pairs, rows):
        for frame in range(FRAMES):
            rows[line_order(frame), :] = pairs[frame].astype(F32)
        return rows[...].astype(BF16)

    def split_pairs(rows, pairs):
        for frame in range(FRAMES):
            pairs[frame] = rows[line_order(frame), :].astype(BF16)

    loads[0].wait()
    cot[...] = join_pairs(cot_pairs, rows_wide)
    pl.semaphore_wait(barrier, len(greeted))
    cot_z = start_z(0, cot, in_z_wide)
    for copy in loads[11:]:
        copy.start()
    loads[1].wait()
    loads[2].wait()
    tq[...] = join_pairs(tq_pairs, rows_one)
    tk[...] = join_pairs(tk_pairs, rows_two)
    row_patch = lax.broadcasted_iota(jnp.int32, (TOKENS, TOKENS), 0) % 2
    column_patch = lax.broadcasted_iota(jnp.int32, (TOKENS, TOKENS), 1) % 2
    softmax_heads(tq, tk, chance_t, jnp.where(row_patch == column_patch, 0.0, -1e30))
    loads[3].wait()
    loads[4].wait()
    at_grad[...] = dot_nt(cot[...], weights[3]).astype(BF16)
    vt_grad[...] = attend_values_back(chance_t, at_grad).astype(BF16)
    out_plane[0] = move_tokens(1, vt_grad[...])
    grad_plane = start_plane(1, out_plane.at[0], in_plane.at[0])

    for number in (5, 6, 7, 8, 9, 10):
        loads[number].wait()
    sq[...] = sq_turned[...].T
    sk[...] = sk_turned[...].T
    value_s[...] = dot_nt(block[...], weights[0]).astype(BF16)
    softmax_heads(sq, sk, chance_s, None)
    attended_s[...] = attend(chance_s, value_s).astype(BF16)
    mixed[...] = (block[...].astype(F32) + dot(attended_s[...], weights[1])).astype(BF16)
    out_plane[1] = move_tokens(5, dot_nt(mixed[...], weights[2]).astype(BF16))
    value_plane = start_plane(2, out_plane.at[1], in_plane.at[1])

    arrive(grad_plane)
    out_z[0] = move_tokens(4, in_plane[0])
    grad_z = start_z(1, out_z.at[0], in_z.at[0])
    for number in (11, 12, 13, 14):
        loads[number].wait()
    feature_copies, column_copies = {}, {}
    feature_copies[0] = start_features(0, block)
    column_copies[1] = start_columns(1, attended_s[...])
    arrive(cot_z)
    out_plane_wide[...] = move_tokens(1, in_z_wide[...])
    cot_plane = start_plane(0, out_plane_wide, in_plane_wide)
    arrive(value_plane)
    out_z[1] = move_tokens(4, in_plane[1])
    value_z = start_z(2, out_z.at[1], in_z.at[1])
    feature_copies[2] = start_features(2, mixed)
    feature_copies[3] = start_features(3, cot)

    arrive(cot_plane)
    cot_frame[...] = move_tokens(2, in_plane_wide[...])
    arrive(grad_z)
    vt_grad_frame[...] = move_tokens(3, in_z[0])
    column_copies[2] = start_columns(2, vt_grad_frame[...])
    mixed_grad[...] = (cot_frame[...].astype(F32) + dot(vt_grad_frame[...], weights[2])).astype(BF16)
    feature_copies[1] = start_features(1, mixed_grad)
    as_grad[...] = dot_nt(mixed_grad[...], weights[1]).astype(BF16)
    vs_grad[...] = attend_values_back(chance_s, as_grad).astype(BF16)
    column_copies[0] = start_columns(0, vs_grad[...])

    arrive([feature_copies[1], feature_copies[2], column_copies[1], column_copies[2]])
    first_x = first_ring(0)
    arrive(value_z)
    value_t[...] = in_z[1]
    attended_t[...] = attend(chance_t, value_t).astype(BF16)
    column_copies[3] = start_columns(3, attended_t[...])
    arrive([feature_copies[0], feature_copies[3], column_copies[0], column_copies[3]])
    first_y = first_ring(1)
    first_relay(0, first_x)
    query_part, key_part = attend_scores_back(chance_s, sq, sk, value_s, as_grad)
    sq_grad[...] = query_part.astype(BF16).T
    sk_grad[...] = key_part.astype(BF16).T
    first_relay(1, first_y)
    input_grad[...] = (mixed_grad[...].astype(F32) + dot(vs_grad[...], weights[0])).astype(BF16)
    query_part, key_part = attend_scores_back(chance_t, tq, tk, value_t, at_grad)
    rows_one[...] = query_part
    rows_two[...] = key_part
    split_pairs(rows_one, tq_grad)
    split_pairs(rows_two, tk_grad)

    first_end(0, first_x)
    second_y = second_ring(0)
    first_end(1, first_y)
    second_x = second_ring(1)
    last = last_line([second_end(0, second_y), second_end(1, second_x)])
    finish(last)
    for copy in sent:
        copy.wait_send()


def hand_over(*refs):
    for at in range(6):
        refs[6 + at][...] = refs[at][...]


def body(
    block_input, spatial_queries, spatial_keys, cotangent, temporal_queries, temporal_keys, weights
):
    grad_scale = float(4 * 64 * 128) ** (-0.5)
    tables = make_tables()
    arrays = [
        block_input.reshape(TOKENS, WIDTH),
        spatial_queries.reshape(TOKENS, INNER).T,
        spatial_keys.reshape(TOKENS, INNER).T,
        cotangent.reshape(FRAMES, 2, WIDTH),
        temporal_queries.reshape(FRAMES, 2, INNER),
        temporal_keys.reshape(FRAMES, 2, INNER),
        weights.transpose(0, 2, 1),
    ] + tables
    wide, narrow = (TOKENS, WIDTH), (TOKENS, INNER)
    chances = pltpu.VMEM((HEADS, TOKENS, TOKENS), F32)
    dma = pltpu.SemaphoreType.DMA
    scratch = [pltpu.VMEM(array.shape, BF16) for array in arrays]
    scratch += [pltpu.VMEM(narrow, BF16)] * 2 + [pltpu.VMEM(wide, BF16)] + [pltpu.VMEM(narrow, BF16)] * 2
    scratch += [pltpu.VMEM(wide, F32)] + [pltpu.VMEM(narrow, F32)] * 2
    scratch += [chances, chances] + [pltpu.VMEM(narrow, BF16)] * 8
    scratch += [pltpu.VMEM(wide, BF16)] * 3 + [pltpu.VMEM(narrow, BF16)]
    scratch += [pltpu.VMEM(wide, BF16)] * 3 + [pltpu.VMEM((2,) + narrow, BF16)] * 4
    scratch += [
        pltpu.VMEM((4, WIDTH, 2 * TOKENS), BF16),
        pltpu.VMEM((4, 2, 2 * TOKENS, LANES), BF16),
        pltpu.VMEM((4, 2, TOKENS, LANES), BF16),
        pltpu.VMEM((2, 4, PIECE, 128), BF16),
        pltpu.VMEM((2, 6, PIECE - CUT, 128), BF16),
        pltpu.VMEM((PIECE, 128), F32),
        pltpu.VMEM((2, 4, BLOCK_ROWS, 128), BF16),
        pltpu.VMEM((2, 3, BLOCK_ROWS, 128), BF16),
        pltpu.VMEM((8, SHARE_ROWS, 128), BF16),
        pltpu.VMEM((7, SHARE_ROWS, 128), BF16),
        pltpu.VMEM((SHARE_ROWS, 128), F32),
    ]
    scratch += [dma((15,))] + [dma((3, 7))] * 4 + [dma((4,))] * 4 + [dma((2, 6))] * 2 + [dma((2, 3))] * 2 + [dma((7,))] * 2
    results = [
        jax.ShapeDtypeStruct(wide, BF16),
        jax.ShapeDtypeStruct((INNER, TOKENS), BF16),
        jax.ShapeDtypeStruct((INNER, TOKENS), BF16),
        jax.ShapeDtypeStruct((FRAMES, 2, INNER), BF16),
        jax.ShapeDtypeStruct((FRAMES, 2, INNER), BF16),
        jax.ShapeDtypeStruct((18, 4, 144), F32),
    ]
    made = pl.pallas_call(
        functools.partial(kernel, grad_scale),
        out_shape=results,
        in_specs=[pl.BlockSpec(memory_space=pl.ANY)] * len(arrays),
        out_specs=[pl.BlockSpec(memory_space=pltpu.VMEM)] * 6,
        scratch_shapes=scratch,
        compiler_params=pltpu.CompilerParams(
            collective_id=0, has_side_effects=True, vmem_limit_bytes=56 * 2**20
        ),
        name="block_backward",
    )(*arrays)
    input_grad, sq_grad, sk_grad, tq_grad, tk_grad, weight_grads = pl.pallas_call(
        hand_over,
        out_shape=results,
        in_specs=[pl.BlockSpec(memory_space=pltpu.VMEM)] * 6,
        out_specs=[pl.BlockSpec(memory_space=pltpu.VMEM)] * 6,
        compiler_params=pltpu.CompilerParams(vmem_limit_bytes=60 * 2**20),
        name="hand_over",
    )(*made)
    return (
        input_grad.reshape(block_input.shape),
        sq_grad.T.reshape(spatial_queries.shape),
        sk_grad.T.reshape(spatial_keys.shape),
        tq_grad.reshape(temporal_queries.shape),
        tk_grad.reshape(temporal_keys.shape),
        weight_grads.transpose(1, 0, 2),
    )


def solution(mesh):
    placed = (
        P("dp", "seq", None, None),
        P("dp", "seq", None, None),
        P("dp", "seq", None, None),
        P("dp", None, "seq", None),
        P("dp", None, "seq", None),
        P("dp", None, "seq", None),
        P(),
    )
    return jax.shard_map(
        body,
        mesh=mesh,
        in_specs=placed,
        out_specs=(
            P("dp", "seq", None, None),
            P("dp", "seq", None, None),
            P("dp", "seq", None, None),
            P("dp", None, "seq", None),
            P("dp", None, "seq", None),
            P(None, "seq", "dp"),
        ),
        check_vma=False,
    )
```

```python
import functools

import jax
import jax.numpy as jnp
import numpy as np
from jax import lax
from jax.experimental import pallas as pl
from jax.experimental.pallas import tpu as pltpu
from jax.sharding import PartitionSpec as P

HEADS = 8
HEAD_DIM = 72
WIDTH = 1152
INNER = 576
TOKENS = 128
FRAMES = 64
SCORE_SCALE = HEAD_DIM ** (-0.5)
ROW_BLOCK = 144
LANES = 256
PIECE = 4 * ROW_BLOCK + 80
CUT = 336
BLOCK_ROWS = 2 * ROW_BLOCK + 48
SHARE_ROWS = 96
PAIRS = ((1, 3), (2, 0))
F32 = jnp.float32
BF16 = jnp.bfloat16
MESH = pl.DeviceIdType.MESH


def one_hot(source, size):
    table = np.zeros((len(source), size), np.float32)
    for row, at in enumerate(source):
        if at >= 0:
            table[row, at] = 1.0
    return table


def make_tables():
    def natural(y_lo, z, x, p):
        return 2 * (y_lo * 32 + z * 4 + x) + p

    to_z = [natural(y, z, x, p) for z in range(8) for y in range(2) for x in range(4) for p in range(2)]
    to_plane = [z * 16 + q * 2 + p for q in range(8) for z in range(8) for p in range(2)]
    to_natural = [
        (y * 4 + x) * 16 + z * 2 + p for y in range(2) for z in range(8) for x in range(4) for p in range(2)
    ]
    forth = [one_hot(order, TOKENS) for order in (to_z, to_plane, to_natural)]
    token_moves = np.stack(forth + [table.T for table in forth])
    feature_moves = np.stack(
        [
            one_hot(
                [y * 64 + z * 72 + x * 18 + r for x in range(4) for z in range(8) for r in range(18)], 640
            )
            for y in range(2)
        ]
    )
    picks = np.zeros((2, 2, INNER, LANES), np.float32)
    for core in range(2):
        for y_hi in range(2):
            for column in range(144):
                picks[core, y_hi, (2 * y_hi + core) * 144 + column, column] = 1.0
    share_moves = one_hot(
        [
            part * 144 + z * 18 + r if part < 4 else -1
            for z in range(8)
            for part, r in [divmod(row, 18) for row in range(80)]
        ],
        4 * ROW_BLOCK,
    )
    rest_moves = []
    for group in range(4):
        source = []
        for z in range(8):
            for row in range(16):
                at = z * 18 + 9 * (group % 2) + row
                place, turn = at // 16, (group - at // 16) % 4
                source.append(turn * 48 + place // 4 * 16 + at % 16 if row < 9 else -1)
        rest_moves.append(one_hot(source, 192))
    tables = (token_moves, feature_moves, picks, share_moves, np.stack(rest_moves))
    return [jnp.asarray(table, BF16) for table in tables]


def line_order(frame):
    y_lo, z, x = frame // 32, frame // 4 % 8, frame % 4
    start = 2 * (z * 8 + y_lo * 4 + x)
    return slice(start, start + 2)


def dot(left, right):
    return jnp.dot(left, right, preferred_element_type=F32)


def dot_nt(left, right):
    return lax.dot_general(left, right, (((1,), (1,)), ((), ())), preferred_element_type=F32)


def dot_tn(left, right):
    return lax.dot_general(left, right, (((0,), (0,)), ((), ())), preferred_element_type=F32)


def head_window(head):
    start = head * HEAD_DIM // 128 * 128
    stop = min(-(-(head * HEAD_DIM + HEAD_DIM) // 128) * 128, INNER)
    return start, stop


def head_mask(head):
    start, stop = head_window(head)
    lane = lax.broadcasted_iota(jnp.int32, (TOKENS, stop - start), 1) + start
    return (lane >= head * HEAD_DIM) & (lane < (head + 1) * HEAD_DIM)


def window(ref, head):
    start, stop = head_window(head)
    return ref[:, start:stop]


def masked_window(ref, head):
    return jnp.where(head_mask(head), window(ref, head).astype(F32), 0.0).astype(BF16)


def join_heads(parts):
    tiles = [None] * 5
    for head, part in enumerate(parts):
        start, stop = head_window(head)
        part = jnp.where(head_mask(head), part, 0.0)
        for at in range(start, stop, 128):
            piece = part[:, at - start : min(at - start + 128, stop - start)]
            tiles[at // 128] = piece if tiles[at // 128] is None else tiles[at // 128] + piece
    return jnp.concatenate(tiles, axis=1)


def softmax_heads(queries, key_rows, chance_ref, bias):
    for head in range(HEADS):
        scores = dot_nt(masked_window(queries, head), window(key_rows, head)) * SCORE_SCALE
        if bias is not None:
            scores = scores + bias
        powers = jnp.exp(scores - jnp.max(scores, axis=1, keepdims=True))
        chance_ref[head] = powers / jnp.sum(powers, axis=1, keepdims=True)


def attend(chance_ref, values):
    return join_heads([dot(chance_ref[h].astype(BF16), window(values, h)) for h in range(HEADS)])


def attend_values_back(chance_ref, out_grad):
    return join_heads([dot_tn(chance_ref[h].astype(BF16), window(out_grad, h)) for h in range(HEADS)])


def attend_scores_back(chance_ref, queries, key_rows, values, out_grad):
    query_parts, key_parts = [], []
    for head in range(HEADS):
        chance = chance_ref[head]
        chance_grad = dot_nt(masked_window(out_grad, head), window(values, head))
        centre = jnp.sum(chance * chance_grad, axis=1, keepdims=True)
        score_grad = (chance * (chance_grad - centre)).astype(BF16)
        query_parts.append(dot(score_grad, window(key_rows, head)))
        key_parts.append(dot_tn(score_grad, window(queries, head)))
    return join_heads(query_parts) * SCORE_SCALE, join_heads(key_parts) * SCORE_SCALE


def kernel(
    grad_scale,
    block_hbm, sq_hbm, sk_hbm, cot_hbm, tq_hbm, tk_hbm, weights_hbm,
    token_moves_hbm, feature_moves_hbm, picks_hbm, share_moves_hbm, rest_moves_hbm,
    input_grad, sq_grad, sk_grad, tq_grad, tk_grad, weight_grads,
    block, sq_turned, sk_turned, cot_pairs, tq_pairs, tk_pairs, weights, token_moves, feature_moves, picks, share_moves, rest_moves,
    sq, sk, cot, tq, tk, rows_wide, rows_one, rows_two,
    chance_s, chance_t, value_s, value_t, attended_s, attended_t, at_grad, as_grad, vt_grad, vs_grad,
    mixed, mixed_grad, cot_frame, vt_grad_frame,
    in_z_wide, out_plane_wide, in_plane_wide, out_plane, in_plane, out_z, in_z,
    factors, picked, picked_out, sums, arrived, total_one, sums_two, arrived_two, shares, shares_in, total_share,
    load_sem, z_send, z_recv, plane_send, plane_recv, factor_send, factor_recv, picked_send, picked_recv,
    ring_send, ring_recv, ring_two_send, ring_two_recv, share_send, share_recv,
):
    dp, seq = lax.axis_index("dp"), lax.axis_index("seq")
    y_hi, core = dp // 2, dp % 2
    y_lo, z, x = seq // 32, (seq // 4) % 8, seq % 4
    y = y_hi * 2 + y_lo
    q = y_lo * 4 + x

    def device(y_hi_at=y_hi, core_at=core, y_lo_at=y_lo, z_at=z, x_at=x):
        return (y_hi_at * 2 + core_at, y_lo_at * 32 + z_at * 4 + x_at)

    def along_z(step):
        return device(z_at=(z + step) % 8)

    def in_the_plane(step):
        to = (q + step) % 8
        return device(y_lo_at=to // 4, x_at=to % 4)

    def along_x(step):
        return device(x_at=(x + step) % 4)

    def along_y(step):
        to = (y + step) % 4
        return device(y_hi_at=to // 2, y_lo_at=to % 2)

    sibling = device(core_at=1 - core)

    loads = []
    for number, (source, target) in enumerate(
        [
            (cot_hbm, cot_pairs), (tq_hbm, tq_pairs), (tk_hbm, tk_pairs), (weights_hbm.at[3], weights.at[3]),
            (token_moves_hbm, token_moves), (block_hbm, block), (weights_hbm.at[0], weights.at[0]),
            (sq_hbm, sq_turned), (sk_hbm, sk_turned), (weights_hbm.at[1], weights.at[1]), (weights_hbm.at[2], weights.at[2]),
            (feature_moves_hbm, feature_moves), (picks_hbm, picks), (share_moves_hbm, share_moves),
            (rest_moves_hbm, rest_moves),
        ]
    ):
        copy = pltpu.make_async_copy(source, target, load_sem.at[number])
        if number < 3:
            copy.start()
        loads.append(copy)

    barrier = pltpu.get_barrier_semaphore()
    greeted = [along_z(step) for step in range(1, 8)] + [in_the_plane(step) for step in range(1, 8)]
    greeted += [device(y_hi_at=1 - y_hi, y_lo_at=1 - y_lo), sibling]
    for peer in greeted:
        pl.semaphore_signal(barrier, inc=1, device_id=peer, device_id_type=MESH)

    sent = []

    def send(source, target, send_sem, recv_sem, peer):
        copy = pltpu.make_async_remote_copy(
            src_ref=source, dst_ref=target, send_sem=send_sem, recv_sem=recv_sem,
            device_id=peer, device_id_type=MESH,
        )
        copy.start()
        sent.append(copy)
        return copy

    def move_tokens(number, rows):
        return dot(token_moves[number], rows).astype(BF16)

    def start_z(item, source, target):
        copies = []
        for step in range(1, 8):
            to = (z + step) % 8
            copies.append(
                send(
                    source.at[pl.ds(to * 16, 16)], target.at[pl.ds(z * 16, 16)],
                    z_send.at[item, step - 1], z_recv.at[item, step - 1], along_z(step),
                )
            )
        own = pl.ds(pl.multiple_of(z * 16, 16), 16)
        target[own, :] = source[own, :]
        return copies

    def start_plane(item, source, target):
        copies = []
        for step in range(1, 8):
            to = (q + step) % 8
            copies.append(
                send(
                    source.at[pl.ds(to * 16, 16)], target.at[pl.ds(q * 16, 16)],
                    plane_send.at[item, step - 1], plane_recv.at[item, step - 1], in_the_plane(step),
                )
            )
        own = pl.ds(pl.multiple_of(q * 16, 16), 16)
        target[own, :] = source[own, :]
        return copies

    def arrive(copies):
        for copy in copies:
            copy.wait_recv()

    def start_features(number, rows_ref):
        for half in range(2):
            factors[number, half * INNER : (half + 1) * INNER, 0:TOKENS] = dot_nt(
                feature_moves[half], rows_ref[:, half * 512 : half * 512 + 640]
            ).astype(BF16)
        return send(
            factors.at[number, :, 0:TOKENS], factors.at[number, :, TOKENS : 2 * TOKENS],
            factor_send.at[number], factor_recv.at[number], sibling,
        )

    def start_columns(number, rows):
        for side in range(2):
            picked[number, side, 0:TOKENS, :] = dot(rows, picks[core, side]).astype(BF16)
            picked_out[number, side] = dot(rows, picks[1 - core, side]).astype(BF16)
        return send(
            picked_out.at[number], picked.at[number, :, TOKENS : 2 * TOKENS],
            picked_send.at[number], picked_recv.at[number], sibling,
        )

    places = (x, y)
    rings = (along_x, along_y)
    ring_of = {number: ring for ring, numbers in enumerate(PAIRS) for number in numbers}
    slot_half = (0, 1, 1, 0, 0, 1)

    def make_pieces(number, to):
        rests = None
        for sub in range(4):
            side, y_lo_at, x_at = (sub // 2, sub % 2, to) if ring_of[number] == 0 else (to // 2, to % 2, sub)
            rows = pl.ds(pl.multiple_of((y_lo_at * 4 + x_at) * ROW_BLOCK, 16), ROW_BLOCK)
            total = dot(factors[number, rows, :], picked[number, side])
            sums[number, to, sub * ROW_BLOCK : (sub + 1) * ROW_BLOCK, :] = total[:, 0:128].astype(BF16)
            rest = total[:, 128:256]
            rests = rest if sub == 0 else rests + pltpu.roll(rest, 16 * sub, 1)
        beside = jnp.concatenate([pltpu.roll(rests[80:ROW_BLOCK], 64, 1), jnp.zeros((16, 128), F32)], axis=0)
        sums[number, to, 4 * ROW_BLOCK : PIECE, :] = (rests[0:80] + beside).astype(BF16)

    def piece(number, to, half):
        return sums.at[number, to, 0:CUT] if half == 0 else sums.at[number, to, CUT:PIECE]

    def slot_ref(number, slot):
        return arrived.at[number, slot, 0 : (CUT if slot_half[slot] == 0 else PIECE - CUT)]

    def ring_copy(number, slot, source):
        peer = rings[ring_of[number]](1 if slot % 2 == 0 else 3)
        return send(source, slot_ref(number, slot), ring_send.at[number, slot], ring_recv.at[number, slot], peer)

    def first_ring(number):
        place = places[ring_of[number]]
        after, across, before = (place + 1) % 4, (place + 2) % 4, (place + 3) % 4
        copies = {}
        make_pieces(number, across)
        copies[0] = ring_copy(number, 0, piece(number, across, 0))
        copies[1] = ring_copy(number, 1, piece(number, across, 1))
        make_pieces(number, after)
        copies[2] = ring_copy(number, 2, piece(number, after, 1))
        make_pieces(number, before)
        copies[3] = ring_copy(number, 3, piece(number, before, 0))
        make_pieces(number, place)
        return copies

    def first_relay(number, copies):
        place = places[ring_of[number]]
        after, before = (place + 1) % 4, (place + 3) % 4
        for slot, to, half in ((0, after, 0), (1, before, 1)):
            copies[slot].wait_recv()
            ref = piece(number, to, half)
            ref[...] = (ref[...].astype(F32) + slot_ref(number, slot)[...].astype(F32)).astype(BF16)
            copies[slot + 4] = ring_copy(number, slot + 4, ref)

    lane_group = lax.broadcasted_iota(jnp.int32, (16, 128), 1) // 16

    def first_end(pair, copies):
        for place, number in enumerate(PAIRS[pair]):
            for half, slots in ((0, (3, 4)), (1, (2, 5))):
                total = piece(number, places[pair], half)[...].astype(F32)
                for slot in slots:
                    copies[number][slot].wait_recv()
                    total += slot_ref(number, slot)[...].astype(F32)
                total_one[place, (0 if half == 0 else CUT) : (CUT if half == 0 else PIECE), :] = total
            for sub in range(4):
                sums_two[pair, sub, place * ROW_BLOCK : (place + 1) * ROW_BLOCK, :] = total_one[
                    place, sub * ROW_BLOCK : (sub + 1) * ROW_BLOCK, :
                ].astype(BF16)
        for sub in range(4):
            for tile in range(3):
                packed = jnp.zeros((16, 128), F32)
                for group in range(4 * tile, min(4 * tile + 4, 9)):
                    for place in range(2):
                        start = 4 * ROW_BLOCK + 16 * (group % 5)
                        turn = (32 * (group % 4) + 16 * place - 16 * sub - (64 if group >= 5 else 0)) % 128
                        rest = pltpu.roll(total_one[place, start : start + 16, :], turn, 1)
                        packed = jnp.where(lane_group == 2 * (group % 4) + place, rest, packed)
                start = 2 * ROW_BLOCK + 16 * tile
                sums_two[pair, sub, start : start + 16, :] = packed.astype(BF16)

    def second_ring(pair):
        place = places[1 - pair]
        copies = []
        for step in range(1, 4):
            copies.append(
                send(
                    sums_two.at[pair, (place + step) % 4], arrived_two.at[pair, step - 1],
                    ring_two_send.at[pair, step - 1], ring_two_recv.at[pair, step - 1], rings[1 - pair](step),
                )
            )
        return copies

    def second_end(pair, copies):
        total = sums_two[pair, places[1 - pair]].astype(F32)
        for step in range(1, 4):
            copies[step - 1].wait_recv()
            total += arrived_two[pair, step - 1].astype(F32)
        return total

    def last_line(totals):
        whole = jnp.concatenate([total[0 : 2 * ROW_BLOCK] for total in totals], axis=0).astype(BF16)
        moved = dot(share_moves[...], whole).astype(BF16)
        rest = jnp.zeros((TOKENS, 128), F32)
        lanes = lax.broadcasted_iota(jnp.int32, (TOKENS, 128), 1) // 32
        for pair, total in enumerate(totals):
            ends = total[2 * ROW_BLOCK : BLOCK_ROWS]
            turned = [ends] + [pltpu.roll(ends, 32 * turn, 1) for turn in range(1, 4)]
            turned = jnp.concatenate(turned, axis=0).astype(BF16)
            for group in (2 * pair, 2 * pair + 1):
                rest = jnp.where(lanes == group, dot(rest_moves[group], turned), rest)
        rest = rest.astype(BF16)
        for z_at in range(8):
            shares[z_at, 0:80, :] = moved[80 * z_at : 80 * z_at + 80]
            shares[z_at, 80:96, :] = rest[16 * z_at : 16 * z_at + 16]
        copies = []
        for step in range(1, 8):
            copies.append(
                send(
                    shares.at[(z + step) % 8], shares_in.at[step - 1],
                    share_send.at[step - 1], share_recv.at[step - 1], along_z(step),
                )
            )
        return copies

    def finish(copies):
        total = shares[z].astype(F32)
        for step in range(1, 8):
            copies[step - 1].wait_recv()
            total += shares_in[step - 1].astype(F32)
        total_share[...] = total * grad_scale
        for pair, numbers in enumerate(PAIRS):
            for place, number in enumerate(numbers):
                start = 36 * pair + 18 * place
                weight_grads[:, number, 0:128] = total_share[start : start + 18, :]
                for half in range(2):
                    lane = 64 * pair + 32 * half + 16 * place
                    weight_grads[9 * half : 9 * half + 9, number, 128:144] = total_share[80:89, lane : lane + 16]

    def join_pairs(pairs, rows):
        for frame in range(FRAMES):
            rows[line_order(frame), :] = pairs[frame].astype(F32)
        return rows[...].astype(BF16)

    def split_pairs(rows, pairs):
        for frame in range(FRAMES):
            pairs[frame] = rows[line_order(frame), :].astype(BF16)

    loads[0].wait()
    for copy in loads[3:11]:
        copy.start()
    cot[...] = join_pairs(cot_pairs, rows_wide)
    pl.semaphore_wait(barrier, len(greeted))
    cot_z = start_z(0, cot, in_z_wide)
    for copy in loads[11:]:
        copy.start()
    loads[1].wait()
    loads[2].wait()
    tq[...] = join_pairs(tq_pairs, rows_one)
    tk[...] = join_pairs(tk_pairs, rows_two)
    row_patch = lax.broadcasted_iota(jnp.int32, (TOKENS, TOKENS), 0) % 2
    column_patch = lax.broadcasted_iota(jnp.int32, (TOKENS, TOKENS), 1) % 2
    softmax_heads(tq, tk, chance_t, jnp.where(row_patch == column_patch, 0.0, -1e30))
    loads[3].wait()
    loads[4].wait()
    at_grad[...] = dot_nt(cot[...], weights[3]).astype(BF16)
    vt_grad[...] = attend_values_back(chance_t, at_grad).astype(BF16)
    out_plane[0] = move_tokens(1, vt_grad[...])
    grad_plane = start_plane(1, out_plane.at[0], in_plane.at[0])

    for number in (5, 6, 7, 8, 9, 10):
        loads[number].wait()
    sq[...] = sq_turned[...].T
    sk[...] = sk_turned[...].T
    value_s[...] = dot_nt(block[...], weights[0]).astype(BF16)
    softmax_heads(sq, sk, chance_s, None)
    attended_s[...] = attend(chance_s, value_s).astype(BF16)
    mixed[...] = (block[...].astype(F32) + dot(attended_s[...], weights[1])).astype(BF16)
    out_plane[1] = move_tokens(5, dot_nt(mixed[...], weights[2]).astype(BF16))
    value_plane = start_plane(2, out_plane.at[1], in_plane.at[1])

    arrive(grad_plane)
    out_z[0] = move_tokens(4, in_plane[0])
    grad_z = start_z(1, out_z.at[0], in_z.at[0])
    for number in (11, 12, 13, 14):
        loads[number].wait()
    feature_copies, column_copies = {}, {}
    feature_copies[0] = start_features(0, block)
    column_copies[1] = start_columns(1, attended_s[...])
    arrive(cot_z)
    out_plane_wide[...] = move_tokens(1, in_z_wide[...])
    cot_plane = start_plane(0, out_plane_wide, in_plane_wide)
    arrive(value_plane)
    out_z[1] = move_tokens(4, in_plane[1])
    value_z = start_z(2, out_z.at[1], in_z.at[1])
    feature_copies[2] = start_features(2, mixed)

    rings_at = {}

    def ready(number):
        arrive([feature_copies[number], column_copies[number]])
        rings_at[number] = first_ring(number)

    arrive(grad_z)
    vt_grad_frame[...] = move_tokens(3, in_z[0])
    column_copies[2] = start_columns(2, vt_grad_frame[...])
    feature_copies[3] = start_features(3, cot)
    ready(2)
    arrive(cot_plane)
    cot_frame[...] = move_tokens(2, in_plane_wide[...])
    mixed_grad[...] = (cot_frame[...].astype(F32) + dot(vt_grad_frame[...], weights[2])).astype(BF16)
    feature_copies[1] = start_features(1, mixed_grad)
    as_grad[...] = dot_nt(mixed_grad[...], weights[1]).astype(BF16)
    vs_grad[...] = attend_values_back(chance_s, as_grad).astype(BF16)
    column_copies[0] = start_columns(0, vs_grad[...])
    ready(1)
    first_relay(2, rings_at[2])
    ready(0)
    arrive(value_z)
    value_t[...] = in_z[1]
    attended_t[...] = attend(chance_t, value_t).astype(BF16)
    column_copies[3] = start_columns(3, attended_t[...])
    first_relay(1, rings_at[1])
    ready(3)
    first_relay(0, rings_at[0])
    query_part, key_part = attend_scores_back(chance_s, sq, sk, value_s, as_grad)
    sq_grad[...] = query_part.astype(BF16).T
    sk_grad[...] = key_part.astype(BF16).T
    first_relay(3, rings_at[3])
    input_grad[...] = (mixed_grad[...].astype(F32) + dot(vs_grad[...], weights[0])).astype(BF16)
    query_part, key_part = attend_scores_back(chance_t, tq, tk, value_t, at_grad)
    rows_one[...] = query_part
    rows_two[...] = key_part
    split_pairs(rows_one, tq_grad)
    split_pairs(rows_two, tk_grad)

    first_end(1, rings_at)
    second_x = second_ring(1)
    first_end(0, rings_at)
    second_y = second_ring(0)
    last = last_line([second_end(0, second_y), second_end(1, second_x)])
    finish(last)
    for copy in sent:
        copy.wait_send()


def hand_over(*refs):
    for at in range(6):
        refs[6 + at][...] = refs[at][...]


def body(
    block_input, spatial_queries, spatial_keys, cotangent, temporal_queries, temporal_keys, weights
):
    grad_scale = float(4 * 64 * 128) ** (-0.5)
    tables = make_tables()
    arrays = [
        block_input.reshape(TOKENS, WIDTH),
        spatial_queries.reshape(TOKENS, INNER).T,
        spatial_keys.reshape(TOKENS, INNER).T,
        cotangent.reshape(FRAMES, 2, WIDTH),
        temporal_queries.reshape(FRAMES, 2, INNER),
        temporal_keys.reshape(FRAMES, 2, INNER),
        weights.transpose(0, 2, 1),
    ] + tables
    wide, narrow = (TOKENS, WIDTH), (TOKENS, INNER)
    chances = pltpu.VMEM((HEADS, TOKENS, TOKENS), F32)
    dma = pltpu.SemaphoreType.DMA
    scratch = [pltpu.VMEM(array.shape, BF16) for array in arrays]
    scratch += [pltpu.VMEM(narrow, BF16)] * 2 + [pltpu.VMEM(wide, BF16)] + [pltpu.VMEM(narrow, BF16)] * 2
    scratch += [pltpu.VMEM(wide, F32)] + [pltpu.VMEM(narrow, F32)] * 2
    scratch += [chances, chances] + [pltpu.VMEM(narrow, BF16)] * 8
    scratch += [pltpu.VMEM(wide, BF16)] * 3 + [pltpu.VMEM(narrow, BF16)]
    scratch += [pltpu.VMEM(wide, BF16)] * 3 + [pltpu.VMEM((2,) + narrow, BF16)] * 4
    scratch += [
        pltpu.VMEM((4, WIDTH, 2 * TOKENS), BF16),
        pltpu.VMEM((4, 2, 2 * TOKENS, LANES), BF16),
        pltpu.VMEM((4, 2, TOKENS, LANES), BF16),
        pltpu.VMEM((4, 4, PIECE, 128), BF16),
        pltpu.VMEM((4, 6, CUT, 128), BF16),
        pltpu.VMEM((2, PIECE, 128), F32),
        pltpu.VMEM((2, 4, BLOCK_ROWS, 128), BF16),
        pltpu.VMEM((2, 3, BLOCK_ROWS, 128), BF16),
        pltpu.VMEM((8, SHARE_ROWS, 128), BF16),
        pltpu.VMEM((7, SHARE_ROWS, 128), BF16),
        pltpu.VMEM((SHARE_ROWS, 128), F32),
    ]
    scratch += [dma((15,))] + [dma((3, 7))] * 4 + [dma((4,))] * 4 + [dma((4, 6))] * 2 + [dma((2, 3))] * 2 + [dma((7,))] * 2
    results = [
        jax.ShapeDtypeStruct(wide, BF16),
        jax.ShapeDtypeStruct((INNER, TOKENS), BF16),
        jax.ShapeDtypeStruct((INNER, TOKENS), BF16),
        jax.ShapeDtypeStruct((FRAMES, 2, INNER), BF16),
        jax.ShapeDtypeStruct((FRAMES, 2, INNER), BF16),
        jax.ShapeDtypeStruct((18, 4, 144), F32),
    ]
    made = pl.pallas_call(
        functools.partial(kernel, grad_scale),
        out_shape=results,
        in_specs=[pl.BlockSpec(memory_space=pl.ANY)] * len(arrays),
        out_specs=[pl.BlockSpec(memory_space=pltpu.VMEM)] * 6,
        scratch_shapes=scratch,
        compiler_params=pltpu.CompilerParams(
            collective_id=0, has_side_effects=True, vmem_limit_bytes=56 * 2**20
        ),
        name="block_backward",
    )(*arrays)
    input_grad, sq_grad, sk_grad, tq_grad, tk_grad, weight_grads = pl.pallas_call(
        hand_over,
        out_shape=results,
        in_specs=[pl.BlockSpec(memory_space=pltpu.VMEM)] * 6,
        out_specs=[pl.BlockSpec(memory_space=pltpu.VMEM)] * 6,
        compiler_params=pltpu.CompilerParams(vmem_limit_bytes=60 * 2**20),
        name="hand_over",
    )(*made)
    return (
        input_grad.reshape(block_input.shape),
        sq_grad.T.reshape(spatial_queries.shape),
        sk_grad.T.reshape(spatial_keys.shape),
        tq_grad.reshape(temporal_queries.shape),
        tk_grad.reshape(temporal_keys.shape),
        weight_grads.transpose(1, 0, 2),
    )


def solution(mesh):
    placed = (
        P("dp", "seq", None, None),
        P("dp", "seq", None, None),
        P("dp", "seq", None, None),
        P("dp", None, "seq", None),
        P("dp", None, "seq", None),
        P("dp", None, "seq", None),
        P(),
    )
    return jax.shard_map(
        body,
        mesh=mesh,
        in_specs=placed,
        out_specs=(
            P("dp", "seq", None, None),
            P("dp", "seq", None, None),
            P("dp", "seq", None, None),
            P("dp", None, "seq", None),
            P("dp", None, "seq", None),
            P(None, "seq", "dp"),
        ),
        check_vma=False,
    )
```

```python
import functools

import jax
import jax.numpy as jnp
import numpy as np
from jax import lax
from jax.experimental import pallas as pl
from jax.experimental.pallas import tpu as pltpu
from jax.sharding import PartitionSpec as P

HEADS = 8
HEAD_DIM = 72
WIDTH = 1152
INNER = 576
TOKENS = 128
FRAMES = 64
SCORE_SCALE = HEAD_DIM ** (-0.5)
ROW_BLOCK = 144
LANES = 256
PIECE = 4 * ROW_BLOCK + 80
CUT = 336
BLOCK_ROWS = ROW_BLOCK + 32
SHARE_ROWS = 32
PAIRS = ((1, 3), (2, 0))
F32 = jnp.float32
BF16 = jnp.bfloat16
MESH = pl.DeviceIdType.MESH


def one_hot(source, size):
    table = np.zeros((len(source), size), np.float32)
    for row, at in enumerate(source):
        if at >= 0:
            table[row, at] = 1.0
    return table


def make_tables():
    def natural(y_lo, z, x, p):
        return 2 * (y_lo * 32 + z * 4 + x) + p

    to_z = [natural(y, z, x, p) for z in range(8) for y in range(2) for x in range(4) for p in range(2)]
    to_plane = [z * 16 + q * 2 + p for q in range(8) for z in range(8) for p in range(2)]
    to_natural = [
        (y * 4 + x) * 16 + z * 2 + p for y in range(2) for z in range(8) for x in range(4) for p in range(2)
    ]
    forth = [one_hot(order, TOKENS) for order in (to_z, to_plane, to_natural)]
    token_moves = np.stack(forth + [table.T for table in forth])
    feature_moves = np.stack(
        [
            one_hot(
                [y * 64 + z * 72 + x * 18 + r for x in range(4) for z in range(8) for r in range(18)], 640
            )
            for y in range(2)
        ]
    )
    picks = np.zeros((2, 2, INNER, LANES), np.float32)
    for core in range(2):
        for y_hi in range(2):
            for column in range(144):
                picks[core, y_hi, (2 * y_hi + core) * 144 + column, column] = 1.0
    share_moves = one_hot(
        [z * 18 + row if row < 18 else -1 for z in range(8) for row in range(SHARE_ROWS)], ROW_BLOCK
    )
    rest_moves = []
    for group in range(2):
        source = []
        for z in range(8):
            for row in range(SHARE_ROWS):
                at = z * 18 + 9 * group + row - 18
                place, turn = at // 16, (group - at // 16) % 8
                source.append(turn * 32 + place // 8 * 16 + at % 16 if 18 <= row < 27 else -1)
        rest_moves.append(one_hot(source, 256))
    tables = (token_moves, feature_moves, picks, share_moves, np.stack(rest_moves))
    return [jnp.asarray(table, BF16) for table in tables]


def line_order(frame):
    y_lo, z, x = frame // 32, frame // 4 % 8, frame % 4
    start = 2 * (z * 8 + y_lo * 4 + x)
    return slice(start, start + 2)


def dot(left, right):
    return jnp.dot(left, right, preferred_element_type=F32)


def dot_nt(left, right):
    return lax.dot_general(left, right, (((1,), (1,)), ((), ())), preferred_element_type=F32)


def dot_tn(left, right):
    return lax.dot_general(left, right, (((0,), (0,)), ((), ())), preferred_element_type=F32)


def head_window(head):
    start = head * HEAD_DIM // 128 * 128
    stop = min(-(-(head * HEAD_DIM + HEAD_DIM) // 128) * 128, INNER)
    return start, stop


def head_mask(head):
    start, stop = head_window(head)
    lane = lax.broadcasted_iota(jnp.int32, (TOKENS, stop - start), 1) + start
    return (lane >= head * HEAD_DIM) & (lane < (head + 1) * HEAD_DIM)


def window(ref, head):
    start, stop = head_window(head)
    return ref[:, start:stop]


def masked_window(ref, head):
    return jnp.where(head_mask(head), window(ref, head).astype(F32), 0.0).astype(BF16)


def join_heads(parts):
    tiles = [None] * 5
    for head, part in enumerate(parts):
        start, stop = head_window(head)
        part = jnp.where(head_mask(head), part, 0.0)
        for at in range(start, stop, 128):
            piece = part[:, at - start : min(at - start + 128, stop - start)]
            tiles[at // 128] = piece if tiles[at // 128] is None else tiles[at // 128] + piece
    return jnp.concatenate(tiles, axis=1)


def softmax_heads(queries, key_rows, chance_ref, bias):
    for head in range(HEADS):
        scores = dot_nt(masked_window(queries, head), window(key_rows, head)) * SCORE_SCALE
        if bias is not None:
            scores = scores + bias
        powers = jnp.exp(scores - jnp.max(scores, axis=1, keepdims=True))
        chance_ref[head] = powers / jnp.sum(powers, axis=1, keepdims=True)


def attend(chance_ref, values):
    return join_heads([dot(chance_ref[h].astype(BF16), window(values, h)) for h in range(HEADS)])


def attend_values_back(chance_ref, out_grad):
    return join_heads([dot_tn(chance_ref[h].astype(BF16), window(out_grad, h)) for h in range(HEADS)])


def attend_scores_back(chance_ref, queries, key_rows, values, out_grad):
    query_parts, key_parts = [], []
    for head in range(HEADS):
        chance = chance_ref[head]
        chance_grad = dot_nt(masked_window(out_grad, head), window(values, head))
        centre = jnp.sum(chance * chance_grad, axis=1, keepdims=True)
        score_grad = (chance * (chance_grad - centre)).astype(BF16)
        query_parts.append(dot(score_grad, window(key_rows, head)))
        key_parts.append(dot_tn(score_grad, window(queries, head)))
    return join_heads(query_parts) * SCORE_SCALE, join_heads(key_parts) * SCORE_SCALE


def kernel(
    grad_scale,
    block_hbm, sq_hbm, sk_hbm, cot_hbm, tq_hbm, tk_hbm, weights_hbm,
    token_moves_hbm, feature_moves_hbm, picks_hbm, share_moves_hbm, rest_moves_hbm,
    input_grad, sq_grad, sk_grad, tq_grad, tk_grad, weight_grads,
    block, sq_turned, sk_turned, cot_pairs, tq_pairs, tk_pairs, weights, token_moves, feature_moves, picks, share_moves, rest_moves,
    sq, sk, cot, tq, tk, rows_wide, rows_one, rows_two,
    chance_s, chance_t, value_s, value_t, attended_s, attended_t, at_grad, as_grad, vt_grad, vs_grad,
    mixed, mixed_grad, cot_frame, vt_grad_frame,
    in_z_wide, out_plane_wide, in_plane_wide, out_plane, in_plane, out_z, in_z,
    factors, picked, picked_out, sums, arrived, total_one, sums_two, arrived_two, shares, shares_in, total_share,
    load_sem, z_send, z_recv, plane_send, plane_recv, factor_send, factor_recv, picked_send, picked_recv,
    ring_send, ring_recv, ring_two_send, ring_two_recv, share_send, share_recv,
):
    dp, seq = lax.axis_index("dp"), lax.axis_index("seq")
    y_hi, core = dp // 2, dp % 2
    y_lo, z, x = seq // 32, (seq // 4) % 8, seq % 4
    y = y_hi * 2 + y_lo
    q = y_lo * 4 + x

    def device(y_hi_at=y_hi, core_at=core, y_lo_at=y_lo, z_at=z, x_at=x):
        return (y_hi_at * 2 + core_at, y_lo_at * 32 + z_at * 4 + x_at)

    def along_z(step):
        return device(z_at=(z + step) % 8)

    def in_the_plane(step):
        to = (q + step) % 8
        return device(y_lo_at=to // 4, x_at=to % 4)

    def along_x(step):
        return device(x_at=(x + step) % 4)

    def along_y(step):
        to = (y + step) % 4
        return device(y_hi_at=to // 2, y_lo_at=to % 2)

    sibling = device(core_at=1 - core)

    loads = []
    for number, (source, target) in enumerate(
        [
            (cot_hbm, cot_pairs), (tq_hbm, tq_pairs), (tk_hbm, tk_pairs), (weights_hbm.at[3], weights.at[3]),
            (token_moves_hbm, token_moves), (block_hbm, block), (weights_hbm.at[0], weights.at[0]),
            (sq_hbm, sq_turned), (sk_hbm, sk_turned), (weights_hbm.at[1], weights.at[1]), (weights_hbm.at[2], weights.at[2]),
            (feature_moves_hbm, feature_moves), (picks_hbm, picks), (share_moves_hbm, share_moves),
            (rest_moves_hbm, rest_moves),
        ]
    ):
        copy = pltpu.make_async_copy(source, target, load_sem.at[number])
        if number < 3:
            copy.start()
        loads.append(copy)

    barrier = pltpu.get_barrier_semaphore()
    greeted = [along_z(step) for step in range(1, 8)] + [in_the_plane(step) for step in range(1, 8)]
    greeted += [device(y_hi_at=1 - y_hi, y_lo_at=1 - y_lo), sibling]
    for peer in greeted:
        pl.semaphore_signal(barrier, inc=1, device_id=peer, device_id_type=MESH)

    sent = []

    def send(source, target, send_sem, recv_sem, peer):
        copy = pltpu.make_async_remote_copy(
            src_ref=source, dst_ref=target, send_sem=send_sem, recv_sem=recv_sem,
            device_id=peer, device_id_type=MESH,
        )
        copy.start()
        sent.append(copy)
        return copy

    def move_tokens(number, rows):
        return dot(token_moves[number], rows).astype(BF16)

    def start_z(item, source, target):
        copies = []
        for step in range(1, 8):
            to = (z + step) % 8
            copies.append(
                send(
                    source.at[pl.ds(to * 16, 16)], target.at[pl.ds(z * 16, 16)],
                    z_send.at[item, step - 1], z_recv.at[item, step - 1], along_z(step),
                )
            )
        own = pl.ds(pl.multiple_of(z * 16, 16), 16)
        target[own, :] = source[own, :]
        return copies

    def start_plane(item, source, target):
        copies = []
        for step in range(1, 8):
            to = (q + step) % 8
            copies.append(
                send(
                    source.at[pl.ds(to * 16, 16)], target.at[pl.ds(q * 16, 16)],
                    plane_send.at[item, step - 1], plane_recv.at[item, step - 1], in_the_plane(step),
                )
            )
        own = pl.ds(pl.multiple_of(q * 16, 16), 16)
        target[own, :] = source[own, :]
        return copies

    def arrive(copies):
        for copy in copies:
            copy.wait_recv()

    def start_features(number, rows_ref):
        for half in range(2):
            factors[number, half * INNER : (half + 1) * INNER, 0:TOKENS] = dot_nt(
                feature_moves[half], rows_ref[:, half * 512 : half * 512 + 640]
            ).astype(BF16)
        return send(
            factors.at[number, :, 0:TOKENS], factors.at[number, :, TOKENS : 2 * TOKENS],
            factor_send.at[number], factor_recv.at[number], sibling,
        )

    def start_columns(number, rows):
        for side in range(2):
            picked[number, side, 0:TOKENS, :] = dot(rows, picks[core, side]).astype(BF16)
            picked_out[number, side] = dot(rows, picks[1 - core, side]).astype(BF16)
        return send(
            picked_out.at[number], picked.at[number, :, TOKENS : 2 * TOKENS],
            picked_send.at[number], picked_recv.at[number], sibling,
        )

    places = (x, y)
    rings = (along_x, along_y)
    ring_of = {number: ring for ring, numbers in enumerate(PAIRS) for number in numbers}
    slot_half = (0, 1, 1, 0, 0, 1)

    def make_pieces(number, to):
        rests = None
        for sub in range(4):
            side, y_lo_at, x_at = (sub // 2, sub % 2, to) if ring_of[number] == 0 else (to // 2, to % 2, sub)
            rows = pl.ds(pl.multiple_of((y_lo_at * 4 + x_at) * ROW_BLOCK, 16), ROW_BLOCK)
            total = dot(factors[number, rows, :], picked[number, side])
            sums[number, to, sub * ROW_BLOCK : (sub + 1) * ROW_BLOCK, :] = total[:, 0:128].astype(BF16)
            rest = total[:, 128:256]
            rests = rest if sub == 0 else rests + pltpu.roll(rest, 16 * sub, 1)
        beside = jnp.concatenate([pltpu.roll(rests[80:ROW_BLOCK], 64, 1), jnp.zeros((16, 128), F32)], axis=0)
        sums[number, to, 4 * ROW_BLOCK : PIECE, :] = (rests[0:80] + beside).astype(BF16)

    def piece(number, to, half):
        return sums.at[number, to, 0:CUT] if half == 0 else sums.at[number, to, CUT:PIECE]

    def slot_ref(number, slot):
        return arrived.at[number, slot, 0 : (CUT if slot_half[slot] == 0 else PIECE - CUT)]

    def ring_copy(number, slot, source):
        peer = rings[ring_of[number]](1 if slot % 2 == 0 else 3)
        return send(source, slot_ref(number, slot), ring_send.at[number, slot], ring_recv.at[number, slot], peer)

    def first_ring(number):
        place = places[ring_of[number]]
        after, across, before = (place + 1) % 4, (place + 2) % 4, (place + 3) % 4
        copies = {}
        make_pieces(number, across)
        copies[0] = ring_copy(number, 0, piece(number, across, 0))
        copies[1] = ring_copy(number, 1, piece(number, across, 1))
        make_pieces(number, after)
        copies[2] = ring_copy(number, 2, piece(number, after, 1))
        make_pieces(number, before)
        copies[3] = ring_copy(number, 3, piece(number, before, 0))
        make_pieces(number, place)
        return copies

    def first_relay(number, copies):
        place = places[ring_of[number]]
        after, before = (place + 1) % 4, (place + 3) % 4
        for slot, to, half in ((0, after, 0), (1, before, 1)):
            copies[slot].wait_recv()
            ref = piece(number, to, half)
            ref[...] = (ref[...].astype(F32) + slot_ref(number, slot)[...].astype(F32)).astype(BF16)
            copies[slot + 4] = ring_copy(number, slot + 4, ref)

    lane_group = lax.broadcasted_iota(jnp.int32, (16, 128), 1) // 16
    share_group = lax.broadcasted_iota(jnp.int32, (8 * SHARE_ROWS, 128), 1) // 16

    def second_place(number):
        return places[1 - ring_of[number]]

    def second_line(number):
        copies = rings_at[number]
        for half, slots in ((0, (3, 4)), (1, (2, 5))):
            total = piece(number, places[ring_of[number]], half)[...].astype(F32)
            for slot in slots:
                copies[slot].wait_recv()
                total += slot_ref(number, slot)[...].astype(F32)
            total_one[(0 if half == 0 else CUT) : (CUT if half == 0 else PIECE), :] = total
        for sub in range(4):
            sums_two[number, sub, 0:ROW_BLOCK, :] = total_one[sub * ROW_BLOCK : (sub + 1) * ROW_BLOCK, :].astype(BF16)
            for tile in range(2):
                packed = jnp.zeros((16, 128), F32)
                for group in range(8) if tile == 0 else (8,):
                    start = 4 * ROW_BLOCK + 16 * (group % 5)
                    turn = (16 * (group % 8) - 16 * sub - (64 if group >= 5 else 0)) % 128
                    rest = total_one[start : start + 16, :]
                    rest = pltpu.roll(rest, turn, 1) if turn else rest
                    packed = jnp.where(lane_group == group % 8, rest, packed)
                start = ROW_BLOCK + 16 * tile
                sums_two[number, sub, start : start + 16, :] = packed.astype(BF16)
        seconds[number] = [
            send(
                sums_two.at[number, (second_place(number) + step) % 4], arrived_two.at[number, step - 1],
                ring_two_send.at[number, step - 1], ring_two_recv.at[number, step - 1],
                rings[1 - ring_of[number]](step),
            )
            for step in range(1, 4)
        ]

    def third_line(number):
        total = sums_two[number, second_place(number)].astype(F32)
        for step in range(1, 4):
            seconds[number][step - 1].wait_recv()
            total += arrived_two[number, step - 1].astype(F32)
        moved = dot(share_moves[...], total[0:ROW_BLOCK].astype(BF16))
        ends = total[ROW_BLOCK:BLOCK_ROWS]
        turned = [ends] + [pltpu.roll(ends, 16 * turn, 1) for turn in range(1, 8)]
        turned = jnp.concatenate(turned, axis=0).astype(BF16)
        for group in range(2):
            moved += jnp.where(share_group == group, dot(rest_moves[group], turned), 0.0)
        moved = moved.astype(BF16)
        for z_at in range(8):
            shares[number, z_at] = moved[SHARE_ROWS * z_at : SHARE_ROWS * (z_at + 1)]
        thirds[number] = [
            send(
                shares.at[number, (z + step) % 8], shares_in.at[number, step - 1],
                share_send.at[number, step - 1], share_recv.at[number, step - 1], along_z(step),
            )
            for step in range(1, 8)
        ]

    def finish(number):
        total = shares[number, z].astype(F32)
        for step in range(1, 8):
            thirds[number][step - 1].wait_recv()
            total += shares_in[number, step - 1].astype(F32)
        total_share[...] = total * grad_scale
        weight_grads[:, number, 0:128] = total_share[0:18, :]
        for half in range(2):
            weight_grads[9 * half : 9 * half + 9, number, 128:144] = total_share[18:27, 16 * half : 16 * half + 16]

    rings_at, seconds, thirds = {}, {}, {}

    def ready(number):
        arrive([feature_copies[number], column_copies[number]])
        rings_at[number] = first_ring(number)

    def join_pairs(pairs, rows):
        for frame in range(FRAMES):
            rows[line_order(frame), :] = pairs[frame].astype(F32)
        return rows[...].astype(BF16)

    def split_pairs(rows, pairs):
        for frame in range(FRAMES):
            pairs[frame] = rows[line_order(frame), :].astype(BF16)

    loads[0].wait()
    for copy in loads[3:11]:
        copy.start()
    cot[...] = join_pairs(cot_pairs, rows_wide)
    pl.semaphore_wait(barrier, len(greeted))
    cot_z = start_z(0, cot, in_z_wide)
    for copy in loads[11:]:
        copy.start()
    loads[1].wait()
    loads[2].wait()
    tq[...] = join_pairs(tq_pairs, rows_one)
    tk[...] = join_pairs(tk_pairs, rows_two)
    row_patch = lax.broadcasted_iota(jnp.int32, (TOKENS, TOKENS), 0) % 2
    column_patch = lax.broadcasted_iota(jnp.int32, (TOKENS, TOKENS), 1) % 2
    softmax_heads(tq, tk, chance_t, jnp.where(row_patch == column_patch, 0.0, -1e30))
    loads[3].wait()
    loads[4].wait()
    at_grad[...] = dot_nt(cot[...], weights[3]).astype(BF16)
    vt_grad[...] = attend_values_back(chance_t, at_grad).astype(BF16)
    out_plane[0] = move_tokens(1, vt_grad[...])
    grad_plane = start_plane(1, out_plane.at[0], in_plane.at[0])

    for number in (5, 6, 7, 8, 9, 10):
        loads[number].wait()
    sq[...] = sq_turned[...].T
    sk[...] = sk_turned[...].T
    value_s[...] = dot_nt(block[...], weights[0]).astype(BF16)
    softmax_heads(sq, sk, chance_s, None)
    attended_s[...] = attend(chance_s, value_s).astype(BF16)
    mixed[...] = (block[...].astype(F32) + dot(attended_s[...], weights[1])).astype(BF16)
    out_plane[1] = move_tokens(5, dot_nt(mixed[...], weights[2]).astype(BF16))
    value_plane = start_plane(2, out_plane.at[1], in_plane.at[1])

    arrive(grad_plane)
    out_z[0] = move_tokens(4, in_plane[0])
    grad_z = start_z(1, out_z.at[0], in_z.at[0])
    for number in (11, 12, 13, 14):
        loads[number].wait()
    feature_copies, column_copies = {}, {}
    feature_copies[0] = start_features(0, block)
    column_copies[1] = start_columns(1, attended_s[...])
    arrive(cot_z)
    out_plane_wide[...] = move_tokens(1, in_z_wide[...])
    cot_plane = start_plane(0, out_plane_wide, in_plane_wide)
    arrive(value_plane)
    out_z[1] = move_tokens(4, in_plane[1])
    value_z = start_z(2, out_z.at[1], in_z.at[1])
    feature_copies[2] = start_features(2, mixed)

    feature_copies[3] = start_features(3, cot)
    arrive(grad_z)
    vt_grad_frame[...] = move_tokens(3, in_z[0])
    column_copies[2] = start_columns(2, vt_grad_frame[...])
    arrive(cot_plane)
    cot_frame[...] = move_tokens(2, in_plane_wide[...])
    mixed_grad[...] = (cot_frame[...].astype(F32) + dot(vt_grad_frame[...], weights[2])).astype(BF16)
    feature_copies[1] = start_features(1, mixed_grad)
    ready(2)
    as_grad[...] = dot_nt(mixed_grad[...], weights[1]).astype(BF16)
    vs_grad[...] = attend_values_back(chance_s, as_grad).astype(BF16)
    column_copies[0] = start_columns(0, vs_grad[...])
    ready(1)
    arrive(value_z)
    value_t[...] = in_z[1]
    attended_t[...] = attend(chance_t, value_t).astype(BF16)
    column_copies[3] = start_columns(3, attended_t[...])
    first_relay(2, rings_at[2])
    ready(0)
    ready(3)
    first_relay(1, rings_at[1])
    input_grad[...] = (mixed_grad[...].astype(F32) + dot(vs_grad[...], weights[0])).astype(BF16)
    first_relay(0, rings_at[0])
    query_part, key_part = attend_scores_back(chance_s, sq, sk, value_s, as_grad)
    sq_grad[...] = query_part.astype(BF16).T
    sk_grad[...] = key_part.astype(BF16).T
    first_relay(3, rings_at[3])
    second_line(2)
    query_part, key_part = attend_scores_back(chance_t, tq, tk, value_t, at_grad)
    rows_one[...] = query_part
    rows_two[...] = key_part
    split_pairs(rows_one, tq_grad)
    split_pairs(rows_two, tk_grad)
    second_line(1)
    third_line(2)
    second_line(0)
    third_line(1)
    second_line(3)
    third_line(0)
    third_line(3)
    for number in (2, 1, 0, 3):
        finish(number)
    for copy in sent:
        copy.wait_send()


def hand_over(*refs):
    for at in range(6):
        refs[6 + at][...] = refs[at][...]


def body(
    block_input, spatial_queries, spatial_keys, cotangent, temporal_queries, temporal_keys, weights
):
    grad_scale = float(4 * 64 * 128) ** (-0.5)
    tables = make_tables()
    arrays = [
        block_input.reshape(TOKENS, WIDTH),
        spatial_queries.reshape(TOKENS, INNER).T,
        spatial_keys.reshape(TOKENS, INNER).T,
        cotangent.reshape(FRAMES, 2, WIDTH),
        temporal_queries.reshape(FRAMES, 2, INNER),
        temporal_keys.reshape(FRAMES, 2, INNER),
        weights.transpose(0, 2, 1),
    ] + tables
    wide, narrow = (TOKENS, WIDTH), (TOKENS, INNER)
    chances = pltpu.VMEM((HEADS, TOKENS, TOKENS), F32)
    dma = pltpu.SemaphoreType.DMA
    scratch = [pltpu.VMEM(array.shape, BF16) for array in arrays]
    scratch += [pltpu.VMEM(narrow, BF16)] * 2 + [pltpu.VMEM(wide, BF16)] + [pltpu.VMEM(narrow, BF16)] * 2
    scratch += [pltpu.VMEM(wide, F32)] + [pltpu.VMEM(narrow, F32)] * 2
    scratch += [chances, chances] + [pltpu.VMEM(narrow, BF16)] * 8
    scratch += [pltpu.VMEM(wide, BF16)] * 3 + [pltpu.VMEM(narrow, BF16)]
    scratch += [pltpu.VMEM(wide, BF16)] * 3 + [pltpu.VMEM((2,) + narrow, BF16)] * 4
    scratch += [
        pltpu.VMEM((4, WIDTH, 2 * TOKENS), BF16),
        pltpu.VMEM((4, 2, 2 * TOKENS, LANES), BF16),
        pltpu.VMEM((4, 2, TOKENS, LANES), BF16),
        pltpu.VMEM((4, 4, PIECE, 128), BF16),
        pltpu.VMEM((4, 6, CUT, 128), BF16),
        pltpu.VMEM((PIECE, 128), F32),
        pltpu.VMEM((4, 4, BLOCK_ROWS, 128), BF16),
        pltpu.VMEM((4, 3, BLOCK_ROWS, 128), BF16),
        pltpu.VMEM((4, 8, SHARE_ROWS, 128), BF16),
        pltpu.VMEM((4, 7, SHARE_ROWS, 128), BF16),
        pltpu.VMEM((SHARE_ROWS, 128), F32),
    ]
    scratch += [dma((15,))] + [dma((3, 7))] * 4 + [dma((4,))] * 4 + [dma((4, 6))] * 2 + [dma((4, 3))] * 2 + [dma((4, 7))] * 2
    results = [
        jax.ShapeDtypeStruct(wide, BF16),
        jax.ShapeDtypeStruct((INNER, TOKENS), BF16),
        jax.ShapeDtypeStruct((INNER, TOKENS), BF16),
        jax.ShapeDtypeStruct((FRAMES, 2, INNER), BF16),
        jax.ShapeDtypeStruct((FRAMES, 2, INNER), BF16),
        jax.ShapeDtypeStruct((18, 4, 144), F32),
    ]
    made = pl.pallas_call(
        functools.partial(kernel, grad_scale),
        out_shape=results,
        in_specs=[pl.BlockSpec(memory_space=pl.ANY)] * len(arrays),
        out_specs=[pl.BlockSpec(memory_space=pltpu.VMEM)] * 6,
        scratch_shapes=scratch,
        compiler_params=pltpu.CompilerParams(
            collective_id=0, has_side_effects=True, vmem_limit_bytes=56 * 2**20
        ),
        name="block_backward",
    )(*arrays)
    input_grad, sq_grad, sk_grad, tq_grad, tk_grad, weight_grads = pl.pallas_call(
        hand_over,
        out_shape=results,
        in_specs=[pl.BlockSpec(memory_space=pltpu.VMEM)] * 6,
        out_specs=[pl.BlockSpec(memory_space=pltpu.VMEM)] * 6,
        compiler_params=pltpu.CompilerParams(vmem_limit_bytes=60 * 2**20),
        name="hand_over",
    )(*made)
    return (
        input_grad.reshape(block_input.shape),
        sq_grad.T.reshape(spatial_queries.shape),
        sk_grad.T.reshape(spatial_keys.shape),
        tq_grad.reshape(temporal_queries.shape),
        tk_grad.reshape(temporal_keys.shape),
        weight_grads.transpose(1, 0, 2),
    )


def solution(mesh):
    placed = (
        P("dp", "seq", None, None),
        P("dp", "seq", None, None),
        P("dp", "seq", None, None),
        P("dp", None, "seq", None),
        P("dp", None, "seq", None),
        P("dp", None, "seq", None),
        P(),
    )
    return jax.shard_map(
        body,
        mesh=mesh,
        in_specs=placed,
        out_specs=(
            P("dp", "seq", None, None),
            P("dp", "seq", None, None),
            P("dp", "seq", None, None),
            P("dp", None, "seq", None),
            P("dp", None, "seq", None),
            P(None, "seq", "dp"),
        ),
        check_vma=False,
    )
```

```python
import functools

import jax
import jax.numpy as jnp
import numpy as np
from jax import lax
from jax.experimental import pallas as pl
from jax.experimental.pallas import tpu as pltpu
from jax.sharding import PartitionSpec as P

HEADS = 8
HEAD_DIM = 72
WIDTH = 1152
INNER = 576
TOKENS = 128
FRAMES = 64
SCORE_SCALE = HEAD_DIM ** (-0.5)
ROW_BLOCK = 144
LANES = 256
PIECE = 4 * ROW_BLOCK + 80
CUT = 336
BLOCK_ROWS = ROW_BLOCK + 32
SHARE_ROWS = 32
PAIRS = ((1, 3), (2, 0))
F32 = jnp.float32
BF16 = jnp.bfloat16
MESH = pl.DeviceIdType.MESH


def one_hot(source, size):
    table = np.zeros((len(source), size), np.float32)
    for row, at in enumerate(source):
        if at >= 0:
            table[row, at] = 1.0
    return table


def make_tables():
    def natural(y_lo, z, x, p):
        return 2 * (y_lo * 32 + z * 4 + x) + p

    to_z = [natural(y, z, x, p) for z in range(8) for y in range(2) for x in range(4) for p in range(2)]
    to_plane = [z * 16 + q * 2 + p for q in range(8) for z in range(8) for p in range(2)]
    to_natural = [
        (y * 4 + x) * 16 + z * 2 + p for y in range(2) for z in range(8) for x in range(4) for p in range(2)
    ]
    forth = [one_hot(order, TOKENS) for order in (to_z, to_plane, to_natural)]
    token_moves = np.stack(forth + [table.T for table in forth])
    feature_moves = np.stack(
        [
            one_hot(
                [y * 64 + z * 72 + x * 18 + r for x in range(4) for z in range(8) for r in range(18)], 640
            )
            for y in range(2)
        ]
    )
    picks = np.zeros((2, 2, INNER, LANES), np.float32)
    for core in range(2):
        for y_hi in range(2):
            for column in range(144):
                picks[core, y_hi, (2 * y_hi + core) * 144 + column, column] = 1.0
    share_moves = one_hot(
        [z * 18 + row if row < 18 else -1 for z in range(8) for row in range(SHARE_ROWS)], ROW_BLOCK
    )
    rest_moves = []
    for group in range(2):
        source = []
        for z in range(8):
            for row in range(SHARE_ROWS):
                at = z * 18 + 9 * group + row - 18
                place, turn = at // 16, (group - at // 16) % 8
                source.append(turn * 32 + place // 8 * 16 + at % 16 if 18 <= row < 27 else -1)
        rest_moves.append(one_hot(source, 256))
    tables = (token_moves, feature_moves, picks, share_moves, np.stack(rest_moves))
    return [jnp.asarray(table, BF16) for table in tables]


def line_order(frame):
    y_lo, z, x = frame // 32, frame // 4 % 8, frame % 4
    start = 2 * (z * 8 + y_lo * 4 + x)
    return slice(start, start + 2)


def dot(left, right):
    return jnp.dot(left, right, preferred_element_type=F32)


def dot_nt(left, right):
    return lax.dot_general(left, right, (((1,), (1,)), ((), ())), preferred_element_type=F32)


def dot_tn(left, right):
    return lax.dot_general(left, right, (((0,), (0,)), ((), ())), preferred_element_type=F32)


def head_window(head):
    start = head * HEAD_DIM // 128 * 128
    stop = min(-(-(head * HEAD_DIM + HEAD_DIM) // 128) * 128, INNER)
    return start, stop


def head_mask(head):
    start, stop = head_window(head)
    lane = lax.broadcasted_iota(jnp.int32, (TOKENS, stop - start), 1) + start
    return (lane >= head * HEAD_DIM) & (lane < (head + 1) * HEAD_DIM)


def window(ref, head):
    start, stop = head_window(head)
    return ref[:, start:stop]


def masked_window(ref, head):
    return jnp.where(head_mask(head), window(ref, head).astype(F32), 0.0).astype(BF16)


def join_heads(parts):
    tiles = [None] * 5
    for head, part in enumerate(parts):
        start, stop = head_window(head)
        part = jnp.where(head_mask(head), part, 0.0)
        for at in range(start, stop, 128):
            piece = part[:, at - start : min(at - start + 128, stop - start)]
            tiles[at // 128] = piece if tiles[at // 128] is None else tiles[at // 128] + piece
    return jnp.concatenate(tiles, axis=1)


def softmax_heads(queries, key_rows, chance_ref, bias):
    for head in range(HEADS):
        scores = dot_nt(masked_window(queries, head), window(key_rows, head)) * SCORE_SCALE
        if bias is not None:
            scores = scores + bias
        powers = jnp.exp(scores - jnp.max(scores, axis=1, keepdims=True))
        chance_ref[head] = powers / jnp.sum(powers, axis=1, keepdims=True)


def attend(chance_ref, values):
    return join_heads([dot(chance_ref[h].astype(BF16), window(values, h)) for h in range(HEADS)])


def attend_values_back(chance_ref, out_grad):
    return join_heads([dot_tn(chance_ref[h].astype(BF16), window(out_grad, h)) for h in range(HEADS)])


def attend_scores_back(chance_ref, queries, key_rows, values, out_grad):
    query_parts, key_parts = [], []
    for head in range(HEADS):
        chance = chance_ref[head]
        chance_grad = dot_nt(masked_window(out_grad, head), window(values, head))
        centre = jnp.sum(chance * chance_grad, axis=1, keepdims=True)
        score_grad = (chance * (chance_grad - centre)).astype(BF16)
        query_parts.append(dot(score_grad, window(key_rows, head)))
        key_parts.append(dot_tn(score_grad, window(queries, head)))
    return join_heads(query_parts) * SCORE_SCALE, join_heads(key_parts) * SCORE_SCALE


def kernel(
    grad_scale,
    block_hbm, sq_hbm, sk_hbm, cot_hbm, tq_hbm, tk_hbm, weights_hbm,
    token_moves_hbm, feature_moves_hbm, picks_hbm, share_moves_hbm, rest_moves_hbm,
    input_grad_hbm, sq_grad_hbm, sk_grad_hbm, tq_grad_hbm, tk_grad_hbm, weight_grads_hbm,
    input_grad, sq_grad, sk_grad, tq_grad, tk_grad, weight_grads,
    block, sq_turned, sk_turned, cot_pairs, tq_pairs, tk_pairs, weights, token_moves, feature_moves, picks, share_moves, rest_moves,
    sq, sk, cot, tq, tk, rows_wide, rows_one, rows_two,
    chance_s, chance_t, value_s, value_t, attended_s, attended_t, at_grad, as_grad, vt_grad, vs_grad,
    mixed, mixed_grad, cot_frame, vt_grad_frame,
    in_z_wide, out_plane_wide, in_plane_wide, out_plane, in_plane, out_z, in_z,
    factors, picked, picked_out, sums, arrived, total_one, sums_two, arrived_two, shares, shares_in, total_share,
    load_sem, store_sem, z_send, z_recv, plane_send, plane_recv, factor_send, factor_recv, picked_send, picked_recv,
    ring_send, ring_recv, ring_two_send, ring_two_recv, share_send, share_recv,
):
    dp, seq = lax.axis_index("dp"), lax.axis_index("seq")
    y_hi, core = dp // 2, dp % 2
    y_lo, z, x = seq // 32, (seq // 4) % 8, seq % 4
    y = y_hi * 2 + y_lo
    q = y_lo * 4 + x

    def device(y_hi_at=y_hi, core_at=core, y_lo_at=y_lo, z_at=z, x_at=x):
        return (y_hi_at * 2 + core_at, y_lo_at * 32 + z_at * 4 + x_at)

    def along_z(step):
        return device(z_at=(z + step) % 8)

    def in_the_plane(step):
        to = (q + step) % 8
        return device(y_lo_at=to // 4, x_at=to % 4)

    def along_x(step):
        return device(x_at=(x + step) % 4)

    def along_y(step):
        to = (y + step) % 4
        return device(y_hi_at=to // 2, y_lo_at=to % 2)

    sibling = device(core_at=1 - core)

    loads = []
    for number, (source, target) in enumerate(
        [
            (cot_hbm, cot_pairs), (tq_hbm, tq_pairs), (tk_hbm, tk_pairs), (weights_hbm.at[3], weights.at[3]),
            (token_moves_hbm, token_moves), (block_hbm, block), (weights_hbm.at[0], weights.at[0]),
            (sq_hbm, sq_turned), (sk_hbm, sk_turned), (weights_hbm.at[1], weights.at[1]), (weights_hbm.at[2], weights.at[2]),
            (feature_moves_hbm, feature_moves), (picks_hbm, picks), (share_moves_hbm, share_moves),
            (rest_moves_hbm, rest_moves),
        ]
    ):
        copy = pltpu.make_async_copy(source, target, load_sem.at[number])
        if number < 3:
            copy.start()
        loads.append(copy)

    barrier = pltpu.get_barrier_semaphore()
    greeted = [along_z(step) for step in range(1, 8)] + [in_the_plane(step) for step in range(1, 8)]
    greeted += [device(y_hi_at=1 - y_hi, y_lo_at=1 - y_lo), sibling]
    for peer in greeted:
        pl.semaphore_signal(barrier, inc=1, device_id=peer, device_id_type=MESH)

    sent, stored = [], []

    def store(source, target):
        copy = pltpu.make_async_copy(source, target, store_sem.at[len(stored)])
        copy.start()
        stored.append(copy)

    def send(source, target, send_sem, recv_sem, peer):
        copy = pltpu.make_async_remote_copy(
            src_ref=source, dst_ref=target, send_sem=send_sem, recv_sem=recv_sem,
            device_id=peer, device_id_type=MESH,
        )
        copy.start()
        sent.append(copy)
        return copy

    def move_tokens(number, rows):
        return dot(token_moves[number], rows).astype(BF16)

    def start_z(item, source, target):
        copies = []
        for step in range(1, 8):
            to = (z + step) % 8
            copies.append(
                send(
                    source.at[pl.ds(to * 16, 16)], target.at[pl.ds(z * 16, 16)],
                    z_send.at[item, step - 1], z_recv.at[item, step - 1], along_z(step),
                )
            )
        own = pl.ds(pl.multiple_of(z * 16, 16), 16)
        target[own, :] = source[own, :]
        return copies

    def start_plane(item, source, target):
        copies = []
        for step in range(1, 8):
            to = (q + step) % 8
            copies.append(
                send(
                    source.at[pl.ds(to * 16, 16)], target.at[pl.ds(q * 16, 16)],
                    plane_send.at[item, step - 1], plane_recv.at[item, step - 1], in_the_plane(step),
                )
            )
        own = pl.ds(pl.multiple_of(q * 16, 16), 16)
        target[own, :] = source[own, :]
        return copies

    def arrive(copies):
        for copy in copies:
            copy.wait_recv()

    def start_features(number, rows_ref):
        for half in range(2):
            factors[number, half * INNER : (half + 1) * INNER, 0:TOKENS] = dot_nt(
                feature_moves[half], rows_ref[:, half * 512 : half * 512 + 640]
            ).astype(BF16)
        return send(
            factors.at[number, :, 0:TOKENS], factors.at[number, :, TOKENS : 2 * TOKENS],
            factor_send.at[number], factor_recv.at[number], sibling,
        )

    def start_columns(number, rows):
        for side in range(2):
            picked[number, side, 0:TOKENS, :] = dot(rows, picks[core, side]).astype(BF16)
            picked_out[number, side] = dot(rows, picks[1 - core, side]).astype(BF16)
        return send(
            picked_out.at[number], picked.at[number, :, TOKENS : 2 * TOKENS],
            picked_send.at[number], picked_recv.at[number], sibling,
        )

    places = (x, y)
    rings = (along_x, along_y)
    ring_of = {number: ring for ring, numbers in enumerate(PAIRS) for number in numbers}
    slot_half = (0, 1, 1, 0, 0, 1)

    def make_pieces(number, to):
        rests = None
        for sub in range(4):
            side, y_lo_at, x_at = (sub // 2, sub % 2, to) if ring_of[number] == 0 else (to // 2, to % 2, sub)
            rows = pl.ds(pl.multiple_of((y_lo_at * 4 + x_at) * ROW_BLOCK, 16), ROW_BLOCK)
            total = dot(factors[number, rows, :], picked[number, side])
            sums[number, to, sub * ROW_BLOCK : (sub + 1) * ROW_BLOCK, :] = total[:, 0:128].astype(BF16)
            rest = total[:, 128:256]
            rests = rest if sub == 0 else rests + pltpu.roll(rest, 16 * sub, 1)
        beside = jnp.concatenate([pltpu.roll(rests[80:ROW_BLOCK], 64, 1), jnp.zeros((16, 128), F32)], axis=0)
        sums[number, to, 4 * ROW_BLOCK : PIECE, :] = (rests[0:80] + beside).astype(BF16)

    def piece(number, to, half):
        return sums.at[number, to, 0:CUT] if half == 0 else sums.at[number, to, CUT:PIECE]

    def slot_ref(number, slot):
        return arrived.at[number, slot, 0 : (CUT if slot_half[slot] == 0 else PIECE - CUT)]

    def ring_copy(number, slot, source):
        peer = rings[ring_of[number]](1 if slot % 2 == 0 else 3)
        return send(source, slot_ref(number, slot), ring_send.at[number, slot], ring_recv.at[number, slot], peer)

    def first_ring(number):
        place = places[ring_of[number]]
        after, across, before = (place + 1) % 4, (place + 2) % 4, (place + 3) % 4
        copies = {}
        make_pieces(number, across)
        copies[0] = ring_copy(number, 0, piece(number, across, 0))
        copies[1] = ring_copy(number, 1, piece(number, across, 1))
        make_pieces(number, after)
        copies[2] = ring_copy(number, 2, piece(number, after, 1))
        make_pieces(number, before)
        copies[3] = ring_copy(number, 3, piece(number, before, 0))
        make_pieces(number, place)
        return copies

    def first_relay(number, copies):
        place = places[ring_of[number]]
        after, before = (place + 1) % 4, (place + 3) % 4
        for slot, to, half in ((0, after, 0), (1, before, 1)):
            copies[slot].wait_recv()
            ref = piece(number, to, half)
            ref[...] = (ref[...].astype(F32) + slot_ref(number, slot)[...].astype(F32)).astype(BF16)
            copies[slot + 4] = ring_copy(number, slot + 4, ref)

    lane_group = lax.broadcasted_iota(jnp.int32, (16, 128), 1) // 16
    share_group = lax.broadcasted_iota(jnp.int32, (8 * SHARE_ROWS, 128), 1) // 16

    def second_place(number):
        return places[1 - ring_of[number]]

    def second_line(number):
        copies = rings_at[number]
        for half, slots in ((0, (3, 4)), (1, (2, 5))):
            total = piece(number, places[ring_of[number]], half)[...].astype(F32)
            for slot in slots:
                copies[slot].wait_recv()
                total += slot_ref(number, slot)[...].astype(F32)
            total_one[(0 if half == 0 else CUT) : (CUT if half == 0 else PIECE), :] = total
        for sub in range(4):
            sums_two[number, sub, 0:ROW_BLOCK, :] = total_one[sub * ROW_BLOCK : (sub + 1) * ROW_BLOCK, :].astype(BF16)
            for tile in range(2):
                packed = jnp.zeros((16, 128), F32)
                for group in range(8) if tile == 0 else (8,):
                    start = 4 * ROW_BLOCK + 16 * (group % 5)
                    turn = (16 * (group % 8) - 16 * sub - (64 if group >= 5 else 0)) % 128
                    rest = total_one[start : start + 16, :]
                    rest = pltpu.roll(rest, turn, 1) if turn else rest
                    packed = jnp.where(lane_group == group % 8, rest, packed)
                start = ROW_BLOCK + 16 * tile
                sums_two[number, sub, start : start + 16, :] = packed.astype(BF16)
        seconds[number] = [
            send(
                sums_two.at[number, (second_place(number) + step) % 4], arrived_two.at[number, step - 1],
                ring_two_send.at[number, step - 1], ring_two_recv.at[number, step - 1],
                rings[1 - ring_of[number]](step),
            )
            for step in range(1, 4)
        ]

    def third_line(number):
        total = sums_two[number, second_place(number)].astype(F32)
        for step in range(1, 4):
            seconds[number][step - 1].wait_recv()
            total += arrived_two[number, step - 1].astype(F32)
        moved = dot(share_moves[...], total[0:ROW_BLOCK].astype(BF16))
        ends = total[ROW_BLOCK:BLOCK_ROWS]
        turned = [ends] + [pltpu.roll(ends, 16 * turn, 1) for turn in range(1, 8)]
        turned = jnp.concatenate(turned, axis=0).astype(BF16)
        for group in range(2):
            moved += jnp.where(share_group == group, dot(rest_moves[group], turned), 0.0)
        moved = moved.astype(BF16)
        for z_at in range(8):
            shares[number, z_at] = moved[SHARE_ROWS * z_at : SHARE_ROWS * (z_at + 1)]
        thirds[number] = [
            send(
                shares.at[number, (z + step) % 8], shares_in.at[number, step - 1],
                share_send.at[number, step - 1], share_recv.at[number, step - 1], along_z(step),
            )
            for step in range(1, 8)
        ]

    def finish(number):
        total = shares[number, z].astype(F32)
        for step in range(1, 8):
            thirds[number][step - 1].wait_recv()
            total += shares_in[number, step - 1].astype(F32)
        total_share[...] = total * grad_scale
        weight_grads[:, number, 0:128] = total_share[0:18, :]
        for half in range(2):
            weight_grads[9 * half : 9 * half + 9, number, 128:144] = total_share[18:27, 16 * half : 16 * half + 16]

    rings_at, seconds, thirds = {}, {}, {}

    def ready(number):
        arrive([feature_copies[number], column_copies[number]])
        rings_at[number] = first_ring(number)

    def join_pairs(pairs, rows):
        for frame in range(FRAMES):
            rows[line_order(frame), :] = pairs[frame].astype(F32)
        return rows[...].astype(BF16)

    def split_pairs(rows, pairs):
        for frame in range(FRAMES):
            pairs[frame] = rows[line_order(frame), :].astype(BF16)

    loads[0].wait()
    for copy in loads[3:11]:
        copy.start()
    cot[...] = join_pairs(cot_pairs, rows_wide)
    pl.semaphore_wait(barrier, len(greeted))
    cot_z = start_z(0, cot, in_z_wide)
    for copy in loads[11:]:
        copy.start()
    loads[1].wait()
    loads[2].wait()
    tq[...] = join_pairs(tq_pairs, rows_one)
    tk[...] = join_pairs(tk_pairs, rows_two)
    row_patch = lax.broadcasted_iota(jnp.int32, (TOKENS, TOKENS), 0) % 2
    column_patch = lax.broadcasted_iota(jnp.int32, (TOKENS, TOKENS), 1) % 2
    softmax_heads(tq, tk, chance_t, jnp.where(row_patch == column_patch, 0.0, -1e30))
    loads[3].wait()
    loads[4].wait()
    at_grad[...] = dot_nt(cot[...], weights[3]).astype(BF16)
    vt_grad[...] = attend_values_back(chance_t, at_grad).astype(BF16)
    out_plane[0] = move_tokens(1, vt_grad[...])
    grad_plane = start_plane(1, out_plane.at[0], in_plane.at[0])

    for number in (5, 6, 7, 8, 9, 10):
        loads[number].wait()
    sq[...] = sq_turned[...].T
    sk[...] = sk_turned[...].T
    value_s[...] = dot_nt(block[...], weights[0]).astype(BF16)
    softmax_heads(sq, sk, chance_s, None)
    attended_s[...] = attend(chance_s, value_s).astype(BF16)
    mixed[...] = (block[...].astype(F32) + dot(attended_s[...], weights[1])).astype(BF16)
    out_plane[1] = move_tokens(5, dot_nt(mixed[...], weights[2]).astype(BF16))
    value_plane = start_plane(2, out_plane.at[1], in_plane.at[1])

    arrive(grad_plane)
    out_z[0] = move_tokens(4, in_plane[0])
    grad_z = start_z(1, out_z.at[0], in_z.at[0])
    for number in (11, 12, 13, 14):
        loads[number].wait()
    feature_copies, column_copies = {}, {}
    feature_copies[0] = start_features(0, block)
    column_copies[1] = start_columns(1, attended_s[...])
    arrive(cot_z)
    out_plane_wide[...] = move_tokens(1, in_z_wide[...])
    cot_plane = start_plane(0, out_plane_wide, in_plane_wide)
    arrive(value_plane)
    out_z[1] = move_tokens(4, in_plane[1])
    value_z = start_z(2, out_z.at[1], in_z.at[1])
    feature_copies[2] = start_features(2, mixed)

    feature_copies[3] = start_features(3, cot)
    arrive(grad_z)
    vt_grad_frame[...] = move_tokens(3, in_z[0])
    column_copies[2] = start_columns(2, vt_grad_frame[...])
    arrive(cot_plane)
    cot_frame[...] = move_tokens(2, in_plane_wide[...])
    mixed_grad[...] = (cot_frame[...].astype(F32) + dot(vt_grad_frame[...], weights[2])).astype(BF16)
    feature_copies[1] = start_features(1, mixed_grad)
    ready(2)
    ready(1)
    as_grad[...] = dot_nt(mixed_grad[...], weights[1]).astype(BF16)
    vs_grad[...] = attend_values_back(chance_s, as_grad).astype(BF16)
    column_copies[0] = start_columns(0, vs_grad[...])
    arrive(value_z)
    value_t[...] = in_z[1]
    attended_t[...] = attend(chance_t, value_t).astype(BF16)
    column_copies[3] = start_columns(3, attended_t[...])
    first_relay(2, rings_at[2])
    ready(0)
    ready(3)
    first_relay(1, rings_at[1])
    input_grad[...] = (mixed_grad[...].astype(F32) + dot(vs_grad[...], weights[0])).astype(BF16)
    store(input_grad, input_grad_hbm)
    first_relay(0, rings_at[0])
    query_part, key_part = attend_scores_back(chance_s, sq, sk, value_s, as_grad)
    sq_grad[...] = query_part.astype(BF16).T
    sk_grad[...] = key_part.astype(BF16).T
    store(sq_grad, sq_grad_hbm)
    store(sk_grad, sk_grad_hbm)
    first_relay(3, rings_at[3])
    second_line(2)
    query_part, key_part = attend_scores_back(chance_t, tq, tk, value_t, at_grad)
    rows_one[...] = query_part
    rows_two[...] = key_part
    split_pairs(rows_one, tq_grad)
    split_pairs(rows_two, tk_grad)
    store(tq_grad, tq_grad_hbm)
    store(tk_grad, tk_grad_hbm)
    second_line(1)
    third_line(2)
    second_line(0)
    third_line(1)
    second_line(3)
    third_line(0)
    third_line(3)
    for number in (2, 1, 0, 3):
        finish(number)
    store(weight_grads, weight_grads_hbm)
    for copy in sent:
        copy.wait_send()
    for copy in stored:
        copy.wait()


def hand_over(*refs):
    sources, targets, buffers, (in_sem, out_sem) = refs[0:6], refs[6:12], refs[12:18], refs[18:20]
    arriving = [pltpu.make_async_copy(sources[at], buffers[at], in_sem.at[at]) for at in range(6)]
    leaving = [pltpu.make_async_copy(buffers[at], targets[at], out_sem.at[at]) for at in range(6)]
    for copy in arriving:
        copy.start()
    for copy, onward in zip(arriving, leaving):
        copy.wait()
        onward.start()
    for onward in leaving:
        onward.wait()


def body(
    block_input, spatial_queries, spatial_keys, cotangent, temporal_queries, temporal_keys, weights
):
    grad_scale = float(4 * 64 * 128) ** (-0.5)
    tables = make_tables()
    arrays = [
        block_input.reshape(TOKENS, WIDTH),
        spatial_queries.reshape(TOKENS, INNER).T,
        spatial_keys.reshape(TOKENS, INNER).T,
        cotangent.reshape(FRAMES, 2, WIDTH),
        temporal_queries.reshape(FRAMES, 2, INNER),
        temporal_keys.reshape(FRAMES, 2, INNER),
        weights.transpose(0, 2, 1),
    ] + tables
    wide, narrow = (TOKENS, WIDTH), (TOKENS, INNER)
    chances = pltpu.VMEM((HEADS, TOKENS, TOKENS), F32)
    dma = pltpu.SemaphoreType.DMA
    results = [
        jax.ShapeDtypeStruct(wide, BF16),
        jax.ShapeDtypeStruct((INNER, TOKENS), BF16),
        jax.ShapeDtypeStruct((INNER, TOKENS), BF16),
        jax.ShapeDtypeStruct((FRAMES, 2, INNER), BF16),
        jax.ShapeDtypeStruct((FRAMES, 2, INNER), BF16),
        jax.ShapeDtypeStruct((18, 4, 144), F32),
    ]
    buffers = [pltpu.VMEM(result.shape, result.dtype) for result in results]
    scratch = buffers + [pltpu.VMEM(array.shape, BF16) for array in arrays]
    scratch += [pltpu.VMEM(narrow, BF16)] * 2 + [pltpu.VMEM(wide, BF16)] + [pltpu.VMEM(narrow, BF16)] * 2
    scratch += [pltpu.VMEM(wide, F32)] + [pltpu.VMEM(narrow, F32)] * 2
    scratch += [chances, chances] + [pltpu.VMEM(narrow, BF16)] * 8
    scratch += [pltpu.VMEM(wide, BF16)] * 3 + [pltpu.VMEM(narrow, BF16)]
    scratch += [pltpu.VMEM(wide, BF16)] * 3 + [pltpu.VMEM((2,) + narrow, BF16)] * 4
    scratch += [
        pltpu.VMEM((4, WIDTH, 2 * TOKENS), BF16),
        pltpu.VMEM((4, 2, 2 * TOKENS, LANES), BF16),
        pltpu.VMEM((4, 2, TOKENS, LANES), BF16),
        pltpu.VMEM((4, 4, PIECE, 128), BF16),
        pltpu.VMEM((4, 6, CUT, 128), BF16),
        pltpu.VMEM((PIECE, 128), F32),
        pltpu.VMEM((4, 4, BLOCK_ROWS, 128), BF16),
        pltpu.VMEM((4, 3, BLOCK_ROWS, 128), BF16),
        pltpu.VMEM((4, 8, SHARE_ROWS, 128), BF16),
        pltpu.VMEM((4, 7, SHARE_ROWS, 128), BF16),
        pltpu.VMEM((SHARE_ROWS, 128), F32),
    ]
    scratch += [dma((15,)), dma((6,))] + [dma((3, 7))] * 4 + [dma((4,))] * 4 + [dma((4, 6))] * 2 + [dma((4, 3))] * 2 + [dma((4, 7))] * 2
    made = pl.pallas_call(
        functools.partial(kernel, grad_scale),
        out_shape=results,
        in_specs=[pl.BlockSpec(memory_space=pl.ANY)] * len(arrays),
        out_specs=[pl.BlockSpec(memory_space=pl.ANY)] * 6,
        scratch_shapes=scratch,
        compiler_params=pltpu.CompilerParams(
            collective_id=0, has_side_effects=True, vmem_limit_bytes=56 * 2**20
        ),
        name="block_backward",
    )(*arrays)
    input_grad, sq_grad, sk_grad, tq_grad, tk_grad, weight_grads = pl.pallas_call(
        hand_over,
        out_shape=results,
        in_specs=[pl.BlockSpec(memory_space=pl.ANY)] * 6,
        out_specs=[pl.BlockSpec(memory_space=pl.ANY)] * 6,
        scratch_shapes=buffers + [dma((6,)), dma((6,))],
        compiler_params=pltpu.CompilerParams(vmem_limit_bytes=60 * 2**20),
        name="hand_over",
    )(*made)
    return (
        input_grad.reshape(block_input.shape),
        sq_grad.T.reshape(spatial_queries.shape),
        sk_grad.T.reshape(spatial_keys.shape),
        tq_grad.reshape(temporal_queries.shape),
        tk_grad.reshape(temporal_keys.shape),
        weight_grads.transpose(1, 0, 2),
    )


def solution(mesh):
    placed = (
        P("dp", "seq", None, None),
        P("dp", "seq", None, None),
        P("dp", "seq", None, None),
        P("dp", None, "seq", None),
        P("dp", None, "seq", None),
        P("dp", None, "seq", None),
        P(),
    )
    return jax.shard_map(
        body,
        mesh=mesh,
        in_specs=placed,
        out_specs=(
            P("dp", "seq", None, None),
            P("dp", "seq", None, None),
            P("dp", "seq", None, None),
            P("dp", None, "seq", None),
            P("dp", None, "seq", None),
            P(None, "seq", "dp"),
        ),
        check_vma=False,
    )
```

```python
import functools

import jax
import jax.numpy as jnp
import numpy as np
from jax import lax
from jax.experimental import pallas as pl
from jax.experimental.pallas import tpu as pltpu
from jax.sharding import PartitionSpec as P

HEADS = 8
HEAD_DIM = 72
WIDTH = 1152
INNER = 576
TOKENS = 128
FRAMES = 64
SCORE_SCALE = HEAD_DIM ** (-0.5)
ROW_BLOCK = 144
LANES = 256
ROWS_OF = (80, 64)
REST_ROWS = (48, 32)
PIECE = (4 * 80 + 48, 4 * 64 + 32)
CUT = (192, 144)
SHARE_ROWS = 32
F32 = jnp.float32
BF16 = jnp.bfloat16
MESH = pl.DeviceIdType.MESH


def one_hot(source, size):
    table = np.zeros((len(source), size), np.float32)
    for row, at in enumerate(source):
        if at >= 0:
            table[row, at] = 1.0
    return table


def make_tables():
    def natural(y_lo, z, x, p):
        return 2 * (y_lo * 32 + z * 4 + x) + p

    to_z = [natural(y, z, x, p) for z in range(8) for y in range(2) for x in range(4) for p in range(2)]
    to_plane = [z * 16 + q * 2 + p for q in range(8) for z in range(8) for p in range(2)]
    to_natural = [
        (y * 4 + x) * 16 + z * 2 + p for y in range(2) for z in range(8) for x in range(4) for p in range(2)
    ]
    forth = [one_hot(order, TOKENS) for order in (to_z, to_plane, to_natural)]
    token_moves = np.stack(forth + [table.T for table in forth])
    feature_moves = np.stack(
        [
            one_hot(
                [y * 64 + z * 72 + x * 18 + r for x in range(4) for z in range(8) for r in range(18)], 640
            )
            for y in range(2)
        ]
    )
    picks = np.zeros((2, 2, INNER, LANES), np.float32)
    for core in range(2):
        for y_hi in range(2):
            for column in range(144):
                picks[core, y_hi, (2 * y_hi + core) * 144 + column, column] = 1.0
    share_moves = one_hot(
        [z * 18 + row if row < 18 else -1 for z in range(8) for row in range(SHARE_ROWS)], ROW_BLOCK
    )
    rest_moves = []
    for group in range(2):
        source = []
        for z in range(8):
            for row in range(SHARE_ROWS):
                at = z * 18 + 9 * group + row - 18
                tile, place = divmod(at // 16, 5)
                source.append((group - place) % 8 * 32 + tile * 16 + at % 16 if 18 <= row < 27 else -1)
        rest_moves.append(one_hot(source, 256))
    tables = (token_moves, feature_moves, picks, share_moves, np.stack(rest_moves))
    return [jnp.asarray(table, BF16) for table in tables]


def line_order(frame):
    y_lo, z, x = frame // 32, frame // 4 % 8, frame % 4
    start = 2 * (z * 8 + y_lo * 4 + x)
    return slice(start, start + 2)


def dot(left, right):
    return jnp.dot(left, right, preferred_element_type=F32)


def dot_nt(left, right):
    return lax.dot_general(left, right, (((1,), (1,)), ((), ())), preferred_element_type=F32)


def dot_tn(left, right):
    return lax.dot_general(left, right, (((0,), (0,)), ((), ())), preferred_element_type=F32)


def head_window(head):
    start = head * HEAD_DIM // 128 * 128
    stop = min(-(-(head * HEAD_DIM + HEAD_DIM) // 128) * 128, INNER)
    return start, stop


def head_mask(head):
    start, stop = head_window(head)
    lane = lax.broadcasted_iota(jnp.int32, (TOKENS, stop - start), 1) + start
    return (lane >= head * HEAD_DIM) & (lane < (head + 1) * HEAD_DIM)


def window(ref, head):
    start, stop = head_window(head)
    return ref[:, start:stop]


def masked_window(ref, head):
    return jnp.where(head_mask(head), window(ref, head).astype(F32), 0.0).astype(BF16)


def join_heads(parts):
    tiles = [None] * 5
    for head, part in enumerate(parts):
        start, stop = head_window(head)
        part = jnp.where(head_mask(head), part, 0.0)
        for at in range(start, stop, 128):
            piece = part[:, at - start : min(at - start + 128, stop - start)]
            tiles[at // 128] = piece if tiles[at // 128] is None else tiles[at // 128] + piece
    return jnp.concatenate(tiles, axis=1)


def softmax_heads(queries, key_rows, chance_ref, bias):
    for head in range(HEADS):
        scores = dot_nt(masked_window(queries, head), window(key_rows, head)) * SCORE_SCALE
        if bias is not None:
            scores = scores + bias
        powers = jnp.exp(scores - jnp.max(scores, axis=1, keepdims=True))
        chance_ref[head] = powers / jnp.sum(powers, axis=1, keepdims=True)


def attend(chance_ref, values):
    return join_heads([dot(chance_ref[h].astype(BF16), window(values, h)) for h in range(HEADS)])


def attend_values_back(chance_ref, out_grad):
    return join_heads([dot_tn(chance_ref[h].astype(BF16), window(out_grad, h)) for h in range(HEADS)])


def attend_scores_back(chance_ref, queries, key_rows, values, out_grad):
    query_parts, key_parts = [], []
    for head in range(HEADS):
        chance = chance_ref[head]
        chance_grad = dot_nt(masked_window(out_grad, head), window(values, head))
        centre = jnp.sum(chance * chance_grad, axis=1, keepdims=True)
        score_grad = (chance * (chance_grad - centre)).astype(BF16)
        query_parts.append(dot(score_grad, window(key_rows, head)))
        key_parts.append(dot_tn(score_grad, window(queries, head)))
    return join_heads(query_parts) * SCORE_SCALE, join_heads(key_parts) * SCORE_SCALE


def kernel(
    grad_scale,
    block_hbm, sq_hbm, sk_hbm, cot_hbm, tq_hbm, tk_hbm, weights_hbm,
    token_moves_hbm, feature_moves_hbm, picks_hbm, share_moves_hbm, rest_moves_hbm,
    input_grad_hbm, sq_grad_hbm, sk_grad_hbm, tq_grad_hbm, tk_grad_hbm, weight_grads_hbm,
    input_grad, sq_grad, sk_grad, tq_grad, tk_grad, weight_grads,
    block, sq_turned, sk_turned, cot_pairs, tq_pairs, tk_pairs, weights, token_moves, feature_moves, picks, share_moves, rest_moves,
    sq, sk, cot, tq, tk, rows_wide, rows_one, rows_two,
    chance_s, chance_t, value_s, value_t, attended_s, attended_t, at_grad, as_grad, vt_grad, vs_grad,
    mixed, mixed_grad, cot_frame, vt_grad_frame,
    in_z_wide, out_plane_wide, in_plane_wide, out_plane, in_plane, out_z, in_z,
    factors, picked, picked_out, sums, arrived, total_one, sums_two, arrived_two, shares, shares_in, total_share,
    load_sem, store_sem, z_send, z_recv, plane_send, plane_recv, factor_send, factor_recv, picked_send, picked_recv,
    ring_send, ring_recv, ring_two_send, ring_two_recv, share_send, share_recv,
):
    dp, seq = lax.axis_index("dp"), lax.axis_index("seq")
    y_hi, core = dp // 2, dp % 2
    y_lo, z, x = seq // 32, (seq // 4) % 8, seq % 4
    y = y_hi * 2 + y_lo
    q = y_lo * 4 + x

    def device(y_hi_at=y_hi, core_at=core, y_lo_at=y_lo, z_at=z, x_at=x):
        return (y_hi_at * 2 + core_at, y_lo_at * 32 + z_at * 4 + x_at)

    def along_z(step):
        return device(z_at=(z + step) % 8)

    def in_the_plane(step):
        to = (q + step) % 8
        return device(y_lo_at=to // 4, x_at=to % 4)

    def along_x(step):
        return device(x_at=(x + step) % 4)

    def along_y(step):
        to = (y + step) % 4
        return device(y_hi_at=to // 2, y_lo_at=to % 2)

    sibling = device(core_at=1 - core)

    loads = []
    for number, (source, target) in enumerate(
        [
            (cot_hbm, cot_pairs), (tq_hbm, tq_pairs), (tk_hbm, tk_pairs), (weights_hbm.at[3], weights.at[3]),
            (token_moves_hbm, token_moves), (block_hbm, block), (weights_hbm.at[0], weights.at[0]),
            (sq_hbm, sq_turned), (sk_hbm, sk_turned), (weights_hbm.at[1], weights.at[1]), (weights_hbm.at[2], weights.at[2]),
            (feature_moves_hbm, feature_moves), (picks_hbm, picks), (share_moves_hbm, share_moves),
            (rest_moves_hbm, rest_moves),
        ]
    ):
        copy = pltpu.make_async_copy(source, target, load_sem.at[number])
        if number < 3:
            copy.start()
        loads.append(copy)

    barrier = pltpu.get_barrier_semaphore()
    greeted = [along_z(step) for step in range(1, 8)] + [in_the_plane(step) for step in range(1, 8)]
    greeted += [device(y_hi_at=1 - y_hi, y_lo_at=1 - y_lo), sibling]
    for peer in greeted:
        pl.semaphore_signal(barrier, inc=1, device_id=peer, device_id_type=MESH)

    sent, stored = [], []

    def store(source, target):
        copy = pltpu.make_async_copy(source, target, store_sem.at[len(stored)])
        copy.start()
        stored.append(copy)

    def send(source, target, send_sem, recv_sem, peer):
        copy = pltpu.make_async_remote_copy(
            src_ref=source, dst_ref=target, send_sem=send_sem, recv_sem=recv_sem,
            device_id=peer, device_id_type=MESH,
        )
        copy.start()
        sent.append(copy)
        return copy

    def move_tokens(number, rows):
        return dot(token_moves[number], rows).astype(BF16)

    def start_z(item, source, target):
        copies = []
        for step in range(1, 8):
            to = (z + step) % 8
            copies.append(
                send(
                    source.at[pl.ds(to * 16, 16)], target.at[pl.ds(z * 16, 16)],
                    z_send.at[item, step - 1], z_recv.at[item, step - 1], along_z(step),
                )
            )
        own = pl.ds(pl.multiple_of(z * 16, 16), 16)
        target[own, :] = source[own, :]
        return copies

    def start_plane(item, source, target):
        copies = []
        for step in range(1, 8):
            to = (q + step) % 8
            copies.append(
                send(
                    source.at[pl.ds(to * 16, 16)], target.at[pl.ds(q * 16, 16)],
                    plane_send.at[item, step - 1], plane_recv.at[item, step - 1], in_the_plane(step),
                )
            )
        own = pl.ds(pl.multiple_of(q * 16, 16), 16)
        target[own, :] = source[own, :]
        return copies

    def arrive(copies):
        for copy in copies:
            copy.wait_recv()

    def start_features(number, rows_ref):
        for half in range(2):
            factors[number, half * INNER : (half + 1) * INNER, 0:TOKENS] = dot_nt(
                feature_moves[half], rows_ref[:, half * 512 : half * 512 + 640]
            ).astype(BF16)
        return send(
            factors.at[number, :, 0:TOKENS], factors.at[number, :, TOKENS : 2 * TOKENS],
            factor_send.at[number], factor_recv.at[number], sibling,
        )

    def start_columns(number, rows):
        for side in range(2):
            picked[number, side, 0:TOKENS, :] = dot(rows, picks[core, side]).astype(BF16)
            picked_out[number, side] = dot(rows, picks[1 - core, side]).astype(BF16)
        return send(
            picked_out.at[number], picked.at[number, :, TOKENS : 2 * TOKENS],
            picked_send.at[number], picked_recv.at[number], sibling,
        )

    places = (x, y)
    rings = (along_x, along_y)
    slot_half = (0, 1, 1, 0, 0, 1)

    def make_pieces(number):
        rests = {}
        for y_lo_at in range(2):
            for x_at in range(4):
                block_rows = (y_lo_at * 4 + x_at) * ROW_BLOCK
                for side in range(2):
                    total = dot(factors[number, block_rows : block_rows + ROW_BLOCK, :], picked[number, side])
                    y_at = 2 * side + y_lo_at
                    for axis, to, sub in ((0, x_at, y_at), (1, y_at, x_at)):
                        count = ROWS_OF[axis]
                        part = total[0:80] if axis == 0 else total[80:ROW_BLOCK]
                        sums[number, axis, to, sub * count : (sub + 1) * count, :] = part[:, 0:128].astype(BF16)
                        rest = pltpu.roll(part[:, 128:256], 16 * sub, 1) if sub else part[:, 128:256]
                        rests[axis, to] = rests[axis, to] + rest if (axis, to) in rests else rest
        for (axis, to), rest in rests.items():
            first, count = REST_ROWS[axis], ROWS_OF[axis]
            beside = pltpu.roll(rest[first:count], 64, 1)
            if count < 2 * first:
                beside = jnp.concatenate([beside, jnp.zeros((2 * first - count, 128), F32)], axis=0)
            sums[number, axis, to, 4 * count : PIECE[axis], :] = (rest[0:first] + beside).astype(BF16)

    def half_rows(axis, half):
        return slice(0, CUT[axis]) if half == 0 else slice(CUT[axis], PIECE[axis])

    def piece(number, axis, to, half):
        return sums.at[number, axis, to, half_rows(axis, half)]

    def slot_ref(number, axis, slot):
        count = CUT[axis] if slot_half[slot] == 0 else PIECE[axis] - CUT[axis]
        return arrived.at[number, axis, slot, 0:count]

    def ring_copy(number, axis, slot, source):
        return send(
            source, slot_ref(number, axis, slot), ring_send.at[number, axis, slot], ring_recv.at[number, axis, slot],
            rings[axis](1 if slot % 2 == 0 else 3),
        )

    def first_ring(number):
        copies = {}
        for slot, step, half in ((0, 2, 0), (1, 2, 1), (2, 1, 1), (3, 3, 0)):
            for axis in range(2):
                to = (places[axis] + step) % 4
                copies[axis, slot] = ring_copy(number, axis, slot, piece(number, axis, to, half))
        return copies

    def first_relay(number, copies):
        for slot, step, half in ((0, 1, 0), (1, 3, 1)):
            for axis in range(2):
                copies[axis, slot].wait_recv()
                ref = piece(number, axis, (places[axis] + step) % 4, half)
                ref[...] = (ref[...].astype(F32) + slot_ref(number, axis, slot)[...].astype(F32)).astype(BF16)
                copies[axis, slot + 4] = ring_copy(number, axis, slot + 4, ref)

    lane_group = lax.broadcasted_iota(jnp.int32, (16, 128), 1) // 16
    share_group = lax.broadcasted_iota(jnp.int32, (8 * SHARE_ROWS, 128), 1) // 16

    def block_two(ref, axis):
        return ref.at[0 : ROWS_OF[axis] + 16]

    def second_line(number):
        copies = rings_at[number]
        seconds[number] = {}
        for axis in range(2):
            count = ROWS_OF[axis]
            for half, slots in ((0, (3, 4)), (1, (2, 5))):
                total = piece(number, axis, places[axis], half)[...].astype(F32)
                for slot in slots:
                    copies[axis, slot].wait_recv()
                    total += slot_ref(number, axis, slot)[...].astype(F32)
                total_one[half_rows(axis, half), :] = total
            for sub in range(4):
                sums_two[number, axis, sub, 0:count, :] = total_one[sub * count : (sub + 1) * count, :].astype(BF16)
                packed = jnp.zeros((16, 128), F32)
                for group in range(count // 16):
                    over = 16 * group >= REST_ROWS[axis]
                    start = 4 * count + 16 * group - (REST_ROWS[axis] if over else 0)
                    turn = (16 * group - 16 * sub - (64 if over else 0)) % 128
                    rest = total_one[start : start + 16, :]
                    rest = pltpu.roll(rest, turn, 1) if turn else rest
                    packed = jnp.where(lane_group == group, rest, packed)
                sums_two[number, axis, sub, count : count + 16, :] = packed.astype(BF16)
            for step in range(1, 4):
                seconds[number][axis, step] = send(
                    block_two(sums_two.at[number, axis, (places[1 - axis] + step) % 4], axis),
                    block_two(arrived_two.at[number, axis, step - 1], axis),
                    ring_two_send.at[number, axis, step - 1], ring_two_recv.at[number, axis, step - 1],
                    rings[1 - axis](step),
                )

    def third_line(number):
        wholes, ends = [], []
        for axis in range(2):
            count = ROWS_OF[axis]
            total = block_two(sums_two.at[number, axis, places[1 - axis]], axis)[...].astype(F32)
            for step in range(1, 4):
                seconds[number][axis, step].wait_recv()
                total += block_two(arrived_two.at[number, axis, step - 1], axis)[...].astype(F32)
            wholes.append(total[0:count])
            ends.append(total[count : count + 16])
        moved = dot(share_moves[...], jnp.concatenate(wholes, axis=0).astype(BF16))
        ends = jnp.concatenate(ends, axis=0)
        turned = [ends] + [pltpu.roll(ends, 16 * turn, 1) for turn in range(1, 8)]
        turned = jnp.concatenate(turned, axis=0).astype(BF16)
        for group in range(2):
            moved += jnp.where(share_group == group, dot(rest_moves[group], turned), 0.0)
        moved = moved.astype(BF16)
        for z_at in range(8):
            shares[number, z_at] = moved[SHARE_ROWS * z_at : SHARE_ROWS * (z_at + 1)]
        thirds[number] = [
            send(
                shares.at[number, (z + step) % 8], shares_in.at[number, step - 1],
                share_send.at[number, step - 1], share_recv.at[number, step - 1], along_z(step),
            )
            for step in range(1, 8)
        ]

    def finish(number):
        total = shares[number, z].astype(F32)
        for step in range(1, 8):
            thirds[number][step - 1].wait_recv()
            total += shares_in[number, step - 1].astype(F32)
        total_share[...] = total * grad_scale
        weight_grads[:, number, 0:128] = total_share[0:18, :]
        for half in range(2):
            weight_grads[9 * half : 9 * half + 9, number, 128:144] = total_share[18:27, 16 * half : 16 * half + 16]

    rings_at, seconds, thirds = {}, {}, {}

    def ready(number):
        arrive([feature_copies[number], column_copies[number]])
        make_pieces(number)
        rings_at[number] = first_ring(number)

    def join_pairs(pairs, rows):
        for frame in range(FRAMES):
            rows[line_order(frame), :] = pairs[frame].astype(F32)
        return rows[...].astype(BF16)

    def split_pairs(rows, pairs):
        for frame in range(FRAMES):
            pairs[frame] = rows[line_order(frame), :].astype(BF16)

    loads[0].wait()
    for copy in loads[3:11]:
        copy.start()
    cot[...] = join_pairs(cot_pairs, rows_wide)
    pl.semaphore_wait(barrier, len(greeted))
    cot_z = start_z(0, cot, in_z_wide)
    for copy in loads[11:]:
        copy.start()
    loads[1].wait()
    loads[2].wait()
    tq[...] = join_pairs(tq_pairs, rows_one)
    tk[...] = join_pairs(tk_pairs, rows_two)
    row_patch = lax.broadcasted_iota(jnp.int32, (TOKENS, TOKENS), 0) % 2
    column_patch = lax.broadcasted_iota(jnp.int32, (TOKENS, TOKENS), 1) % 2
    softmax_heads(tq, tk, chance_t, jnp.where(row_patch == column_patch, 0.0, -1e30))
    loads[3].wait()
    loads[4].wait()
    at_grad[...] = dot_nt(cot[...], weights[3]).astype(BF16)
    vt_grad[...] = attend_values_back(chance_t, at_grad).astype(BF16)
    out_plane[0] = move_tokens(1, vt_grad[...])
    grad_plane = start_plane(1, out_plane.at[0], in_plane.at[0])

    for number in (5, 6, 7, 8, 9, 10):
        loads[number].wait()
    sq[...] = sq_turned[...].T
    sk[...] = sk_turned[...].T
    value_s[...] = dot_nt(block[...], weights[0]).astype(BF16)
    softmax_heads(sq, sk, chance_s, None)
    attended_s[...] = attend(chance_s, value_s).astype(BF16)
    mixed[...] = (block[...].astype(F32) + dot(attended_s[...], weights[1])).astype(BF16)
    out_plane[1] = move_tokens(5, dot_nt(mixed[...], weights[2]).astype(BF16))
    value_plane = start_plane(2, out_plane.at[1], in_plane.at[1])

    arrive(grad_plane)
    out_z[0] = move_tokens(4, in_plane[0])
    grad_z = start_z(1, out_z.at[0], in_z.at[0])
    for number in (11, 12, 13, 14):
        loads[number].wait()
    feature_copies, column_copies = {}, {}
    feature_copies[0] = start_features(0, block)
    column_copies[1] = start_columns(1, attended_s[...])
    arrive(cot_z)
    out_plane_wide[...] = move_tokens(1, in_z_wide[...])
    cot_plane = start_plane(0, out_plane_wide, in_plane_wide)
    arrive(value_plane)
    out_z[1] = move_tokens(4, in_plane[1])
    value_z = start_z(2, out_z.at[1], in_z.at[1])
    feature_copies[2] = start_features(2, mixed)

    feature_copies[3] = start_features(3, cot)
    arrive(grad_z)
    vt_grad_frame[...] = move_tokens(3, in_z[0])
    column_copies[2] = start_columns(2, vt_grad_frame[...])
    arrive(cot_plane)
    cot_frame[...] = move_tokens(2, in_plane_wide[...])
    mixed_grad[...] = (cot_frame[...].astype(F32) + dot(vt_grad_frame[...], weights[2])).astype(BF16)
    feature_copies[1] = start_features(1, mixed_grad)
    ready(2)
    ready(1)
    as_grad[...] = dot_nt(mixed_grad[...], weights[1]).astype(BF16)
    vs_grad[...] = attend_values_back(chance_s, as_grad).astype(BF16)
    column_copies[0] = start_columns(0, vs_grad[...])
    first_relay(2, rings_at[2])
    arrive(value_z)
    value_t[...] = in_z[1]
    attended_t[...] = attend(chance_t, value_t).astype(BF16)
    column_copies[3] = start_columns(3, attended_t[...])
    ready(0)
    first_relay(1, rings_at[1])
    ready(3)
    first_relay(0, rings_at[0])
    second_line(2)
    input_grad[...] = (mixed_grad[...].astype(F32) + dot(vs_grad[...], weights[0])).astype(BF16)
    store(input_grad, input_grad_hbm)
    query_part, key_part = attend_scores_back(chance_s, sq, sk, value_s, as_grad)
    sq_grad[...] = query_part.astype(BF16).T
    sk_grad[...] = key_part.astype(BF16).T
    store(sq_grad, sq_grad_hbm)
    store(sk_grad, sk_grad_hbm)
    first_relay(3, rings_at[3])
    second_line(1)
    third_line(2)
    query_part, key_part = attend_scores_back(chance_t, tq, tk, value_t, at_grad)
    rows_one[...] = query_part
    rows_two[...] = key_part
    split_pairs(rows_one, tq_grad)
    split_pairs(rows_two, tk_grad)
    store(tq_grad, tq_grad_hbm)
    store(tk_grad, tk_grad_hbm)
    second_line(0)
    third_line(1)
    second_line(3)
    third_line(0)
    finish(2)
    finish(1)
    third_line(3)
    finish(0)
    finish(3)
    store(weight_grads, weight_grads_hbm)
    for copy in sent:
        copy.wait_send()
    for copy in stored:
        copy.wait()


def hand_over(*refs):
    sources, targets, buffers, (in_sem, out_sem) = refs[0:6], refs[6:12], refs[12:18], refs[18:20]
    arriving = [pltpu.make_async_copy(sources[at], buffers[at], in_sem.at[at]) for at in range(6)]
    leaving = [pltpu.make_async_copy(buffers[at], targets[at], out_sem.at[at]) for at in range(6)]
    for copy in arriving:
        copy.start()
    for copy, onward in zip(arriving, leaving):
        copy.wait()
        onward.start()
    for onward in leaving:
        onward.wait()


def body(
    block_input, spatial_queries, spatial_keys, cotangent, temporal_queries, temporal_keys, weights
):
    grad_scale = float(4 * 64 * 128) ** (-0.5)
    tables = make_tables()
    arrays = [
        block_input.reshape(TOKENS, WIDTH),
        spatial_queries.reshape(TOKENS, INNER).T,
        spatial_keys.reshape(TOKENS, INNER).T,
        cotangent.reshape(FRAMES, 2, WIDTH),
        temporal_queries.reshape(FRAMES, 2, INNER),
        temporal_keys.reshape(FRAMES, 2, INNER),
        weights.transpose(0, 2, 1),
    ] + tables
    wide, narrow = (TOKENS, WIDTH), (TOKENS, INNER)
    chances = pltpu.VMEM((HEADS, TOKENS, TOKENS), F32)
    dma = pltpu.SemaphoreType.DMA
    results = [
        jax.ShapeDtypeStruct(wide, BF16),
        jax.ShapeDtypeStruct((INNER, TOKENS), BF16),
        jax.ShapeDtypeStruct((INNER, TOKENS), BF16),
        jax.ShapeDtypeStruct((FRAMES, 2, INNER), BF16),
        jax.ShapeDtypeStruct((FRAMES, 2, INNER), BF16),
        jax.ShapeDtypeStruct((18, 4, 144), F32),
    ]
    buffers = [pltpu.VMEM(result.shape, result.dtype) for result in results]
    scratch = buffers + [pltpu.VMEM(array.shape, BF16) for array in arrays]
    scratch += [pltpu.VMEM(narrow, BF16)] * 2 + [pltpu.VMEM(wide, BF16)] + [pltpu.VMEM(narrow, BF16)] * 2
    scratch += [pltpu.VMEM(wide, F32)] + [pltpu.VMEM(narrow, F32)] * 2
    scratch += [chances, chances] + [pltpu.VMEM(narrow, BF16)] * 8
    scratch += [pltpu.VMEM(wide, BF16)] * 3 + [pltpu.VMEM(narrow, BF16)]
    scratch += [pltpu.VMEM(wide, BF16)] * 3 + [pltpu.VMEM((2,) + narrow, BF16)] * 4
    scratch += [
        pltpu.VMEM((4, WIDTH, 2 * TOKENS), BF16),
        pltpu.VMEM((4, 2, 2 * TOKENS, LANES), BF16),
        pltpu.VMEM((4, 2, TOKENS, LANES), BF16),
        pltpu.VMEM((4, 2, 4, PIECE[0], 128), BF16),
        pltpu.VMEM((4, 2, 6, CUT[0], 128), BF16),
        pltpu.VMEM((PIECE[0], 128), F32),
        pltpu.VMEM((4, 2, 4, 96, 128), BF16),
        pltpu.VMEM((4, 2, 3, 96, 128), BF16),
        pltpu.VMEM((4, 8, SHARE_ROWS, 128), BF16),
        pltpu.VMEM((4, 7, SHARE_ROWS, 128), BF16),
        pltpu.VMEM((SHARE_ROWS, 128), F32),
    ]
    scratch += [dma((15,)), dma((6,))] + [dma((3, 7))] * 4 + [dma((4,))] * 4 + [dma((4, 2, 6))] * 2 + [dma((4, 2, 3))] * 2 + [dma((4, 7))] * 2
    made = pl.pallas_call(
        functools.partial(kernel, grad_scale),
        out_shape=results,
        in_specs=[pl.BlockSpec(memory_space=pl.ANY)] * len(arrays),
        out_specs=[pl.BlockSpec(memory_space=pl.ANY)] * 6,
        scratch_shapes=scratch,
        compiler_params=pltpu.CompilerParams(
            collective_id=0, has_side_effects=True, vmem_limit_bytes=56 * 2**20
        ),
        name="block_backward",
    )(*arrays)
    input_grad, sq_grad, sk_grad, tq_grad, tk_grad, weight_grads = pl.pallas_call(
        hand_over,
        out_shape=results,
        in_specs=[pl.BlockSpec(memory_space=pl.ANY)] * 6,
        out_specs=[pl.BlockSpec(memory_space=pl.ANY)] * 6,
        scratch_shapes=buffers + [dma((6,)), dma((6,))],
        compiler_params=pltpu.CompilerParams(vmem_limit_bytes=60 * 2**20),
        name="hand_over",
    )(*made)
    return (
        input_grad.reshape(block_input.shape),
        sq_grad.T.reshape(spatial_queries.shape),
        sk_grad.T.reshape(spatial_keys.shape),
        tq_grad.reshape(temporal_queries.shape),
        tk_grad.reshape(temporal_keys.shape),
        weight_grads.transpose(1, 0, 2),
    )


def solution(mesh):
    placed = (
        P("dp", "seq", None, None),
        P("dp", "seq", None, None),
        P("dp", "seq", None, None),
        P("dp", None, "seq", None),
        P("dp", None, "seq", None),
        P("dp", None, "seq", None),
        P(),
    )
    return jax.shard_map(
        body,
        mesh=mesh,
        in_specs=placed,
        out_specs=(
            P("dp", "seq", None, None),
            P("dp", "seq", None, None),
            P("dp", "seq", None, None),
            P("dp", None, "seq", None),
            P("dp", None, "seq", None),
            P(None, "seq", "dp"),
        ),
        check_vma=False,
    )
```

```python
import functools

import jax
import jax.numpy as jnp
import numpy as np
from jax import lax
from jax.experimental import pallas as pl
from jax.experimental.pallas import tpu as pltpu
from jax.sharding import PartitionSpec as P

HEADS = 8
HEAD_DIM = 72
WIDTH = 1152
INNER = 576
TOKENS = 128
FRAMES = 64
SCORE_SCALE = HEAD_DIM ** (-0.5)
ROW_BLOCK = 144
LANES = 256
ROWS_OF = (80, 64)
REST_ROWS = (48, 32)
PIECE = (4 * 80 + 48, 4 * 64 + 32)
CUT = (192, 144)
SHARE_ROWS = 32
LINE_STEPS = (4, 3, 5, 2, 6, 1, 7)
PLANE_STEPS = (6, 2, 5, 3, 7, 1, 4)
F32 = jnp.float32
BF16 = jnp.bfloat16
MESH = pl.DeviceIdType.MESH


def one_hot(source, size):
    table = np.zeros((len(source), size), np.float32)
    for row, at in enumerate(source):
        if at >= 0:
            table[row, at] = 1.0
    return table


def make_tables():
    def natural(y_lo, z, x, p):
        return 2 * (y_lo * 32 + z * 4 + x) + p

    to_z = [natural(y, z, x, p) for z in range(8) for y in range(2) for x in range(4) for p in range(2)]
    to_plane = [z * 16 + q * 2 + p for q in range(8) for z in range(8) for p in range(2)]
    to_natural = [
        (y * 4 + x) * 16 + z * 2 + p for y in range(2) for z in range(8) for x in range(4) for p in range(2)
    ]
    forth = [one_hot(order, TOKENS) for order in (to_z, to_plane, to_natural)]
    token_moves = np.stack(forth + [table.T for table in forth])
    feature_moves = np.stack(
        [
            one_hot(
                [y * 64 + z * 72 + x * 18 + r for x in range(4) for z in range(8) for r in range(18)], 640
            )
            for y in range(2)
        ]
    )
    picks = np.zeros((2, 2, INNER, LANES), np.float32)
    for core in range(2):
        for y_hi in range(2):
            for column in range(144):
                picks[core, y_hi, (2 * y_hi + core) * 144 + column, column] = 1.0
    share_moves = one_hot(
        [z * 18 + row if row < 18 else -1 for z in range(8) for row in range(SHARE_ROWS)], ROW_BLOCK
    )
    rest_moves = []
    for group in range(2):
        source = []
        for z in range(8):
            for row in range(SHARE_ROWS):
                at = z * 18 + 9 * group + row - 18
                tile, place = divmod(at // 16, 5)
                source.append((group - place) % 8 * 32 + tile * 16 + at % 16 if 18 <= row < 27 else -1)
        rest_moves.append(one_hot(source, 256))
    tables = (token_moves, feature_moves, picks, share_moves, np.stack(rest_moves))
    return [jnp.asarray(table, BF16) for table in tables]


def line_order(frame):
    y_lo, z, x = frame // 32, frame // 4 % 8, frame % 4
    start = 2 * (z * 8 + y_lo * 4 + x)
    return slice(start, start + 2)


def dot(left, right):
    return jnp.dot(left, right, preferred_element_type=F32)


def dot_nt(left, right):
    return lax.dot_general(left, right, (((1,), (1,)), ((), ())), preferred_element_type=F32)


def dot_tn(left, right):
    return lax.dot_general(left, right, (((0,), (0,)), ((), ())), preferred_element_type=F32)


def head_window(head):
    start = head * HEAD_DIM // 128 * 128
    stop = min(-(-(head * HEAD_DIM + HEAD_DIM) // 128) * 128, INNER)
    return start, stop


def head_mask(head):
    start, stop = head_window(head)
    lane = lax.broadcasted_iota(jnp.int32, (TOKENS, stop - start), 1) + start
    return (lane >= head * HEAD_DIM) & (lane < (head + 1) * HEAD_DIM)


def window(ref, head):
    start, stop = head_window(head)
    return ref[:, start:stop]


def masked_window(ref, head):
    return jnp.where(head_mask(head), window(ref, head).astype(F32), 0.0).astype(BF16)


def join_heads(parts):
    tiles = [None] * 5
    for head, part in enumerate(parts):
        start, stop = head_window(head)
        part = jnp.where(head_mask(head), part, 0.0)
        for at in range(start, stop, 128):
            piece = part[:, at - start : min(at - start + 128, stop - start)]
            tiles[at // 128] = piece if tiles[at // 128] is None else tiles[at // 128] + piece
    return jnp.concatenate(tiles, axis=1)


def softmax_heads(queries, key_rows, chance_ref, bias):
    for head in range(HEADS):
        scores = dot_nt(masked_window(queries, head), window(key_rows, head)) * SCORE_SCALE
        if bias is not None:
            scores = scores + bias
        powers = jnp.exp(scores - jnp.max(scores, axis=1, keepdims=True))
        chance_ref[head] = powers / jnp.sum(powers, axis=1, keepdims=True)


def attend(chance_ref, values):
    return join_heads([dot(chance_ref[h].astype(BF16), window(values, h)) for h in range(HEADS)])


def attend_values_back(chance_ref, out_grad):
    return join_heads([dot_tn(chance_ref[h].astype(BF16), window(out_grad, h)) for h in range(HEADS)])


def attend_scores_back(chance_ref, queries, key_rows, values, out_grad):
    query_parts, key_parts = [], []
    for head in range(HEADS):
        chance = chance_ref[head]
        chance_grad = dot_nt(masked_window(out_grad, head), window(values, head))
        centre = jnp.sum(chance * chance_grad, axis=1, keepdims=True)
        score_grad = (chance * (chance_grad - centre)).astype(BF16)
        query_parts.append(dot(score_grad, window(key_rows, head)))
        key_parts.append(dot_tn(score_grad, window(queries, head)))
    return join_heads(query_parts) * SCORE_SCALE, join_heads(key_parts) * SCORE_SCALE


def kernel(
    grad_scale,
    block_hbm, sq_hbm, sk_hbm, cot_hbm, tq_hbm, tk_hbm, weights_hbm,
    token_moves_hbm, feature_moves_hbm, picks_hbm, share_moves_hbm, rest_moves_hbm,
    input_grad_hbm, sq_grad_hbm, sk_grad_hbm, tq_grad_hbm, tk_grad_hbm, weight_grads_hbm,
    input_grad, sq_grad, sk_grad, tq_grad, tk_grad, weight_grads,
    block, sq_turned, sk_turned, cot_pairs, tq_pairs, tk_pairs, weights, token_moves, feature_moves, picks, share_moves, rest_moves,
    sq, sk, cot, tq, tk, rows_wide, rows_one, rows_two,
    chance_s, chance_t, value_s, value_t, attended_s, attended_t, at_grad, as_grad, vt_grad, vs_grad,
    mixed, mixed_grad, cot_frame, vt_grad_frame,
    in_z_wide, out_plane_wide, in_plane_wide, out_plane, in_plane, out_z, in_z,
    factors, picked, picked_out, sums, arrived, total_one, sums_two, arrived_two, shares, shares_in, total_share,
    load_sem, store_sem, z_send, z_recv, plane_send, plane_recv, factor_send, factor_recv, picked_send, picked_recv,
    ring_send, ring_recv, ring_two_send, ring_two_recv, share_send, share_recv,
):
    dp, seq = lax.axis_index("dp"), lax.axis_index("seq")
    y_hi, core = dp // 2, dp % 2
    y_lo, z, x = seq // 32, (seq // 4) % 8, seq % 4
    y = y_hi * 2 + y_lo
    q = y_lo * 4 + x

    def device(y_hi_at=y_hi, core_at=core, y_lo_at=y_lo, z_at=z, x_at=x):
        return (y_hi_at * 2 + core_at, y_lo_at * 32 + z_at * 4 + x_at)

    def along_z(step):
        return device(z_at=(z + step) % 8)

    def in_the_plane(step):
        to = (q + step) % 8
        return device(y_lo_at=to // 4, x_at=to % 4)

    def along_x(step):
        return device(x_at=(x + step) % 4)

    def along_y(step):
        to = (y + step) % 4
        return device(y_hi_at=to // 2, y_lo_at=to % 2)

    sibling = device(core_at=1 - core)

    loads = []
    for number, (source, target) in enumerate(
        [
            (cot_hbm, cot_pairs), (tq_hbm, tq_pairs), (tk_hbm, tk_pairs), (weights_hbm.at[3], weights.at[3]),
            (token_moves_hbm, token_moves), (block_hbm, block), (weights_hbm.at[0], weights.at[0]),
            (sq_hbm, sq_turned), (sk_hbm, sk_turned), (weights_hbm.at[1], weights.at[1]), (weights_hbm.at[2], weights.at[2]),
            (feature_moves_hbm, feature_moves), (picks_hbm, picks), (share_moves_hbm, share_moves),
            (rest_moves_hbm, rest_moves),
        ]
    ):
        copy = pltpu.make_async_copy(source, target, load_sem.at[number])
        if number < 3:
            copy.start()
        loads.append(copy)

    barrier = pltpu.get_barrier_semaphore()
    greeted = [along_z(step) for step in range(1, 8)] + [in_the_plane(step) for step in range(1, 8)]
    greeted += [device(y_hi_at=1 - y_hi, y_lo_at=1 - y_lo), sibling]
    for peer in greeted:
        pl.semaphore_signal(barrier, inc=1, device_id=peer, device_id_type=MESH)

    sent, stored = [], []

    def store(source, target):
        copy = pltpu.make_async_copy(source, target, store_sem.at[len(stored)])
        copy.start()
        stored.append(copy)

    def send(source, target, send_sem, recv_sem, peer):
        copy = pltpu.make_async_remote_copy(
            src_ref=source, dst_ref=target, send_sem=send_sem, recv_sem=recv_sem,
            device_id=peer, device_id_type=MESH,
        )
        copy.start()
        sent.append(copy)
        return copy

    def move_tokens(number, rows):
        return dot(token_moves[number], rows).astype(BF16)

    def start_z(item, source, target):
        copies = []
        for step in LINE_STEPS:
            to = (z + step) % 8
            copies.append(
                send(
                    source.at[pl.ds(to * 16, 16)], target.at[pl.ds(z * 16, 16)],
                    z_send.at[item, step - 1], z_recv.at[item, step - 1], along_z(step),
                )
            )
        own = pl.ds(pl.multiple_of(z * 16, 16), 16)
        target[own, :] = source[own, :]
        return copies

    def start_plane(item, source, target):
        copies = []
        for step in PLANE_STEPS:
            to = (q + step) % 8
            copies.append(
                send(
                    source.at[pl.ds(to * 16, 16)], target.at[pl.ds(q * 16, 16)],
                    plane_send.at[item, step - 1], plane_recv.at[item, step - 1], in_the_plane(step),
                )
            )
        own = pl.ds(pl.multiple_of(q * 16, 16), 16)
        target[own, :] = source[own, :]
        return copies

    def arrive(copies):
        for copy in copies:
            copy.wait_recv()

    def start_features(number, rows_ref):
        for half in range(2):
            factors[number, half * INNER : (half + 1) * INNER, 0:TOKENS] = dot_nt(
                feature_moves[half], rows_ref[:, half * 512 : half * 512 + 640]
            ).astype(BF16)
        return send(
            factors.at[number, :, 0:TOKENS], factors.at[number, :, TOKENS : 2 * TOKENS],
            factor_send.at[number], factor_recv.at[number], sibling,
        )

    def start_columns(number, rows):
        for side in range(2):
            picked[number, side, 0:TOKENS, :] = dot(rows, picks[core, side]).astype(BF16)
            picked_out[number, side] = dot(rows, picks[1 - core, side]).astype(BF16)
        return send(
            picked_out.at[number], picked.at[number, :, TOKENS : 2 * TOKENS],
            picked_send.at[number], picked_recv.at[number], sibling,
        )

    places = (x, y)
    rings = (along_x, along_y)
    slot_half = (0, 1, 1, 0, 0, 1)

    def make_pieces(number):
        rests = {}
        for y_lo_at in range(2):
            for x_at in range(4):
                block_rows = (y_lo_at * 4 + x_at) * ROW_BLOCK
                for side in range(2):
                    total = dot(factors[number, block_rows : block_rows + ROW_BLOCK, :], picked[number, side])
                    y_at = 2 * side + y_lo_at
                    for axis, to, sub in ((0, x_at, y_at), (1, y_at, x_at)):
                        count = ROWS_OF[axis]
                        part = total[0:80] if axis == 0 else total[80:ROW_BLOCK]
                        sums[number, axis, to, sub * count : (sub + 1) * count, :] = part[:, 0:128].astype(BF16)
                        rest = pltpu.roll(part[:, 128:256], 16 * sub, 1) if sub else part[:, 128:256]
                        rests[axis, to] = rests[axis, to] + rest if (axis, to) in rests else rest
        for (axis, to), rest in rests.items():
            first, count = REST_ROWS[axis], ROWS_OF[axis]
            beside = pltpu.roll(rest[first:count], 64, 1)
            if count < 2 * first:
                beside = jnp.concatenate([beside, jnp.zeros((2 * first - count, 128), F32)], axis=0)
            sums[number, axis, to, 4 * count : PIECE[axis], :] = (rest[0:first] + beside).astype(BF16)

    def half_rows(axis, half):
        return slice(0, CUT[axis]) if half == 0 else slice(CUT[axis], PIECE[axis])

    def piece(number, axis, to, half):
        return sums.at[number, axis, to, half_rows(axis, half)]

    def slot_ref(number, axis, slot):
        count = CUT[axis] if slot_half[slot] == 0 else PIECE[axis] - CUT[axis]
        return arrived.at[number, axis, slot, 0:count]

    def ring_copy(number, axis, slot, source):
        return send(
            source, slot_ref(number, axis, slot), ring_send.at[number, axis, slot], ring_recv.at[number, axis, slot],
            rings[axis](1 if slot % 2 == 0 else 3),
        )

    def first_ring(number):
        copies = {}
        for slot, step, half in ((0, 2, 0), (1, 2, 1), (2, 1, 1), (3, 3, 0)):
            for axis in range(2):
                to = (places[axis] + step) % 4
                copies[axis, slot] = ring_copy(number, axis, slot, piece(number, axis, to, half))
        return copies

    def first_relay(number, copies):
        for slot, step, half in ((0, 1, 0), (1, 3, 1)):
            for axis in range(2):
                copies[axis, slot].wait_recv()
                ref = piece(number, axis, (places[axis] + step) % 4, half)
                ref[...] = (ref[...].astype(F32) + slot_ref(number, axis, slot)[...].astype(F32)).astype(BF16)
                copies[axis, slot + 4] = ring_copy(number, axis, slot + 4, ref)

    lane_group = lax.broadcasted_iota(jnp.int32, (16, 128), 1) // 16
    share_group = lax.broadcasted_iota(jnp.int32, (8 * SHARE_ROWS, 128), 1) // 16

    def block_two(ref, axis):
        return ref.at[0 : ROWS_OF[axis] + 16]

    def second_line(number):
        copies = rings_at[number]
        seconds[number] = {}
        for axis in range(2):
            count = ROWS_OF[axis]
            for half, slots in ((0, (3, 4)), (1, (2, 5))):
                total = piece(number, axis, places[axis], half)[...].astype(F32)
                for slot in slots:
                    copies[axis, slot].wait_recv()
                    total += slot_ref(number, axis, slot)[...].astype(F32)
                total_one[half_rows(axis, half), :] = total
            for sub in range(4):
                sums_two[number, axis, sub, 0:count, :] = total_one[sub * count : (sub + 1) * count, :].astype(BF16)
                packed = jnp.zeros((16, 128), F32)
                for group in range(count // 16):
                    over = 16 * group >= REST_ROWS[axis]
                    start = 4 * count + 16 * group - (REST_ROWS[axis] if over else 0)
                    turn = (16 * group - 16 * sub - (64 if over else 0)) % 128
                    rest = total_one[start : start + 16, :]
                    rest = pltpu.roll(rest, turn, 1) if turn else rest
                    packed = jnp.where(lane_group == group, rest, packed)
                sums_two[number, axis, sub, count : count + 16, :] = packed.astype(BF16)
            for step in (2, 1, 3):
                seconds[number][axis, step] = send(
                    block_two(sums_two.at[number, axis, (places[1 - axis] + step) % 4], axis),
                    block_two(arrived_two.at[number, axis, step - 1], axis),
                    ring_two_send.at[number, axis, step - 1], ring_two_recv.at[number, axis, step - 1],
                    rings[1 - axis](step),
                )

    def third_line(number):
        wholes, ends = [], []
        for axis in range(2):
            count = ROWS_OF[axis]
            total = block_two(sums_two.at[number, axis, places[1 - axis]], axis)[...].astype(F32)
            for step in range(1, 4):
                seconds[number][axis, step].wait_recv()
                total += block_two(arrived_two.at[number, axis, step - 1], axis)[...].astype(F32)
            wholes.append(total[0:count])
            ends.append(total[count : count + 16])
        moved = dot(share_moves[...], jnp.concatenate(wholes, axis=0).astype(BF16))
        ends = jnp.concatenate(ends, axis=0)
        turned = [ends] + [pltpu.roll(ends, 16 * turn, 1) for turn in range(1, 8)]
        turned = jnp.concatenate(turned, axis=0).astype(BF16)
        for group in range(2):
            moved += jnp.where(share_group == group, dot(rest_moves[group], turned), 0.0)
        moved = moved.astype(BF16)
        for z_at in range(8):
            shares[number, z_at] = moved[SHARE_ROWS * z_at : SHARE_ROWS * (z_at + 1)]
        thirds[number] = {
            step: send(
                shares.at[number, (z + step) % 8], shares_in.at[number, step - 1],
                share_send.at[number, step - 1], share_recv.at[number, step - 1], along_z(step),
            )
            for step in LINE_STEPS
        }

    def finish(number):
        total = shares[number, z].astype(F32)
        for step in range(1, 8):
            thirds[number][step].wait_recv()
            total += shares_in[number, step - 1].astype(F32)
        total_share[...] = total * grad_scale
        weight_grads[:, number, 0:128] = total_share[0:18, :]
        for half in range(2):
            weight_grads[9 * half : 9 * half + 9, number, 128:144] = total_share[18:27, 16 * half : 16 * half + 16]

    rings_at, seconds, thirds = {}, {}, {}

    def ready(number):
        arrive([feature_copies[number], column_copies[number]])
        make_pieces(number)
        rings_at[number] = first_ring(number)

    def join_pairs(pairs, rows):
        for frame in range(FRAMES):
            rows[line_order(frame), :] = pairs[frame].astype(F32)
        return rows[...].astype(BF16)

    def split_pairs(rows, pairs):
        for frame in range(FRAMES):
            pairs[frame] = rows[line_order(frame), :].astype(BF16)

    loads[0].wait()
    for copy in loads[3:11]:
        copy.start()
    cot[...] = join_pairs(cot_pairs, rows_wide)
    pl.semaphore_wait(barrier, len(greeted))
    cot_z = start_z(0, cot, in_z_wide)
    for copy in loads[11:]:
        copy.start()
    loads[1].wait()
    loads[2].wait()
    tq[...] = join_pairs(tq_pairs, rows_one)
    tk[...] = join_pairs(tk_pairs, rows_two)
    row_patch = lax.broadcasted_iota(jnp.int32, (TOKENS, TOKENS), 0) % 2
    column_patch = lax.broadcasted_iota(jnp.int32, (TOKENS, TOKENS), 1) % 2
    softmax_heads(tq, tk, chance_t, jnp.where(row_patch == column_patch, 0.0, -1e30))
    loads[3].wait()
    loads[4].wait()
    at_grad[...] = dot_nt(cot[...], weights[3]).astype(BF16)
    vt_grad[...] = attend_values_back(chance_t, at_grad).astype(BF16)
    out_plane[0] = move_tokens(1, vt_grad[...])
    grad_plane = start_plane(1, out_plane.at[0], in_plane.at[0])

    for number in (5, 6, 7, 8, 9, 10):
        loads[number].wait()
    sq[...] = sq_turned[...].T
    sk[...] = sk_turned[...].T
    value_s[...] = dot_nt(block[...], weights[0]).astype(BF16)
    softmax_heads(sq, sk, chance_s, None)
    attended_s[...] = attend(chance_s, value_s).astype(BF16)
    mixed[...] = (block[...].astype(F32) + dot(attended_s[...], weights[1])).astype(BF16)
    out_plane[1] = move_tokens(5, dot_nt(mixed[...], weights[2]).astype(BF16))
    value_plane = start_plane(2, out_plane.at[1], in_plane.at[1])

    arrive(grad_plane)
    out_z[0] = move_tokens(4, in_plane[0])
    grad_z = start_z(1, out_z.at[0], in_z.at[0])
    for number in (11, 12, 13, 14):
        loads[number].wait()
    feature_copies, column_copies = {}, {}
    feature_copies[0] = start_features(0, block)
    column_copies[1] = start_columns(1, attended_s[...])
    arrive(cot_z)
    out_plane_wide[...] = move_tokens(1, in_z_wide[...])
    cot_plane = start_plane(0, out_plane_wide, in_plane_wide)
    arrive(value_plane)
    out_z[1] = move_tokens(4, in_plane[1])
    value_z = start_z(2, out_z.at[1], in_z.at[1])
    feature_copies[2] = start_features(2, mixed)

    feature_copies[3] = start_features(3, cot)
    arrive(grad_z)
    vt_grad_frame[...] = move_tokens(3, in_z[0])
    column_copies[2] = start_columns(2, vt_grad_frame[...])
    arrive(cot_plane)
    cot_frame[...] = move_tokens(2, in_plane_wide[...])
    mixed_grad[...] = (cot_frame[...].astype(F32) + dot(vt_grad_frame[...], weights[2])).astype(BF16)
    feature_copies[1] = start_features(1, mixed_grad)
    ready(2)
    ready(1)
    as_grad[...] = dot_nt(mixed_grad[...], weights[1]).astype(BF16)
    vs_grad[...] = attend_values_back(chance_s, as_grad).astype(BF16)
    column_copies[0] = start_columns(0, vs_grad[...])
    first_relay(2, rings_at[2])
    arrive(value_z)
    value_t[...] = in_z[1]
    attended_t[...] = attend(chance_t, value_t).astype(BF16)
    column_copies[3] = start_columns(3, attended_t[...])
    ready(0)
    first_relay(1, rings_at[1])
    ready(3)
    first_relay(0, rings_at[0])
    second_line(2)
    input_grad[...] = (mixed_grad[...].astype(F32) + dot(vs_grad[...], weights[0])).astype(BF16)
    store(input_grad, input_grad_hbm)
    query_part, key_part = attend_scores_back(chance_s, sq, sk, value_s, as_grad)
    sq_grad[...] = query_part.astype(BF16).T
    sk_grad[...] = key_part.astype(BF16).T
    store(sq_grad, sq_grad_hbm)
    store(sk_grad, sk_grad_hbm)
    first_relay(3, rings_at[3])
    second_line(1)
    third_line(2)
    query_part, key_part = attend_scores_back(chance_t, tq, tk, value_t, at_grad)
    rows_one[...] = query_part
    rows_two[...] = key_part
    split_pairs(rows_one, tq_grad)
    split_pairs(rows_two, tk_grad)
    store(tq_grad, tq_grad_hbm)
    store(tk_grad, tk_grad_hbm)
    second_line(0)
    third_line(1)
    second_line(3)
    third_line(0)
    finish(2)
    finish(1)
    third_line(3)
    finish(0)
    finish(3)
    store(weight_grads, weight_grads_hbm)
    for copy in sent:
        copy.wait_send()
    for copy in stored:
        copy.wait()


def hand_over(*refs):
    sources, targets, buffers, (in_sem, out_sem) = refs[0:6], refs[6:12], refs[12:18], refs[18:20]
    arriving = [pltpu.make_async_copy(sources[at], buffers[at], in_sem.at[at]) for at in range(6)]
    leaving = [pltpu.make_async_copy(buffers[at], targets[at], out_sem.at[at]) for at in range(6)]
    for copy in arriving:
        copy.start()
    for copy, onward in zip(arriving, leaving):
        copy.wait()
        onward.start()
    for onward in leaving:
        onward.wait()


def body(
    block_input, spatial_queries, spatial_keys, cotangent, temporal_queries, temporal_keys, weights
):
    grad_scale = float(4 * 64 * 128) ** (-0.5)
    tables = make_tables()
    arrays = [
        block_input.reshape(TOKENS, WIDTH),
        spatial_queries.reshape(TOKENS, INNER).T,
        spatial_keys.reshape(TOKENS, INNER).T,
        cotangent.reshape(FRAMES, 2, WIDTH),
        temporal_queries.reshape(FRAMES, 2, INNER),
        temporal_keys.reshape(FRAMES, 2, INNER),
        weights.transpose(0, 2, 1),
    ] + tables
    wide, narrow = (TOKENS, WIDTH), (TOKENS, INNER)
    chances = pltpu.VMEM((HEADS, TOKENS, TOKENS), F32)
    dma = pltpu.SemaphoreType.DMA
    results = [
        jax.ShapeDtypeStruct(wide, BF16),
        jax.ShapeDtypeStruct((INNER, TOKENS), BF16),
        jax.ShapeDtypeStruct((INNER, TOKENS), BF16),
        jax.ShapeDtypeStruct((FRAMES, 2, INNER), BF16),
        jax.ShapeDtypeStruct((FRAMES, 2, INNER), BF16),
        jax.ShapeDtypeStruct((18, 4, 144), F32),
    ]
    buffers = [pltpu.VMEM(result.shape, result.dtype) for result in results]
    scratch = buffers + [pltpu.VMEM(array.shape, BF16) for array in arrays]
    scratch += [pltpu.VMEM(narrow, BF16)] * 2 + [pltpu.VMEM(wide, BF16)] + [pltpu.VMEM(narrow, BF16)] * 2
    scratch += [pltpu.VMEM(wide, F32)] + [pltpu.VMEM(narrow, F32)] * 2
    scratch += [chances, chances] + [pltpu.VMEM(narrow, BF16)] * 8
    scratch += [pltpu.VMEM(wide, BF16)] * 3 + [pltpu.VMEM(narrow, BF16)]
    scratch += [pltpu.VMEM(wide, BF16)] * 3 + [pltpu.VMEM((2,) + narrow, BF16)] * 4
    scratch += [
        pltpu.VMEM((4, WIDTH, 2 * TOKENS), BF16),
        pltpu.VMEM((4, 2, 2 * TOKENS, LANES), BF16),
        pltpu.VMEM((4, 2, TOKENS, LANES), BF16),
        pltpu.VMEM((4, 2, 4, PIECE[0], 128), BF16),
        pltpu.VMEM((4, 2, 6, CUT[0], 128), BF16),
        pltpu.VMEM((PIECE[0], 128), F32),
        pltpu.VMEM((4, 2, 4, 96, 128), BF16),
        pltpu.VMEM((4, 2, 3, 96, 128), BF16),
        pltpu.VMEM((4, 8, SHARE_ROWS, 128), BF16),
        pltpu.VMEM((4, 7, SHARE_ROWS, 128), BF16),
        pltpu.VMEM((SHARE_ROWS, 128), F32),
    ]
    scratch += [dma((15,)), dma((6,))] + [dma((3, 7))] * 4 + [dma((4,))] * 4 + [dma((4, 2, 6))] * 2 + [dma((4, 2, 3))] * 2 + [dma((4, 7))] * 2
    made = pl.pallas_call(
        functools.partial(kernel, grad_scale),
        out_shape=results,
        in_specs=[pl.BlockSpec(memory_space=pl.ANY)] * len(arrays),
        out_specs=[pl.BlockSpec(memory_space=pl.ANY)] * 6,
        scratch_shapes=scratch,
        compiler_params=pltpu.CompilerParams(
            collective_id=0, has_side_effects=True, vmem_limit_bytes=56 * 2**20
        ),
        name="block_backward",
    )(*arrays)
    input_grad, sq_grad, sk_grad, tq_grad, tk_grad, weight_grads = pl.pallas_call(
        hand_over,
        out_shape=results,
        in_specs=[pl.BlockSpec(memory_space=pl.ANY)] * 6,
        out_specs=[pl.BlockSpec(memory_space=pl.ANY)] * 6,
        scratch_shapes=buffers + [dma((6,)), dma((6,))],
        compiler_params=pltpu.CompilerParams(vmem_limit_bytes=60 * 2**20),
        name="hand_over",
    )(*made)
    return (
        input_grad.reshape(block_input.shape),
        sq_grad.T.reshape(spatial_queries.shape),
        sk_grad.T.reshape(spatial_keys.shape),
        tq_grad.reshape(temporal_queries.shape),
        tk_grad.reshape(temporal_keys.shape),
        weight_grads.transpose(1, 0, 2),
    )


def solution(mesh):
    placed = (
        P("dp", "seq", None, None),
        P("dp", "seq", None, None),
        P("dp", "seq", None, None),
        P("dp", None, "seq", None),
        P("dp", None, "seq", None),
        P("dp", None, "seq", None),
        P(),
    )
    return jax.shard_map(
        body,
        mesh=mesh,
        in_specs=placed,
        out_specs=(
            P("dp", "seq", None, None),
            P("dp", "seq", None, None),
            P("dp", "seq", None, None),
            P("dp", None, "seq", None),
            P("dp", None, "seq", None),
            P(None, "seq", "dp"),
        ),
        check_vma=False,
    )
```

```python
import functools

import jax
import jax.numpy as jnp
import numpy as np
from jax import lax
from jax.experimental import pallas as pl
from jax.experimental.pallas import tpu as pltpu
from jax.sharding import PartitionSpec as P

HEADS = 8
HEAD_DIM = 72
WIDTH = 1152
INNER = 576
TOKENS = 128
FRAMES = 64
SCORE_SCALE = HEAD_DIM ** (-0.5)
ROW_BLOCK = 144
LANES = 256
ROWS_OF = (80, 64)
REST_ROWS = (48, 32)
PIECE = (4 * 80 + 48, 4 * 64 + 32)
CUT = (192, 144)
SHARE_ROWS = 32
LINE_STEPS = (4, 3, 5, 2, 6, 1, 7)
PLANE_STEPS = (6, 2, 5, 3, 7, 1, 4)
F32 = jnp.float32
BF16 = jnp.bfloat16
MESH = pl.DeviceIdType.MESH


def one_hot(source, size):
    table = np.zeros((len(source), size), np.float32)
    for row, at in enumerate(source):
        if at >= 0:
            table[row, at] = 1.0
    return table


def make_tables():
    def natural(y_lo, z, x, p):
        return 2 * (y_lo * 32 + z * 4 + x) + p

    to_z = [natural(y, z, x, p) for z in range(8) for y in range(2) for x in range(4) for p in range(2)]
    to_plane = [z * 16 + q * 2 + p for q in range(8) for z in range(8) for p in range(2)]
    to_natural = [
        (y * 4 + x) * 16 + z * 2 + p for y in range(2) for z in range(8) for x in range(4) for p in range(2)
    ]
    forth = [one_hot(order, TOKENS) for order in (to_z, to_plane, to_natural)]
    token_moves = np.stack(forth + [table.T for table in forth])
    feature_moves = np.stack(
        [
            one_hot(
                [y * 64 + z * 72 + x * 18 + r for x in range(4) for z in range(8) for r in range(18)], 640
            )
            for y in range(2)
        ]
    )
    picks = np.zeros((2, 2, INNER, LANES), np.float32)
    for core in range(2):
        for y_hi in range(2):
            for column in range(144):
                picks[core, y_hi, (2 * y_hi + core) * 144 + column, column] = 1.0
    share_moves = one_hot(
        [z * 18 + row if row < 18 else -1 for z in range(8) for row in range(SHARE_ROWS)], ROW_BLOCK
    )
    rest_moves = []
    for group in range(2):
        source = []
        for z in range(8):
            for row in range(SHARE_ROWS):
                at = z * 18 + 9 * group + row - 18
                tile, place = divmod(at // 16, 5)
                source.append((group - place) % 8 * 32 + tile * 16 + at % 16 if 18 <= row < 27 else -1)
        rest_moves.append(one_hot(source, 256))
    tables = (token_moves, feature_moves, picks, share_moves, np.stack(rest_moves))
    return [jnp.asarray(table, BF16) for table in tables]


def line_order(frame):
    y_lo, z, x = frame // 32, frame // 4 % 8, frame % 4
    start = 2 * (z * 8 + y_lo * 4 + x)
    return slice(start, start + 2)


def dot(left, right):
    return jnp.dot(left, right, preferred_element_type=F32)


def dot_nt(left, right):
    return lax.dot_general(left, right, (((1,), (1,)), ((), ())), preferred_element_type=F32)


def dot_tn(left, right):
    return lax.dot_general(left, right, (((0,), (0,)), ((), ())), preferred_element_type=F32)


def head_window(head):
    start = head * HEAD_DIM // 128 * 128
    stop = min(-(-(head * HEAD_DIM + HEAD_DIM) // 128) * 128, INNER)
    return start, stop


def head_mask(head):
    start, stop = head_window(head)
    lane = lax.broadcasted_iota(jnp.int32, (TOKENS, stop - start), 1) + start
    return (lane >= head * HEAD_DIM) & (lane < (head + 1) * HEAD_DIM)


def window(ref, head):
    start, stop = head_window(head)
    return ref[:, start:stop]


def masked_window(ref, head):
    return jnp.where(head_mask(head), window(ref, head).astype(F32), 0.0).astype(BF16)


def join_heads(parts):
    tiles = [None] * 5
    for head, part in enumerate(parts):
        start, stop = head_window(head)
        part = jnp.where(head_mask(head), part, 0.0)
        for at in range(start, stop, 128):
            piece = part[:, at - start : min(at - start + 128, stop - start)]
            tiles[at // 128] = piece if tiles[at // 128] is None else tiles[at // 128] + piece
    return jnp.concatenate(tiles, axis=1)


def softmax_heads(queries, key_rows, chance_ref, bias):
    for head in range(HEADS):
        scores = dot_nt(masked_window(queries, head), window(key_rows, head)) * SCORE_SCALE
        if bias is not None:
            scores = scores + bias
        powers = jnp.exp(scores - jnp.max(scores, axis=1, keepdims=True))
        chance_ref[head] = powers / jnp.sum(powers, axis=1, keepdims=True)


def attend(chance_ref, values):
    return join_heads([dot(chance_ref[h].astype(BF16), window(values, h)) for h in range(HEADS)])


def attend_values_back(chance_ref, out_grad):
    return join_heads([dot_tn(chance_ref[h].astype(BF16), window(out_grad, h)) for h in range(HEADS)])


def attend_scores_back(chance_ref, queries, key_rows, values, out_grad):
    query_parts, key_parts = [], []
    for head in range(HEADS):
        chance = chance_ref[head]
        chance_grad = dot_nt(masked_window(out_grad, head), window(values, head))
        centre = jnp.sum(chance * chance_grad, axis=1, keepdims=True)
        score_grad = (chance * (chance_grad - centre)).astype(BF16)
        query_parts.append(dot(score_grad, window(key_rows, head)))
        key_parts.append(dot_tn(score_grad, window(queries, head)))
    return join_heads(query_parts) * SCORE_SCALE, join_heads(key_parts) * SCORE_SCALE


def kernel(
    grad_scale,
    block_hbm, sq_hbm, sk_hbm, cot_hbm, tq_hbm, tk_hbm, weights_hbm,
    token_moves_hbm, feature_moves_hbm, picks_hbm, share_moves_hbm, rest_moves_hbm,
    input_grad_hbm, sq_grad_hbm, sk_grad_hbm, tq_grad_hbm, tk_grad_hbm, weight_grads_hbm,
    input_grad, sq_grad, sk_grad, tq_grad, tk_grad, weight_grads,
    block, sq_turned, sk_turned, cot_pairs, tq_pairs, tk_pairs, weights, token_moves, feature_moves, picks, share_moves, rest_moves,
    sq, sk, cot, tq, tk, rows_wide, rows_one, rows_two,
    chance_s, chance_t, value_s, value_t, attended_s, attended_t, at_grad, as_grad, vt_grad, vs_grad,
    mixed, mixed_grad, cot_frame, vt_grad_frame,
    in_z_wide, out_plane_wide, in_plane_wide, out_plane, in_plane, out_z, in_z,
    factors, picked, picked_out, sums, arrived, total_one, sums_two, arrived_two, shares, shares_in, total_share,
    load_sem, store_sem, z_send, z_recv, plane_send, plane_recv, factor_send, factor_recv, picked_send, picked_recv,
    ring_send, ring_recv, ring_two_send, ring_two_recv, share_send, share_recv,
):
    dp, seq = lax.axis_index("dp"), lax.axis_index("seq")
    y_hi, core = dp // 2, dp % 2
    y_lo, z, x = seq // 32, (seq // 4) % 8, seq % 4
    y = y_hi * 2 + y_lo
    q = y_lo * 4 + x

    def device(y_hi_at=y_hi, core_at=core, y_lo_at=y_lo, z_at=z, x_at=x):
        return (y_hi_at * 2 + core_at, y_lo_at * 32 + z_at * 4 + x_at)

    def along_z(step):
        return device(z_at=(z + step) % 8)

    def in_the_plane(step):
        to = (q + step) % 8
        return device(y_lo_at=to // 4, x_at=to % 4)

    def along_x(step):
        return device(x_at=(x + step) % 4)

    def along_y(step):
        to = (y + step) % 4
        return device(y_hi_at=to // 2, y_lo_at=to % 2)

    sibling = device(core_at=1 - core)

    loads = []
    for number, (source, target) in enumerate(
        [
            (cot_hbm, cot_pairs), (tq_hbm, tq_pairs), (tk_hbm, tk_pairs), (weights_hbm.at[3], weights.at[3]),
            (token_moves_hbm, token_moves), (block_hbm, block), (weights_hbm.at[0], weights.at[0]),
            (sq_hbm, sq_turned), (sk_hbm, sk_turned), (weights_hbm.at[1], weights.at[1]), (weights_hbm.at[2], weights.at[2]),
            (feature_moves_hbm, feature_moves), (picks_hbm, picks), (share_moves_hbm, share_moves),
            (rest_moves_hbm, rest_moves),
        ]
    ):
        copy = pltpu.make_async_copy(source, target, load_sem.at[number])
        if number < 3:
            copy.start()
        loads.append(copy)

    barrier = pltpu.get_barrier_semaphore()
    greeted = [along_z(step) for step in LINE_STEPS] + [in_the_plane(step) for step in PLANE_STEPS]
    greeted += [device(y_hi_at=1 - y_hi, y_lo_at=1 - y_lo), sibling]
    for peer in greeted:
        pl.semaphore_signal(barrier, inc=1, device_id=peer, device_id_type=MESH)

    sent, stored = [], []

    def store(source, target):
        copy = pltpu.make_async_copy(source, target, store_sem.at[len(stored)])
        copy.start()
        stored.append(copy)

    def send(source, target, send_sem, recv_sem, peer):
        copy = pltpu.make_async_remote_copy(
            src_ref=source, dst_ref=target, send_sem=send_sem, recv_sem=recv_sem,
            device_id=peer, device_id_type=MESH,
        )
        copy.start()
        sent.append(copy)
        return copy

    def move_tokens(number, rows):
        return dot(token_moves[number], rows).astype(BF16)

    def start_z(item, source, target):
        copies = []
        for step in LINE_STEPS:
            to = (z + step) % 8
            copies.append(
                send(
                    source.at[pl.ds(to * 16, 16)], target.at[pl.ds(z * 16, 16)],
                    z_send.at[item, step - 1], z_recv.at[item, step - 1], along_z(step),
                )
            )
        own = pl.ds(pl.multiple_of(z * 16, 16), 16)
        target[own, :] = source[own, :]
        return copies

    def start_plane(item, source, target):
        copies = []
        for step in PLANE_STEPS:
            to = (q + step) % 8
            copies.append(
                send(
                    source.at[pl.ds(to * 16, 16)], target.at[pl.ds(q * 16, 16)],
                    plane_send.at[item, step - 1], plane_recv.at[item, step - 1], in_the_plane(step),
                )
            )
        own = pl.ds(pl.multiple_of(q * 16, 16), 16)
        target[own, :] = source[own, :]
        return copies

    def arrive(copies):
        for copy in copies:
            copy.wait_recv()

    def start_features(number, rows_ref):
        for half in range(2):
            factors[number, half * INNER : (half + 1) * INNER, 0:TOKENS] = dot_nt(
                feature_moves[half], rows_ref[:, half * 512 : half * 512 + 640]
            ).astype(BF16)
        return send(
            factors.at[number, :, 0:TOKENS], factors.at[number, :, TOKENS : 2 * TOKENS],
            factor_send.at[number], factor_recv.at[number], sibling,
        )

    def start_columns(number, rows):
        for side in range(2):
            picked[number, side, 0:TOKENS, :] = dot(rows, picks[core, side]).astype(BF16)
            picked_out[number, side] = dot(rows, picks[1 - core, side]).astype(BF16)
        return send(
            picked_out.at[number], picked.at[number, :, TOKENS : 2 * TOKENS],
            picked_send.at[number], picked_recv.at[number], sibling,
        )

    places = (x, y)
    rings = (along_x, along_y)
    slot_half = (0, 1, 1, 0, 0, 1)

    def make_pieces(number):
        rests = {}
        for y_lo_at in range(2):
            for x_at in range(4):
                block_rows = (y_lo_at * 4 + x_at) * ROW_BLOCK
                for side in range(2):
                    total = dot(factors[number, block_rows : block_rows + ROW_BLOCK, :], picked[number, side])
                    y_at = 2 * side + y_lo_at
                    for axis, to, sub in ((0, x_at, y_at), (1, y_at, x_at)):
                        count = ROWS_OF[axis]
                        part = total[0:80] if axis == 0 else total[80:ROW_BLOCK]
                        sums[number, axis, to, sub * count : (sub + 1) * count, :] = part[:, 0:128].astype(BF16)
                        rest = pltpu.roll(part[:, 128:256], 16 * sub, 1) if sub else part[:, 128:256]
                        rests[axis, to] = rests[axis, to] + rest if (axis, to) in rests else rest
        for (axis, to), rest in rests.items():
            first, count = REST_ROWS[axis], ROWS_OF[axis]
            beside = pltpu.roll(rest[first:count], 64, 1)
            if count < 2 * first:
                beside = jnp.concatenate([beside, jnp.zeros((2 * first - count, 128), F32)], axis=0)
            sums[number, axis, to, 4 * count : PIECE[axis], :] = (rest[0:first] + beside).astype(BF16)

    def half_rows(axis, half):
        return slice(0, CUT[axis]) if half == 0 else slice(CUT[axis], PIECE[axis])

    def piece(number, axis, to, half):
        return sums.at[number, axis, to, half_rows(axis, half)]

    def slot_ref(number, axis, slot):
        count = CUT[axis] if slot_half[slot] == 0 else PIECE[axis] - CUT[axis]
        return arrived.at[number, axis, slot, 0:count]

    def ring_copy(number, axis, slot, source):
        return send(
            source, slot_ref(number, axis, slot), ring_send.at[number, axis, slot], ring_recv.at[number, axis, slot],
            rings[axis](1 if slot % 2 == 0 else 3),
        )

    def first_ring(number):
        copies = {}
        for slot, step, half in ((0, 2, 0), (1, 2, 1), (2, 1, 1), (3, 3, 0)):
            for axis in range(2):
                to = (places[axis] + step) % 4
                copies[axis, slot] = ring_copy(number, axis, slot, piece(number, axis, to, half))
        return copies

    def first_relay(number, copies):
        for slot, step, half in ((0, 1, 0), (1, 3, 1)):
            for axis in range(2):
                copies[axis, slot].wait_recv()
                ref = piece(number, axis, (places[axis] + step) % 4, half)
                ref[...] = (ref[...].astype(F32) + slot_ref(number, axis, slot)[...].astype(F32)).astype(BF16)
                copies[axis, slot + 4] = ring_copy(number, axis, slot + 4, ref)

    lane_group = lax.broadcasted_iota(jnp.int32, (16, 128), 1) // 16
    share_group = lax.broadcasted_iota(jnp.int32, (8 * SHARE_ROWS, 128), 1) // 16

    def block_two(ref, axis):
        return ref.at[0 : ROWS_OF[axis] + 16]

    def second_line(number):
        copies = rings_at[number]
        seconds[number] = {}
        for axis in range(2):
            count = ROWS_OF[axis]
            for half, slots in ((0, (3, 4)), (1, (2, 5))):
                total = piece(number, axis, places[axis], half)[...].astype(F32)
                for slot in slots:
                    copies[axis, slot].wait_recv()
                    total += slot_ref(number, axis, slot)[...].astype(F32)
                total_one[half_rows(axis, half), :] = total
            for sub in range(4):
                sums_two[number, axis, sub, 0:count, :] = total_one[sub * count : (sub + 1) * count, :].astype(BF16)
                packed = jnp.zeros((16, 128), F32)
                for group in range(count // 16):
                    over = 16 * group >= REST_ROWS[axis]
                    start = 4 * count + 16 * group - (REST_ROWS[axis] if over else 0)
                    turn = (16 * group - 16 * sub - (64 if over else 0)) % 128
                    rest = total_one[start : start + 16, :]
                    rest = pltpu.roll(rest, turn, 1) if turn else rest
                    packed = jnp.where(lane_group == group, rest, packed)
                sums_two[number, axis, sub, count : count + 16, :] = packed.astype(BF16)
            for step in (2, 1, 3):
                seconds[number][axis, step] = send(
                    block_two(sums_two.at[number, axis, (places[1 - axis] + step) % 4], axis),
                    block_two(arrived_two.at[number, axis, step - 1], axis),
                    ring_two_send.at[number, axis, step - 1], ring_two_recv.at[number, axis, step - 1],
                    rings[1 - axis](step),
                )

    def third_line(number):
        wholes, ends = [], []
        for axis in range(2):
            count = ROWS_OF[axis]
            total = block_two(sums_two.at[number, axis, places[1 - axis]], axis)[...].astype(F32)
            for step in range(1, 4):
                seconds[number][axis, step].wait_recv()
                total += block_two(arrived_two.at[number, axis, step - 1], axis)[...].astype(F32)
            wholes.append(total[0:count])
            ends.append(total[count : count + 16])
        moved = dot(share_moves[...], jnp.concatenate(wholes, axis=0).astype(BF16))
        ends = jnp.concatenate(ends, axis=0)
        turned = [ends] + [pltpu.roll(ends, 16 * turn, 1) for turn in range(1, 8)]
        turned = jnp.concatenate(turned, axis=0).astype(BF16)
        for group in range(2):
            moved += jnp.where(share_group == group, dot(rest_moves[group], turned), 0.0)
        moved = moved.astype(BF16)
        for z_at in range(8):
            shares[number, z_at] = moved[SHARE_ROWS * z_at : SHARE_ROWS * (z_at + 1)]
        thirds[number] = {
            step: send(
                shares.at[number, (z + step) % 8], shares_in.at[number, step - 1],
                share_send.at[number, step - 1], share_recv.at[number, step - 1], along_z(step),
            )
            for step in LINE_STEPS
        }

    def finish(number):
        total = shares[number, z].astype(F32)
        for step in range(1, 8):
            thirds[number][step].wait_recv()
            total += shares_in[number, step - 1].astype(F32)
        total_share[...] = total * grad_scale
        weight_grads[:, number, 0:128] = total_share[0:18, :]
        for half in range(2):
            weight_grads[9 * half : 9 * half + 9, number, 128:144] = total_share[18:27, 16 * half : 16 * half + 16]

    rings_at, seconds, thirds = {}, {}, {}

    def ready(number):
        arrive([feature_copies[number], column_copies[number]])
        make_pieces(number)
        rings_at[number] = first_ring(number)

    def join_pairs(pairs, rows):
        for frame in range(FRAMES):
            rows[line_order(frame), :] = pairs[frame].astype(F32)
        return rows[...].astype(BF16)

    def split_pairs(rows, pairs):
        for frame in range(FRAMES):
            pairs[frame] = rows[line_order(frame), :].astype(BF16)

    loads[0].wait()
    for copy in loads[3:11]:
        copy.start()
    cot[...] = join_pairs(cot_pairs, rows_wide)
    pl.semaphore_wait(barrier, len(greeted))
    cot_z = start_z(0, cot, in_z_wide)
    for copy in loads[11:]:
        copy.start()
    loads[1].wait()
    loads[2].wait()
    tq[...] = join_pairs(tq_pairs, rows_one)
    tk[...] = join_pairs(tk_pairs, rows_two)
    row_patch = lax.broadcasted_iota(jnp.int32, (TOKENS, TOKENS), 0) % 2
    column_patch = lax.broadcasted_iota(jnp.int32, (TOKENS, TOKENS), 1) % 2
    softmax_heads(tq, tk, chance_t, jnp.where(row_patch == column_patch, 0.0, -1e30))
    loads[3].wait()
    loads[4].wait()
    at_grad[...] = dot_nt(cot[...], weights[3]).astype(BF16)
    vt_grad[...] = attend_values_back(chance_t, at_grad).astype(BF16)
    out_plane[0] = move_tokens(1, vt_grad[...])
    grad_plane = start_plane(1, out_plane.at[0], in_plane.at[0])

    for number in (5, 6, 7, 8, 9, 10):
        loads[number].wait()
    sq[...] = sq_turned[...].T
    sk[...] = sk_turned[...].T
    value_s[...] = dot_nt(block[...], weights[0]).astype(BF16)
    softmax_heads(sq, sk, chance_s, None)
    attended_s[...] = attend(chance_s, value_s).astype(BF16)
    mixed[...] = (block[...].astype(F32) + dot(attended_s[...], weights[1])).astype(BF16)
    out_plane[1] = move_tokens(5, dot_nt(mixed[...], weights[2]).astype(BF16))
    value_plane = start_plane(2, out_plane.at[1], in_plane.at[1])

    arrive(grad_plane)
    out_z[0] = move_tokens(4, in_plane[0])
    grad_z = start_z(1, out_z.at[0], in_z.at[0])
    for number in (11, 12, 13, 14):
        loads[number].wait()
    feature_copies, column_copies = {}, {}
    feature_copies[0] = start_features(0, block)
    column_copies[1] = start_columns(1, attended_s[...])
    arrive(cot_z)
    out_plane_wide[...] = move_tokens(1, in_z_wide[...])
    cot_plane = start_plane(0, out_plane_wide, in_plane_wide)
    arrive(value_plane)
    out_z[1] = move_tokens(4, in_plane[1])
    value_z = start_z(2, out_z.at[1], in_z.at[1])
    feature_copies[2] = start_features(2, mixed)

    feature_copies[3] = start_features(3, cot)
    arrive(grad_z)
    vt_grad_frame[...] = move_tokens(3, in_z[0])
    column_copies[2] = start_columns(2, vt_grad_frame[...])
    arrive(cot_plane)
    cot_frame[...] = move_tokens(2, in_plane_wide[...])
    mixed_grad[...] = (cot_frame[...].astype(F32) + dot(vt_grad_frame[...], weights[2])).astype(BF16)
    feature_copies[1] = start_features(1, mixed_grad)
    ready(2)
    ready(1)
    as_grad[...] = dot_nt(mixed_grad[...], weights[1]).astype(BF16)
    vs_grad[...] = attend_values_back(chance_s, as_grad).astype(BF16)
    column_copies[0] = start_columns(0, vs_grad[...])
    first_relay(2, rings_at[2])
    arrive(value_z)
    value_t[...] = in_z[1]
    attended_t[...] = attend(chance_t, value_t).astype(BF16)
    column_copies[3] = start_columns(3, attended_t[...])
    ready(0)
    first_relay(1, rings_at[1])
    ready(3)
    first_relay(0, rings_at[0])
    second_line(2)
    input_grad[...] = (mixed_grad[...].astype(F32) + dot(vs_grad[...], weights[0])).astype(BF16)
    store(input_grad, input_grad_hbm)
    query_part, key_part = attend_scores_back(chance_s, sq, sk, value_s, as_grad)
    sq_grad[...] = query_part.astype(BF16).T
    sk_grad[...] = key_part.astype(BF16).T
    store(sq_grad, sq_grad_hbm)
    store(sk_grad, sk_grad_hbm)
    first_relay(3, rings_at[3])
    second_line(1)
    third_line(2)
    query_part, key_part = attend_scores_back(chance_t, tq, tk, value_t, at_grad)
    rows_one[...] = query_part
    rows_two[...] = key_part
    split_pairs(rows_one, tq_grad)
    split_pairs(rows_two, tk_grad)
    store(tq_grad, tq_grad_hbm)
    store(tk_grad, tk_grad_hbm)
    second_line(0)
    third_line(1)
    second_line(3)
    third_line(0)
    finish(2)
    finish(1)
    third_line(3)
    finish(0)
    finish(3)
    store(weight_grads, weight_grads_hbm)
    for copy in sent:
        copy.wait_send()
    for copy in stored:
        copy.wait()


def hand_over(*refs):
    sources, targets, buffers, (in_sem, out_sem) = refs[0:6], refs[6:12], refs[12:18], refs[18:20]
    arriving = [pltpu.make_async_copy(sources[at], buffers[at], in_sem.at[at]) for at in range(6)]
    leaving = [pltpu.make_async_copy(buffers[at], targets[at], out_sem.at[at]) for at in range(6)]
    for copy in arriving:
        copy.start()
    for copy, onward in zip(arriving, leaving):
        copy.wait()
        onward.start()
    for onward in leaving:
        onward.wait()


def body(
    block_input, spatial_queries, spatial_keys, cotangent, temporal_queries, temporal_keys, weights
):
    grad_scale = float(4 * 64 * 128) ** (-0.5)
    tables = make_tables()
    arrays = [
        block_input.reshape(TOKENS, WIDTH),
        spatial_queries.reshape(TOKENS, INNER).T,
        spatial_keys.reshape(TOKENS, INNER).T,
        cotangent.reshape(FRAMES, 2, WIDTH),
        temporal_queries.reshape(FRAMES, 2, INNER),
        temporal_keys.reshape(FRAMES, 2, INNER),
        weights.transpose(0, 2, 1),
    ] + tables
    wide, narrow = (TOKENS, WIDTH), (TOKENS, INNER)
    chances = pltpu.VMEM((HEADS, TOKENS, TOKENS), F32)
    dma = pltpu.SemaphoreType.DMA
    results = [
        jax.ShapeDtypeStruct(wide, BF16),
        jax.ShapeDtypeStruct((INNER, TOKENS), BF16),
        jax.ShapeDtypeStruct((INNER, TOKENS), BF16),
        jax.ShapeDtypeStruct((FRAMES, 2, INNER), BF16),
        jax.ShapeDtypeStruct((FRAMES, 2, INNER), BF16),
        jax.ShapeDtypeStruct((18, 4, 144), F32),
    ]
    buffers = [pltpu.VMEM(result.shape, result.dtype) for result in results]
    scratch = buffers + [pltpu.VMEM(array.shape, BF16) for array in arrays]
    scratch += [pltpu.VMEM(narrow, BF16)] * 2 + [pltpu.VMEM(wide, BF16)] + [pltpu.VMEM(narrow, BF16)] * 2
    scratch += [pltpu.VMEM(wide, F32)] + [pltpu.VMEM(narrow, F32)] * 2
    scratch += [chances, chances] + [pltpu.VMEM(narrow, BF16)] * 8
    scratch += [pltpu.VMEM(wide, BF16)] * 3 + [pltpu.VMEM(narrow, BF16)]
    scratch += [pltpu.VMEM(wide, BF16)] * 3 + [pltpu.VMEM((2,) + narrow, BF16)] * 4
    scratch += [
        pltpu.VMEM((4, WIDTH, 2 * TOKENS), BF16),
        pltpu.VMEM((4, 2, 2 * TOKENS, LANES), BF16),
        pltpu.VMEM((4, 2, TOKENS, LANES), BF16),
        pltpu.VMEM((4, 2, 4, PIECE[0], 128), BF16),
        pltpu.VMEM((4, 2, 6, CUT[0], 128), BF16),
        pltpu.VMEM((PIECE[0], 128), F32),
        pltpu.VMEM((4, 2, 4, 96, 128), BF16),
        pltpu.VMEM((4, 2, 3, 96, 128), BF16),
        pltpu.VMEM((4, 8, SHARE_ROWS, 128), BF16),
        pltpu.VMEM((4, 7, SHARE_ROWS, 128), BF16),
        pltpu.VMEM((SHARE_ROWS, 128), F32),
    ]
    scratch += [dma((15,)), dma((6,))] + [dma((3, 7))] * 4 + [dma((4,))] * 4 + [dma((4, 2, 6))] * 2 + [dma((4, 2, 3))] * 2 + [dma((4, 7))] * 2
    made = pl.pallas_call(
        functools.partial(kernel, grad_scale),
        out_shape=results,
        in_specs=[pl.BlockSpec(memory_space=pl.ANY)] * len(arrays),
        out_specs=[pl.BlockSpec(memory_space=pl.ANY)] * 6,
        scratch_shapes=scratch,
        compiler_params=pltpu.CompilerParams(
            collective_id=0, has_side_effects=True, vmem_limit_bytes=56 * 2**20
        ),
        name="block_backward",
    )(*arrays)
    input_grad, sq_grad, sk_grad, tq_grad, tk_grad, weight_grads = pl.pallas_call(
        hand_over,
        out_shape=results,
        in_specs=[pl.BlockSpec(memory_space=pl.ANY)] * 6,
        out_specs=[pl.BlockSpec(memory_space=pl.ANY)] * 6,
        scratch_shapes=buffers + [dma((6,)), dma((6,))],
        compiler_params=pltpu.CompilerParams(vmem_limit_bytes=60 * 2**20),
        name="hand_over",
    )(*made)
    return (
        input_grad.reshape(block_input.shape),
        sq_grad.T.reshape(spatial_queries.shape),
        sk_grad.T.reshape(spatial_keys.shape),
        tq_grad.reshape(temporal_queries.shape),
        tk_grad.reshape(temporal_keys.shape),
        weight_grads.transpose(1, 0, 2),
    )


def solution(mesh):
    placed = (
        P("dp", "seq", None, None),
        P("dp", "seq", None, None),
        P("dp", "seq", None, None),
        P("dp", None, "seq", None),
        P("dp", None, "seq", None),
        P("dp", None, "seq", None),
        P(),
    )
    return jax.shard_map(
        body,
        mesh=mesh,
        in_specs=placed,
        out_specs=(
            P("dp", "seq", None, None),
            P("dp", "seq", None, None),
            P("dp", "seq", None, None),
            P("dp", None, "seq", None),
            P("dp", None, "seq", None),
            P(None, "seq", "dp"),
        ),
        check_vma=False,
    )
```
